32 devices in a mesh: group: 2 (over x), ep: 16 (over z, y, core).
Axes of the slice: x: 2, y: 2, z: 4, core: 2. Of those that a mesh axis runs over, the one named last changes fastest.
Arguments:
- hidden: bfloat16 [512, 7168], P(('group', 'ep')), parts along dimension 0, may hold values from -6 to 6
- ffn_gain: float32 [7168], replicated, may hold values from 0.25 to 1.75
- attn_gain: float32 [7168], replicated, may hold values from 0.25 to 1.75
- latent_norm_gain: float32 [512], replicated, may hold values from 0.25 to 1.75
- routes: int32 [512, 2], P(('group', 'ep')), parts along dimension 0, may hold values from 0 to 3, all different within a row; in each aligned block of 16 rows (0 to 15, 16 to 31, ...) at most 9 rows name the same one
- gate_weights: float32 [512, 2], P(('group', 'ep')), parts along dimension 0, may hold values from 0.2 to 1
- expert_in: bfloat16 [16, 7168, 1024], P('ep'), may hold values from -0.0625 to 0.0625
- expert_down: bfloat16 [16, 512, 7168], P('ep'), may hold values from -0.125 to 0.125
- kv_down: bfloat16 [7168, 576], P('ep'), may hold values from -0.0625 to 0.0625
- parents: int32 [32, 16], P(('group', 'ep')), parts along dimension 0, may hold values from -1 to 14, as said below
- lengths: int32 [32], P(('group', 'ep')), parts along dimension 0, may hold values from 128 to 1024, as said below
- queries: bfloat16 [512, 128, 576], P(('group', 'ep')), parts along dimension 0
- cache: bfloat16 [32, 1024, 576], P(('group', 'ep')), parts along dimension 0
Outputs:
- residual_after_expert: bfloat16 [512, 7168], P(('group', 'ep')), parts along dimension 0
- draft_latent_entries: bfloat16 [512, 576], P(('group', 'ep')), parts along dimension 0
- attention_output: bfloat16 [512, 128, 512], P(('group', 'ep')), parts along dimension 0
The draws below stay inside these ranges and needn't reach their ends.
There are 2 independent parts, one for each index of `group`. The reference program is written for one: setup_inputs(seed, part) draws one part's arguments, and reference() takes and returns one part's arrays. A program takes and returns all parts, laid end to end along the dimension named above; an argument that names none is the same for every part. Nothing has to cross between parts.
Inputs may be any that keep to these rules, and one draw needn't show every extreme that they name: `parents`: node 0 of each request is its root, with parent -1; every other node's parent is an earlier node of the same request. `lengths`: cache slots at or past a request's length are not used.
All inputs are finite; a program needn't handle non-finite values.
Results may differ from the reference program's by a relative error of at most 0.008.
Values may be sent and summed in bfloat16 or wider, within the bound.
No kernel may reach another device: no remote copies, remote signals or barrier semaphores. Data moves between devices by JAX's collectives and lax.ppermute only.
A program may use at most 128 MiB of HBM per device.

```python
import math
import jax
import jax.numpy as jnp
import numpy as np
from jax import lax

D = 7168
FF = 2048
HEAD_COUNT = 128
KEY_VALUE_RANK = 512
NODES = 16
TOPK = 2
EXPERTS = 4
CTX = 1024
LATENT = 576
SPLIT = 4
HID_DEV = 512
TOK_DEV = 16
REQUESTS = 16
TOKEN_COUNT = 256
CAP = 9
N_EP = 16


def shared_cache(key):
    return jnp.clip(jax.random.normal(key, (REQUESTS, CTX, LATENT), jnp.float32), -6.0, 6.0)


def draw_cache(key, part):
    base = shared_cache(key)
    return base.astype(jnp.bfloat16)


def draw_queries(key, part):
    key = jax.random.fold_in(key, 11)
    values = 0.5 * jnp.clip(jax.random.normal(key, (TOKEN_COUNT, HEAD_COUNT, LATENT), jnp.float32), -6.0, 6.0)
    return values.astype(jnp.bfloat16)


def draw_parents(key, part):
    key = jax.random.fold_in(key, 3)
    first, second = jax.random.split(key)
    raw = jax.random.randint(first, (REQUESTS, NODES), 0, 1 << 20)
    index = jnp.arange(NODES, dtype=jnp.int32)
    chosen = jnp.where(index[None, :] == 0, -1, raw % jnp.maximum(index, 1)[None, :])
    pick = jax.random.randint(second, (), 0, REQUESTS)
    chosen = chosen.at[pick, NODES - 1].set(NODES - 2)
    return chosen.astype(jnp.int32)


def draw_lengths(key, part):
    key = jax.random.fold_in(key, 5)
    first, second, third = jax.random.split(key, 3)
    values = jax.random.randint(first, (REQUESTS,), CTX // 8, CTX + 1)
    longest = jax.random.randint(second, (), 0, REQUESTS)
    shortest = (longest + 1 + jax.random.randint(third, (), 0, REQUESTS - 1)) % REQUESTS
    values = values.at[longest].set(CTX).at[shortest].set(CTX // 8)
    return values.astype(jnp.int32)


def levels(rng, shape, pieces, low, largest):
    def one(position, blocks):
        heights = jax.random.uniform(jax.random.fold_in(jax.random.fold_in(rng, 6), position), (blocks,), jnp.float32, low / len(pieces), largest / len(pieces))
        return jnp.repeat(jnp.exp(heights), shape[position] // blocks).reshape((-1,) + (1,) * (len(shape) - position - 1))

    factor_of = one(*pieces[0])
    for cut in pieces[1:]:
        factor_of = factor_of * one(*cut)
    return factor_of


def deal_out(rng, own, number, rows, amount, top, limit, lean):
    order = jax.random.permutation(rng, amount)
    heavy_load, usual = shares(amount, rows * top, limit, lean, True), shares(amount, rows * top, limit, lean, False)
    places = jnp.arange(amount)

    def named(sizes, turn):
        used = int((sizes > 0).sum())
        fixed = max(1, used // 4)
        passed = fixed + (places - fixed + turn * (used - fixed)) % max(1, amount - fixed)
        return jnp.zeros((amount,), jnp.int32).at[order[jnp.where(places < fixed, places, passed)]].set(jnp.asarray(sizes, jnp.int32))

    sizes = jnp.where(number % 4 == 0, named(heavy_load, number // 4), named(usual, number - number // 4 - 1))
    mixed = jax.random.permutation(jax.random.fold_in(own, 3), amount)
    source_of, receiver = mixed[0:amount // 2 * 2:2], mixed[1:amount // 2 * 2:2]
    margin = jnp.minimum(sizes[source_of] - 1, limit - sizes[receiver]) // 2
    margin = jnp.where((source_of == order[0]) | (receiver == order[0]) | (sizes[receiver] == 0), 0, jnp.maximum(margin, 0))
    passed = jax.random.randint(jax.random.fold_in(own, 4), (amount // 2,), 0, 1 << 20) % (margin + 1)
    sizes = sizes.at[source_of].add(-passed).at[receiver].add(passed)
    items = jnp.searchsorted(jnp.cumsum(sizes), jnp.arange(rows * top), side="right").astype(jnp.int32)
    listing = items.reshape(top, rows).T
    listing = listing[jax.random.permutation(jax.random.fold_in(own, 1), rows)]
    turn = jax.random.randint(jax.random.fold_in(own, 2), (rows, 1), 0, top)
    return jnp.take_along_axis(listing, (jnp.arange(top)[None, :] + turn) % top, axis=1)


def shares(amount, total, most, slope, full):
    portions = [(1 << 20) // math.isqrt(standing ** slope) + 1 for standing in range(1, amount + 1)]
    largest = most if full else min(most, max(-(-total // amount), total * portions[0] // sum(portions)))
    least = 1 if total - largest >= amount - 1 else 0
    counts, surplus = [largest] + [least] * (amount - 1), total - largest - least * (amount - 1)
    while surplus > 0:
        movable = [i for i in range(1, amount) if counts[i] < largest] or [i for i in range(1, amount) if counts[i] < most]
        mass, left = sum([portions[i] for i in movable]), surplus
        for i in movable:
            addition = min(most - counts[i], max(1, left * portions[i] // mass), surplus)
            counts[i] = counts[i] + addition
            surplus = surplus - addition
    return np.array(counts)


def noise(own_key, extent, width, bound, pieces=(), held_as=jnp.bfloat16):
    values = width * jax.random.normal(own_key, extent, jnp.float32)
    if pieces:
        values = values * levels(own_key, extent, pieces, -0.22, 0.18)
    return jnp.clip(values, -bound, bound).astype(held_as)


def setup_inputs(seed: int = 0, part: int = 0) -> dict:
    seeds = jax.random.split(jax.random.key(seed), 14)
    part_splits = jax.random.split(jax.random.fold_in(seeds[13], part), 14)
    hidden = noise(part_splits[0], (TOKEN_COUNT, D), 1.0, 6.0, ((0, 16),))
    ffn_gain = jnp.clip(1.0 + 0.15 * jax.random.normal(seeds[1], (D,), jnp.float32), 0.25, 1.75)
    attn_gain = jnp.clip(1.0 + 0.15 * jax.random.normal(seeds[2], (D,), jnp.float32), 0.25, 1.75)
    latent_norm_gain = jnp.clip(1.0 + 0.15 * jax.random.normal(seeds[3], (KEY_VALUE_RANK,), jnp.float32), 0.25, 1.75)
    routes_keys = jax.random.split(jax.random.fold_in(part_splits[4], 1), TOKEN_COUNT // TOK_DEV)
    routes_turns = jax.random.permutation(jax.random.fold_in(part_splits[4], 3), TOKEN_COUNT // TOK_DEV)
    routes = jax.vmap(lambda own, number: deal_out(jax.random.fold_in(part_splits[4], 2), own, number, TOK_DEV, EXPERTS, TOPK, CAP, 2))(routes_keys, routes_turns).reshape((TOKEN_COUNT, TOPK))
    gate_weights = jnp.clip(0.2 + 0.8 * jax.random.uniform(part_splits[5], (TOKEN_COUNT, TOPK), jnp.float32) ** levels(part_splits[5], (TOKEN_COUNT, TOPK), ((0, 16),), -0.2, 0.2), 0.2, 1.0)
    expert_in = noise(seeds[6], (N_EP, D, 2 * HID_DEV), D ** -0.5, 0.0625, ((0, 16),))
    expert_down = noise(seeds[7], (N_EP, HID_DEV, D), FF ** -0.5, 0.125, ((0, 16),))
    kv_down = noise(seeds[8], (D, LATENT), D ** -0.5, 0.0625, ((0, 16),))
    parents = draw_parents(jax.random.fold_in(jax.random.fold_in(seeds[13], part), 71), part)
    lengths = draw_lengths(jax.random.fold_in(jax.random.fold_in(seeds[13], part), 71), part)
    queries = draw_queries(jax.random.fold_in(jax.random.fold_in(seeds[13], part), 71), part)
    cache = draw_cache(jax.random.fold_in(jax.random.fold_in(seeds[13], part), 71), part)
    return {"hidden": hidden, "ffn_gain": ffn_gain, "attn_gain": attn_gain, "latent_norm_gain": latent_norm_gain, "routes": routes, "gate_weights": gate_weights, "expert_in": expert_in, "expert_down": expert_down, "kv_down": kv_down, "parents": parents, "lengths": lengths, "queries": queries, "cache": cache}


softmax_scale = 192.0 ** (-0.5)

def normalized_rows(values, gain):
    return values * lax.rsqrt(lax.optimization_barrier(jnp.mean(values * values, axis=-1, keepdims=True)) + 1e-06) * gain

def ancestors(parents):
    count = parents.shape[1]
    link = (parents[:, :, None] == jnp.arange(count, dtype=jnp.int32)[None, None, :]).astype(jnp.float32)
    reach = jnp.eye(count, dtype=jnp.float32)[None] + link
    for _ in range(max(1, (count - 1).bit_length())):
        reach = jnp.minimum(jnp.einsum('rij,rjk->rik', reach, reach, precision=lax.Precision.HIGHEST), 1.0)
    return reach

def apply_rotation(part, token_position):
    half = part.shape[-1] // 2
    index = jnp.arange(half, dtype=jnp.float32)
    inverse = 10000.0 ** (-2.0 * index / part.shape[-1])
    angle = token_position[:, None] * inverse[None, :]
    first = part[:, :half]
    second = part[:, half:]
    return jnp.concatenate([first * jnp.cos(angle) - second * jnp.sin(angle), first * jnp.sin(angle) + second * jnp.cos(angle)], axis=-1)

def slot_table(route_blocks, expert):
    blocks = route_blocks.shape[0]
    flat = route_blocks.reshape(blocks, -1)
    hits = (flat == expert).astype(jnp.float32)
    ranks = jnp.cumsum(hits, axis=1) - hits
    placed = hits[:, :, None] * (ranks[:, :, None] == jnp.arange(CAP, dtype=jnp.float32)[None, None, :]).astype(jnp.float32)
    return placed.reshape(blocks, TOK_DEV, TOPK, CAP)

def reference(hidden, ffn_gain, attn_gain, latent_norm_gain, routes, gate_weights, expert_in, expert_down, kv_down, parents, lengths, queries, cache):
    source = hidden.astype(jnp.float32)
    units = normalized_rows(source, ffn_gain).astype(jnp.bfloat16)
    unit_blocks = units.reshape(N_EP, TOK_DEV, D).astype(jnp.float32)
    route_blocks = routes.reshape(N_EP, TOK_DEV, TOPK)
    gate_blocks = gate_weights.reshape(N_EP, TOK_DEV, TOPK)

    def dispatch(expert):
        placed = slot_table(route_blocks, expert)
        chosen = lax.optimization_barrier(jnp.sum(placed, axis=2))
        rows = jnp.einsum('stc,std->scd', chosen, unit_blocks).astype(jnp.bfloat16)
        weights = jnp.einsum('stk,stkc->stc', gate_blocks, placed)
        return (rows, weights)
    dispatched, combine = lax.map(dispatch, jnp.arange(EXPERTS, dtype=jnp.int32))

    def slice_step(totals, index):
        expert = index // SPLIT
        rows = dispatched[expert].reshape(N_EP * CAP, D)
        proj = jnp.dot(rows, expert_in[index], preferred_element_type=jnp.float32)
        act = (jax.nn.silu(proj[:, :HID_DEV]) * proj[:, HID_DEV:]).astype(jnp.bfloat16)
        partial_value = jnp.dot(act, expert_down[index], preferred_element_type=jnp.float32).astype(jnp.bfloat16)
        return (totals.at[expert].add(partial_value.astype(jnp.float32)), None)
    start = jnp.zeros((EXPERTS, N_EP * CAP, D), jnp.float32)
    expert_out, _ = lax.scan(slice_step, start, jnp.arange(N_EP, dtype=jnp.int32))
    expert_out = expert_out.reshape(EXPERTS, N_EP, CAP, D)
    moe = jnp.einsum('estc,escd->std', combine, expert_out, precision=lax.Precision.HIGHEST).reshape(TOKEN_COUNT, D)
    mixed = source + moe
    residual_after_expert = mixed.astype(jnp.bfloat16)
    normed = normalized_rows(mixed, attn_gain).astype(jnp.bfloat16)
    compressed_rows = jnp.dot(normed, kv_down, preferred_element_type=jnp.float32)
    reach = ancestors(parents)
    depth = lax.optimization_barrier(jnp.sum(reach, axis=-1)) - 1.0
    token_position = (lengths[:, None].astype(jnp.float32) + depth).reshape(TOKEN_COUNT)
    latent_rows = normalized_rows(compressed_rows[:, :KEY_VALUE_RANK], latent_norm_gain)
    draft_latent_entries = jnp.concatenate([latent_rows, apply_rotation(compressed_rows[:, KEY_VALUE_RANK:], token_position)], axis=-1).astype(jnp.bfloat16)
    query_blocks = queries.reshape(REQUESTS, NODES * HEAD_COUNT, LATENT)
    draft_node_keys = draft_latent_entries.reshape(REQUESTS, NODES, LATENT)

    def attend(items):
        query, key_rows, self_entries, allowed, length = items
        ctx_scores = jnp.dot(query, key_rows.T, preferred_element_type=jnp.float32) * softmax_scale
        valid = jnp.arange(CTX, dtype=jnp.int32)[None, :] < length
        ctx_scores = jnp.where(valid, ctx_scores, -jnp.inf)
        own_scores = jnp.dot(query, self_entries.T, preferred_element_type=jnp.float32) * softmax_scale
        mask = jnp.repeat(allowed, HEAD_COUNT, axis=0) > 0.5
        own_scores = jnp.where(mask, own_scores, -jnp.inf)
        top = jnp.maximum(lax.optimization_barrier(jnp.max(ctx_scores, axis=-1, keepdims=True)), lax.optimization_barrier(jnp.max(own_scores, axis=-1, keepdims=True)))
        ctx_exp = jnp.exp(ctx_scores - top)
        own_exp = jnp.exp(own_scores - top)
        total = lax.optimization_barrier(jnp.sum(ctx_exp, axis=-1, keepdims=True)) + lax.optimization_barrier(jnp.sum(own_exp, axis=-1, keepdims=True))
        context_probabilities = (ctx_exp / total).astype(jnp.bfloat16)
        self_probabilities = (own_exp / total).astype(jnp.bfloat16)
        final_result = jnp.dot(context_probabilities, key_rows[:, :KEY_VALUE_RANK], preferred_element_type=jnp.float32)
        final_result = final_result + jnp.dot(self_probabilities, self_entries[:, :KEY_VALUE_RANK], preferred_element_type=jnp.float32)
        return final_result.astype(jnp.bfloat16)
    attention_output = lax.map(attend, (query_blocks, cache, draft_node_keys, reach, lengths))
    return (residual_after_expert, draft_latent_entries, attention_output.reshape(TOKEN_COUNT, HEAD_COUNT, KEY_VALUE_RANK))
```

```python
import functools

import jax
import jax.numpy as jnp
from jax import lax
from jax.experimental import pallas as pl
from jax.experimental.pallas import tpu as pltpu
from jax.sharding import PartitionSpec as P

KEY_VALUE_RANK = 512
NODES = 16
EXPERTS = 4
CAP = 9
TAIL = 128
ROWS = 40
BF = jnp.bfloat16
F32 = jnp.float32
softmax_scale = 192.0 ** (-0.5)
VMEM = 48 * 1024 * 1024


def iota(shape, dim):
    return lax.broadcasted_iota(jnp.int32, shape, dim)


def dot(a, b):
    return jnp.dot(a, b, preferred_element_type=F32)


def dot_t(a, b):
    return lax.dot_general(a, b, (((1,), (1,)), ((), ())), preferred_element_type=F32)


def params(semantics=None):
    return pltpu.CompilerParams(vmem_limit_bytes=VMEM, dimension_semantics=semantics)


def whole(shape):
    zeros = (0,) * len(shape)
    return pl.BlockSpec(shape, lambda *_: zeros)


def pack_kernel(e_ref, hidden_ref, gain_ref, routes_ref, gates_ref, *outs):
    chunks, parts = outs[:EXPERTS], outs[EXPERTS:]
    tokens, width = hidden_ref.shape
    piece = width // 8
    quarter = width // EXPERTS
    x = hidden_ref[...].astype(F32)
    scale = lax.rsqrt(jnp.mean(x * x, axis=-1, keepdims=True) + 1e-06)
    units = (x * scale * gain_ref[...]).astype(BF)
    first = jnp.broadcast_to(routes_ref[0:1, :], (8, tokens))
    second = jnp.broadcast_to(routes_ref[1:2, :], (8, tokens))
    row = iota((8, tokens), 0)
    before = (iota((tokens, tokens), 0) < iota((tokens, tokens), 1)).astype(BF)
    main, ninth = [], []
    for k in range(EXPERTS):
        expert = e_ref[0] ^ k
        hit = jnp.where((first == expert) | (second == expert), 1.0, 0.0)
        rank = dot(hit.astype(BF), before)
        main.append(jnp.where(rank == row.astype(F32), hit, 0.0))
        ninth.append(jnp.where(rank == 8.0, hit, 0.0))
    main = jnp.concatenate(main, axis=0).astype(BF)
    ninth = jnp.concatenate(ninth, axis=0)
    rows = iota(ninth.shape, 0) % 8
    picked = dot(main, units).astype(BF)
    cut = jnp.zeros((8 * EXPERTS, piece), F32)
    for j in range(8):
        cut = cut + dot(
            jnp.where(rows == j, ninth, 0.0).astype(BF), units[:, j * piece : (j + 1) * piece]
        )
    cut = cut.astype(BF)
    info = jnp.where(row == 0, first.astype(F32), second.astype(F32))
    for choice in range(2):
        gate = jnp.broadcast_to(gates_ref[choice : choice + 1, :], (8, tokens))
        for part in range(3):
            rounded = gate.astype(BF).astype(F32)
            info = jnp.where(row == 2 + 3 * choice + part, rounded, info)
            gate = gate - rounded
    spread = (iota((tokens, TAIL), 0) == iota((tokens, TAIL), 1)).astype(BF)
    tail = dot(info.astype(BF), spread).astype(BF)
    for k in range(EXPERTS):
        expert = e_ref[0] ^ k
        chunks[k][:, :width] = picked[8 * k : 8 * k + 8]
        chunks[k][:, width : width + piece] = cut[8 * k : 8 * k + 8]
        chunks[k][:, width + piece :] = tail
        start = pl.multiple_of(expert * quarter, 128)
        parts[k][...] = hidden_ref[:, pl.ds(start, quarter)]


def pack(e, hidden, gain, routes_t, gates_t):
    tokens, width = hidden.shape
    chunk = jax.ShapeDtypeStruct((8, width + width // 8 + TAIL), BF)
    part = jax.ShapeDtypeStruct((tokens, width // EXPERTS), BF)
    return pl.pallas_call(
        pack_kernel,
        out_shape=[chunk] * EXPERTS + [part] * EXPERTS,
        grid_spec=pltpu.PrefetchScalarGridSpec(
            num_scalar_prefetch=1,
            grid=(1,),
            in_specs=[
                whole(hidden.shape),
                whole(gain.shape),
                whole(routes_t.shape),
                whole(gates_t.shape),
            ],
            out_specs=[whole(chunk.shape)] * EXPERTS + [whole(part.shape)] * EXPERTS,
        ),
        compiler_params=params(),
        name="pack",
    )(e, hidden, gain, routes_t, gates_t)


def expert_kernel(split, steps, piece, hid, e_ref, *refs):
    groups = refs[:split]
    w_in, w_out, keep, send, acc, act = refs[split:]
    t = pl.program_id(0)
    width = piece * steps
    main_rows, last_rows = 32 * split, 8 * split

    @pl.when(t < steps)
    def _():
        start = pl.multiple_of(t * piece, 128)
        ext = jnp.concatenate([g[:, width : width + piece] for g in groups], axis=0)
        r = iota((last_rows, main_rows), 0)
        col = iota((last_rows, main_rows), 1)
        want = 32 * (r // 8) + 8 * (r % 8) + t
        pick = jnp.where((r % 8 < 4) & (col == want), 1.0, 0.0).astype(BF)
        last = dot(pick, ext).astype(BF)
        rows = jnp.concatenate([g[:, pl.ds(start, piece)] for g in groups] + [last], axis=0)
        term = dot(rows, w_in[0])

        @pl.when(t == 0)
        def _():
            acc[...] = term

        @pl.when(t > 0)
        def _():
            acc[...] += term

    @pl.when(t >= steps)
    def _():
        @pl.when(t == steps)
        def _():
            gate, up = acc[:, :hid], acc[:, hid:]
            act[...] = (gate / (1.0 + jnp.exp(-gate)) * up).astype(BF)

        out = dot(act[...], w_out[0])
        for r in range(split):
            mine = jnp.concatenate(
                [out[32 * r : 32 * r + 32], out[main_rows + 8 * r : main_rows + 8 * r + 8]], axis=0
            ).astype(BF)
            (send if r % 2 else keep)[r // 2, 0] = mine


def expert_slice(e, groups, w_in, w_out):
    split = len(groups)
    width, hid2 = w_in.shape[1:]
    hid = hid2 // 2
    steps = 8
    piece = width // steps
    quarter = width // EXPERTS
    out = jax.ShapeDtypeStruct((split // 2, EXPERTS, ROWS, quarter), BF)
    out_spec = pl.BlockSpec(
        (split // 2, 1, ROWS, quarter), lambda t, e: (0, jnp.maximum(t - steps, 0), 0, 0)
    )
    rows = ROWS * split
    return pl.pallas_call(
        functools.partial(expert_kernel, split, steps, piece, hid),
        out_shape=[out, out],
        grid_spec=pltpu.PrefetchScalarGridSpec(
            num_scalar_prefetch=1,
            grid=(steps + EXPERTS,),
            in_specs=[whole(g.shape) for g in groups]
            + [
                pl.BlockSpec((1, piece, hid2), lambda t, e: (0, jnp.minimum(t, steps - 1), 0)),
                pl.BlockSpec(
                    (1, hid, quarter), lambda t, e: (0, 0, e[0] ^ jnp.maximum(t - steps, 0))
                ),
            ],
            out_specs=[out_spec, out_spec],
            scratch_shapes=[pltpu.VMEM((rows, hid2), F32), pltpu.VMEM((rows, hid), BF)],
        ),
        compiler_params=params(("arbitrary",)),
        cost_estimate=pl.CostEstimate(
            flops=6 * rows * width * hid, bytes_accessed=6 * width * hid, transcendentals=rows * hid
        ),
        name="experts",
    )(e, *groups, w_in, w_out)


def combine_kernel(split, tokens, e_ref, *refs):
    outs_e, hid = refs[:EXPERTS], refs[EXPERTS : 2 * EXPERTS]
    info_ref, gain_ref = refs[2 * EXPERTS : 2 * EXPERTS + 2]
    kvs = refs[2 * EXPERTS + 2 : 2 * EXPERTS + 2 + split]
    rest = refs[2 * EXPERTS + 2 + split :]
    sums, residuals = rest[:EXPERTS], rest[EXPERTS : 2 * EXPERTS]
    kv_ref, sem = rest[2 * EXPERTS :]
    part = kvs[0].shape[0]
    lat = kvs[0].shape[1]
    copies = []
    for r in range(split):
        place = pl.multiple_of((e_ref[1] ^ r) * part, 16)
        copies.append(
            pltpu.make_async_copy(kvs[r], kv_ref.at[pl.ds(place, part), :], sem.at[r])
        )
        copies[-1].start()
    one = (iota((tokens, TAIL), 0) == iota((tokens, TAIL), 1)).astype(BF)
    info = dot_t(one, info_ref[...])
    earlier = (iota((tokens, tokens), 1) < iota((tokens, tokens), 0)).astype(BF)
    lane = iota((tokens, ROWS), 1).astype(F32)
    hits = []
    for k in range(EXPERTS):
        expert = (e_ref[0] ^ k).astype(F32)
        hits.append(jnp.where(info == expert, 1.0, 0.0))
    moe = None
    for k in range(EXPERTS):
        blocks = [[], [], []]
        for s in range(EXPERTS):
            h0 = hits[k][:, 8 * s : 8 * s + 1]
            h1 = hits[k][:, 8 * s + 1 : 8 * s + 2]
            hit = jnp.broadcast_to(h0 + h1, (tokens, ROWS))
            rank = dot(earlier, hit.astype(BF))
            line = s ^ k
            want = jnp.where(rank < 8.0, rank + 8.0 * line, 32.0 + line)
            chosen = (lane == want) & (hit > 0.5)
            for p in range(3):
                g0 = info[:, 8 * s + 2 + p : 8 * s + 3 + p]
                g1 = info[:, 8 * s + 5 + p : 8 * s + 6 + p]
                gate = jnp.broadcast_to(h0 * g0 + h1 * g1, (tokens, ROWS))
                blocks[p].append(jnp.where(chosen, gate, 0.0))
        weights = jnp.concatenate(blocks[0] + blocks[1] + blocks[2], axis=0).astype(BF)
        term = dot(weights, outs_e[k][...])
        moe = term if moe is None else moe + term
    total = EXPERTS * tokens
    moe = moe[:total] + moe[total : 2 * total] + moe[2 * total :]
    mixed = jnp.concatenate([h[...].astype(F32) for h in hid], axis=0) + moe
    for s in range(EXPERTS):
        residuals[s][...] = mixed[s * tokens : (s + 1) * tokens].astype(BF)
    square = jnp.sum(mixed * mixed, axis=-1, keepdims=True)
    scaled = (mixed * gain_ref[...]).astype(BF)
    for c in copies:
        c.wait()
    rows = dot(scaled, kv_ref[...])
    for s in range(EXPERTS):
        sums[s][:, :lat] = rows[s * tokens : (s + 1) * tokens]
        sums[s][:, lat:] = jnp.broadcast_to(
            square[s * tokens : (s + 1) * tokens], (tokens, sums[s].shape[1] - lat)
        )


def combine(place, outs_e, hid, line, gain, kvs):
    split = len(kvs)
    tokens, quarter = hid[0].shape
    part, lat = kvs[0].shape
    padded = (lat // 128 + 1) * 128
    tail_block = line.shape[1] // TAIL - 1
    sums = jax.ShapeDtypeStruct((tokens, padded), F32)
    residual = jax.ShapeDtypeStruct((tokens, quarter), BF)
    return pl.pallas_call(
        functools.partial(combine_kernel, split, tokens),
        out_shape=[sums] * EXPERTS + [residual] * EXPERTS,
        grid_spec=pltpu.PrefetchScalarGridSpec(
            num_scalar_prefetch=1,
            grid=(1,),
            in_specs=[whole(o.shape) for o in outs_e]
            + [whole(h.shape) for h in hid]
            + [
                pl.BlockSpec((line.shape[0], TAIL), lambda t, e: (0, tail_block)),
                pl.BlockSpec((1, quarter), lambda t, e: (0, e[0])),
            ]
            + [pl.BlockSpec(memory_space=pl.ANY)] * split,
            out_specs=[whole(sums.shape)] * EXPERTS + [whole(residual.shape)] * EXPERTS,
            scratch_shapes=[
                pltpu.VMEM((split * part, lat), BF),
                pltpu.SemaphoreType.DMA((split,)),
            ],
        ),
        compiler_params=params(),
        name="combine",
    )(place, *outs_e, *hid, line, gain, *kvs)


def cached_kernel(length_ref, q_ref, cache_ref, out_ref, top_ref, sum_ref, keys_ref):
    nodes, lat, heads = q_ref.shape
    ctx = cache_ref.shape[2]

    @pl.when(pl.program_id(0) == 0)
    def _():
        keys_ref[...] = cache_ref[0].T

    q = jnp.concatenate([q_ref[i] for i in range(nodes)], axis=1)
    scores = dot(keys_ref[...], q) * softmax_scale
    valid = iota((ctx, nodes * heads), 0) < length_ref[0]
    scores = jnp.where(valid, scores, -jnp.inf)
    top = jnp.max(scores, axis=0, keepdims=True)
    weight = jnp.exp(scores - top)
    total = jnp.sum(weight, axis=0, keepdims=True)
    out = dot(cache_ref[0, :KEY_VALUE_RANK, :], weight.astype(BF)) * (1.0 / total)
    for i in range(nodes):
        span = slice(i * heads, (i + 1) * heads)
        out_ref[i] = out[:, span].T.astype(out_ref.dtype)
        top_ref[i] = top[:, span]
        sum_ref[i] = total[:, span]


def cached_attention(lengths, q_t, cache_t, first, count, per=2):
    tokens, lat, heads = q_t.shape
    ctx = cache_t.shape[2]
    row = jax.ShapeDtypeStruct((count, 1, heads), F32)
    begin = first // per
    return pl.pallas_call(
        cached_kernel,
        out_shape=[jax.ShapeDtypeStruct((count, heads, KEY_VALUE_RANK), BF), row, row],
        grid_spec=pltpu.PrefetchScalarGridSpec(
            num_scalar_prefetch=1,
            grid=(count // per,),
            in_specs=[
                pl.BlockSpec((per, lat, heads), lambda t, n: (t + begin, 0, 0)),
                whole(cache_t.shape),
            ],
            out_specs=[
                pl.BlockSpec((per, heads, KEY_VALUE_RANK), lambda t, n: (t, 0, 0)),
                pl.BlockSpec((per, 1, heads), lambda t, n: (t, 0, 0)),
                pl.BlockSpec((per, 1, heads), lambda t, n: (t, 0, 0)),
            ],
            scratch_shapes=[pltpu.VMEM((ctx, lat), BF)],
        ),
        compiler_params=params(("arbitrary",)),
        cost_estimate=pl.CostEstimate(
            flops=2 * count * heads * ctx * (lat + KEY_VALUE_RANK),
            bytes_accessed=2 * count * heads * (lat + KEY_VALUE_RANK),
            transcendentals=count * heads * ctx,
        ),
        name="cached",
    )(lengths, q_t, cache_t)


def final_kernel(width, *refs):
    sums = refs[:EXPERTS]
    gain_ref, turn_ref, allow_ref, q_ref, ctx_ref, top_ref, sum_ref = refs[EXPERTS : EXPERTS + 7]
    entry_ref, out_ref, keys_ref = refs[EXPERTS + 7 :]
    nodes, lat, heads = q_ref.shape

    @pl.when(pl.program_id(0) == 0)
    def _():
        raw = sums[0][...] + sums[1][...] + sums[2][...] + sums[3][...]
        scale = lax.rsqrt(raw[:, lat : lat + 1] / width + 1e-06)
        raw = raw * scale
        head = raw[:, :KEY_VALUE_RANK]
        head = head * lax.rsqrt(jnp.mean(head * head, axis=-1, keepdims=True) + 1e-06)
        head = head * gain_ref[...]
        tail = raw[:, KEY_VALUE_RANK:]
        half = (lat - KEY_VALUE_RANK) // 2
        lanes = tail.shape[1]
        tail = (
            tail * turn_ref[0]
            + pltpu.roll(tail, lanes - half, 1) * turn_ref[1]
            + pltpu.roll(tail, half, 1) * turn_ref[2]
        )
        entries = jnp.concatenate([head, tail], axis=1).astype(BF)[:, :lat]
        entry_ref[...] = entries
        keys_ref[...] = entries

    keys = keys_ref[...]
    count = keys.shape[0]
    for i in range(nodes):
        scores = dot(keys, q_ref[i]) * softmax_scale
        scores = jnp.where(allow_ref[i] > 0.5, scores, -jnp.inf)
        old = top_ref[i]
        top = jnp.maximum(old, jnp.max(scores, axis=0, keepdims=True))
        weight = jnp.exp(scores - top)
        share = sum_ref[i] * jnp.exp(old - top)
        scale = 1.0 / (share + jnp.sum(weight, axis=0, keepdims=True))
        both = jnp.concatenate(
            [weight * scale, jnp.broadcast_to(share * scale, (8, heads))], axis=0
        ).T
        out = ctx_ref[i].astype(F32) * both[:, count : count + 1]
        out = out + dot(both[:, :count].astype(BF), keys[:, :KEY_VALUE_RANK])
        out_ref[i] = out.astype(BF)


def final_attention(width, sums, gain, turn, allow, q_t, ctx_out, top, total, per=4):
    tokens, lat, heads = q_t.shape
    row = pl.BlockSpec((per, 1, heads), lambda t: (t, 0, 0))
    wide = pl.BlockSpec((per, heads, KEY_VALUE_RANK), lambda t: (t, 0, 0))
    return pl.pallas_call(
        functools.partial(final_kernel, width),
        out_shape=[
            jax.ShapeDtypeStruct((tokens, lat), BF),
            jax.ShapeDtypeStruct((tokens, heads, KEY_VALUE_RANK), BF),
        ],
        grid=(tokens // per,),
        in_specs=[whole(s.shape) for s in sums]
        + [
            whole(gain.shape),
            whole(turn.shape),
            pl.BlockSpec((per, NODES, heads), lambda t: (t, 0, 0)),
            pl.BlockSpec((per, lat, heads), lambda t: (t, 0, 0)),
            wide,
            row,
            row,
        ],
        out_specs=[whole((tokens, lat)), wide],
        scratch_shapes=[pltpu.VMEM((tokens, lat), BF)],
        compiler_params=params(("arbitrary",)),
        name="final",
    )(*sums, gain, turn, allow, q_t, ctx_out, top, total)


def place_kernel(e_ref, *refs):
    out_ref = refs[EXPERTS]
    quarter = refs[0].shape[1]
    for k in range(EXPERTS):
        start = pl.multiple_of((e_ref[0] ^ k) * quarter, 128)
        out_ref[:, pl.ds(start, quarter)] = refs[k][...]


def place_quarters(place, parts):
    tokens, quarter = parts[0].shape
    return pl.pallas_call(
        place_kernel,
        out_shape=jax.ShapeDtypeStruct((tokens, EXPERTS * quarter), BF),
        grid_spec=pltpu.PrefetchScalarGridSpec(
            num_scalar_prefetch=1,
            grid=(1,),
            in_specs=[whole(p.shape) for p in parts],
            out_specs=whole((tokens, EXPERTS * quarter)),
        ),
        compiler_params=params(),
        name="place",
    )(place, *parts)


def tree(parents, lengths, rank, lat):
    count = parents.shape[1]
    link = (parents[0][:, None] == jnp.arange(count, dtype=jnp.int32)[None, :]).astype(F32)
    reach = jnp.eye(count, dtype=F32) + link
    for _ in range(max(1, (count - 1).bit_length())):
        reach = jnp.minimum(jnp.dot(reach, reach, precision=lax.Precision.HIGHEST), 1.0)
    depth = jnp.sum(reach, axis=-1) - 1.0
    position = lengths.astype(F32) + depth
    half = (lat - rank) // 2
    index = jnp.arange(half, dtype=F32)
    inverse = 10000.0 ** (-2.0 * index / (2 * half))
    angle = position[:, None] * inverse[None, :]
    c, s = jnp.cos(angle), jnp.sin(angle)
    gap = jnp.zeros((count, 128 - 2 * half), F32)
    none = jnp.zeros_like(s)
    turn = jnp.stack(
        [
            jnp.concatenate([c, c, gap], axis=1),
            jnp.concatenate([-s, none, gap], axis=1),
            jnp.concatenate([none, s, gap], axis=1),
        ]
    )
    return reach, turn


def local(
    hidden,
    ffn_gain,
    attn_gain,
    latent_norm_gain,
    routes,
    gate_weights,
    expert_in,
    expert_down,
    kv_down,
    parents,
    lengths,
    queries,
    cache,
):
    size = lax.axis_size("ep")
    split = size // EXPERTS
    bits = [1 << b for b in range(split.bit_length() - 1)]
    width = hidden.shape[1]
    lat = kv_down.shape[1]
    heads = queries.shape[1]
    index = lax.axis_index("ep")
    place = jnp.stack([index // split, index % split]).astype(jnp.int32)

    def swap(x, bit):
        return lax.ppermute(x, "ep", [(i, i ^ bit) for i in range(size)])

    packed = pack(place, hidden, ffn_gain[None], routes.T, gate_weights.T)
    chunks, quarters = packed[:EXPERTS], packed[EXPERTS:]
    line = [chunks[0]] + [swap(chunks[k], k * split) for k in range(1, EXPERTS)]
    line = jnp.concatenate(line, axis=0)
    groups = {0: line}
    for bit in reversed(bits):
        for r in sorted(groups):
            groups[r ^ bit] = swap(groups[r], bit)
    groups = [groups[r] for r in range(split)]
    kvs = {0: kv_down}
    for bit in reversed(bits):
        for r in sorted(kvs):
            kvs[r ^ bit] = swap(kvs[r], bit)
    kvs = [kvs[r] for r in range(split)]
    own_quarters = [quarters[0]] + [swap(quarters[k], k * split) for k in range(1, EXPERTS)]

    q_t = jnp.transpose(queries, (0, 2, 1))
    cache_t = jnp.transpose(cache, (0, 2, 1))
    ctx_out, top, total = cached_attention(lengths, q_t, cache_t, 0, queries.shape[0])
    reach, turn = tree(parents, lengths, KEY_VALUE_RANK, lat)
    allow = jnp.broadcast_to(reach[:, :, None], reach.shape + (heads,))

    keep, send = expert_slice(place, groups, expert_in, expert_down)
    terms = [keep, swap(send, bits[0])]
    for bit in bits[1:]:
        out = sum(t[1::2].astype(F32) for t in terms).astype(BF)
        terms = [t[0::2] for t in terms] + [swap(out, bit)]
    sums = [
        sum(t[0, k].astype(F32) for t in terms).astype(BF) for k in range(EXPERTS)
    ]
    outs_e = [sums[0]] + [swap(sums[k], k * split) for k in range(1, EXPERTS)]

    mixed = combine(place, outs_e, own_quarters, line, attn_gain[None], kvs)
    rows, residuals = mixed[:EXPERTS], mixed[EXPERTS:]
    rows = [rows[0]] + [swap(rows[k], k * split) for k in range(1, EXPERTS)]
    residuals = [residuals[0]] + [swap(residuals[k], k * split) for k in range(1, EXPERTS)]
    entries, attention = final_attention(
        width, rows, latent_norm_gain[None], turn, allow, q_t, ctx_out, top, total
    )
    return (place_quarters(place, residuals), entries, attention)


def solution(mesh):
    placed = (
        P(("group", "ep"), None),
        P(),
        P(),
        P(),
        P(("group", "ep"), None),
        P(("group", "ep"), None),
        P("ep", None, None),
        P("ep", None, None),
        P("ep", None),
        P(("group", "ep"), None),
        P(("group", "ep")),
        P(("group", "ep"), None, None),
        P(("group", "ep"), None, None),
    )
    return jax.shard_map(
        local,
        mesh=mesh,
        in_specs=placed,
        out_specs=(
            P(("group", "ep"), None),
            P(("group", "ep"), None),
            P(("group", "ep"), None, None),
        ),
        check_vma=False,
    )
```

```python
import functools

import jax
import jax.numpy as jnp
from jax import lax
from jax.experimental import pallas as pl
from jax.experimental.pallas import tpu as pltpu
from jax.sharding import PartitionSpec as P

KEY_VALUE_RANK = 512
NODES = 16
EXPERTS = 4
CAP = 9
TAIL = 128
ROWS = 40
BF = jnp.bfloat16
F32 = jnp.float32
softmax_scale = 192.0 ** (-0.5)
MIB = 1024 * 1024
COST = pl.CostEstimate(flops=1024, bytes_accessed=1024, transcendentals=0)
LOG2E = 1.4426950408889634


def iota(shape, dim):
    return lax.broadcasted_iota(jnp.int32, shape, dim)


def dot(a, b):
    return jnp.dot(a, b, preferred_element_type=F32)


def dot_t(a, b):
    return lax.dot_general(a, b, (((1,), (1,)), ((), ())), preferred_element_type=F32)


def params(mib, semantics=None):
    return pltpu.CompilerParams(vmem_limit_bytes=mib * MIB, dimension_semantics=semantics)


def after(x, *others):
    return lax.optimization_barrier((x, others))[0]


def whole(shape):
    zeros = (0,) * len(shape)
    return pl.BlockSpec(shape, lambda *_: zeros)


def pack_kernel(e_ref, *refs):
    ins, outs = refs[:4], refs[4 : 4 + 2 * EXPERTS]
    held, sem = refs[4 + 2 * EXPERTS : -1], refs[-1]
    copies = [pltpu.make_async_copy(a, b, sem.at[i]) for i, (a, b) in enumerate(zip(ins, held))]
    for c in copies:
        c.start()
    for c in copies:
        c.wait()
    hidden_ref, gain_ref, routes_ref, gates_ref = held
    chunks, parts = outs[:EXPERTS], outs[EXPERTS:]
    tokens, width = hidden_ref.shape
    piece = width // 8
    quarter = width // EXPERTS
    x = hidden_ref[...].astype(F32)
    scale = lax.rsqrt(jnp.mean(x * x, axis=-1, keepdims=True) + 1e-06)
    units = (x * scale * gain_ref[...]).astype(BF)
    first = jnp.broadcast_to(routes_ref[0:1, :], (8, tokens))
    second = jnp.broadcast_to(routes_ref[1:2, :], (8, tokens))
    row = iota((8, tokens), 0)
    before = (iota((tokens, tokens), 0) < iota((tokens, tokens), 1)).astype(BF)
    main, ninth = [], []
    for k in range(EXPERTS):
        expert = e_ref[0] ^ k
        hit = jnp.where((first == expert) | (second == expert), 1.0, 0.0)
        rank = dot(hit.astype(BF), before)
        main.append(jnp.where(rank == row.astype(F32), hit, 0.0))
        ninth.append(jnp.where(rank == 8.0, hit, 0.0))
    main = jnp.concatenate(main, axis=0).astype(BF)
    ninth = jnp.concatenate(ninth, axis=0)
    rows = iota(ninth.shape, 0) % 8
    picked = dot(main, units).astype(BF)
    cut = jnp.zeros((8 * EXPERTS, piece), F32)
    for j in range(8):
        cut = cut + dot(
            jnp.where(rows == j, ninth, 0.0).astype(BF), units[:, j * piece : (j + 1) * piece]
        )
    cut = cut.astype(BF)
    info = jnp.where(row == 0, first.astype(F32), second.astype(F32))
    for choice in range(2):
        gate = jnp.broadcast_to(gates_ref[choice : choice + 1, :], (8, tokens))
        for part in range(3):
            rounded = gate.astype(BF).astype(F32)
            info = jnp.where(row == 2 + 3 * choice + part, rounded, info)
            gate = gate - rounded
    spread = (iota((tokens, TAIL), 0) == iota((tokens, TAIL), 1)).astype(BF)
    tail = dot(info.astype(BF), spread).astype(BF)
    for k in range(EXPERTS):
        expert = e_ref[0] ^ k
        chunks[k][:, :width] = picked[8 * k : 8 * k + 8]
        chunks[k][:, width : width + piece] = cut[8 * k : 8 * k + 8]
        chunks[k][:, width + piece :] = tail
        start = pl.multiple_of(expert * quarter, 128)
        parts[k][...] = hidden_ref[:, pl.ds(start, quarter)]


def pack(e, hidden, gain, routes_t, gates_t):
    tokens, width = hidden.shape
    chunk = jax.ShapeDtypeStruct((8, width + width // 8 + TAIL), BF)
    part = jax.ShapeDtypeStruct((tokens, width // EXPERTS), BF)
    hbm = pl.BlockSpec(memory_space=pltpu.HBM)
    vmem = pl.BlockSpec(memory_space=pltpu.VMEM)
    given = [hidden, gain, routes_t, gates_t]
    placed = [pltpu.with_memory_space_constraint(a, pltpu.HBM) for a in given]
    return pl.pallas_call(
        pack_kernel,
        out_shape=[chunk] * EXPERTS + [part] * EXPERTS,
        in_specs=[pl.BlockSpec(memory_space=pltpu.SMEM)] + [hbm] * 4,
        out_specs=[vmem] * (2 * EXPERTS),
        scratch_shapes=[pltpu.VMEM(a.shape, a.dtype) for a in given]
        + [pltpu.SemaphoreType.DMA((4,))],
        compiler_params=params(8),
        cost_estimate=COST,
        name="pack",
    )(e, *placed)


def down(split, e_ref, act, w_out, keep, send, first):
    quarter = keep.shape[3]
    step = quarter // 2
    main_rows = 32 * split
    for k in range(keep.shape[1]):
        start = (e_ref[0] ^ (first + k)) * quarter
        for h in range(2):
            columns = pl.ds(pl.multiple_of(start + h * step, 128), step)
            out = dot(act[...], w_out[0, :, columns])
            for r in range(split):
                lower = out[32 * r : 32 * r + 32]
                upper = out[main_rows + 8 * r : main_rows + 8 * r + 8]
                mine = jnp.concatenate([lower, upper], axis=0).astype(BF)
                (send if r % 2 else keep)[r // 2, k, :, h * step : (h + 1) * step] = mine


def expert_kernel(split, e_ref, *refs):
    groups = refs[:split]
    w_in, w_out, act, keep, send, x = refs[split:]
    width = w_in.shape[1]
    hid = act.shape[1]
    piece = width // 8
    main_rows, last_rows = 32 * split, 8 * split
    for r in range(split):
        x[32 * r : 32 * r + 32, :] = groups[r][:, :width]
    ext = jnp.concatenate([g[:, width : width + piece] for g in groups], axis=0)
    row = iota((8 * last_rows, main_rows), 0)
    col = iota((8 * last_rows, main_rows), 1)
    place = row % last_rows
    want = 32 * (place // 8) + 8 * (place % 8) + row // last_rows
    pick = jnp.where((place % 8 < 4) & (col == want), 1.0, 0.0).astype(BF)
    last = dot(pick, ext).astype(BF)
    for j in range(8):
        x[main_rows:, j * piece : (j + 1) * piece] = last[j * last_rows : (j + 1) * last_rows]
    step = min(256, hid)
    for i in range(hid // step):
        gate = dot(x[...], w_in[0, :, i * step : (i + 1) * step])
        up = dot(x[...], w_in[0, :, hid + i * step : hid + (i + 1) * step])
        act[:, i * step : (i + 1) * step] = (gate / (1.0 + jnp.exp(-gate)) * up).astype(BF)
    down(split, e_ref, act, w_out, keep, send, 2)


def expert_rest_kernel(split, e_ref, act, w_out, keep, send):
    down(split, e_ref, act, w_out, keep, send, 0)


def expert_slice(e, groups, w_in, w_out):
    split = len(groups)
    width, hid2 = w_in.shape[1:]
    hid = hid2 // 2
    quarter = width // EXPERTS
    half = jax.ShapeDtypeStruct((split // 2, EXPERTS // 2, ROWS, quarter), BF)
    rows = ROWS * split
    act = jax.ShapeDtypeStruct((rows, hid), BF)
    vmem = pl.BlockSpec(memory_space=pltpu.VMEM)
    smem = pl.BlockSpec(memory_space=pltpu.SMEM)
    act, keep_a, send_a = pl.pallas_call(
        functools.partial(expert_kernel, split),
        out_shape=[act, half, half],
        in_specs=[smem] + [vmem] * (split + 2),
        out_specs=[vmem] * 3,
        scratch_shapes=[pltpu.VMEM((rows, width), BF)],
        compiler_params=params(10),
        cost_estimate=COST,
        name="experts",
    )(e, *groups, w_in, w_out)
    keep_b, send_b = pl.pallas_call(
        functools.partial(expert_rest_kernel, split),
        out_shape=[half, half],
        in_specs=[smem] + [vmem] * 2,
        out_specs=[vmem] * 2,
        compiler_params=params(6),
        cost_estimate=COST,
        name="experts_rest",
    )(e, act, w_out)
    return keep_a, send_a, keep_b, send_b


def combine_kernel(split, tokens, e_ref, *refs):
    outs_e, hid = refs[:EXPERTS], refs[EXPERTS : 2 * EXPERTS]
    info_ref, gain_ref = refs[2 * EXPERTS : 2 * EXPERTS + 2]
    kvs = refs[2 * EXPERTS + 2 : 2 * EXPERTS + 2 + split]
    rest = refs[2 * EXPERTS + 2 + split :]
    own_sum, own_part = rest[:2]
    sent = rest[2 : 1 + EXPERTS]
    kv_ref, sem = rest[1 + EXPERTS :]
    part = kvs[0].shape[0]
    lat = kvs[0].shape[1]
    copies = []
    for r in range(split):
        place = pl.multiple_of((e_ref[1] ^ r) * part, 16)
        copies.append(
            pltpu.make_async_copy(kvs[r], kv_ref.at[pl.ds(place, part), :], sem.at[r])
        )
        copies[-1].start()
    one = (iota((tokens, TAIL), 0) == iota((tokens, TAIL), 1)).astype(BF)
    info = dot_t(one, info_ref[...])
    earlier = (iota((tokens, tokens), 1) < iota((tokens, tokens), 0)).astype(BF)
    lane = iota((tokens, ROWS), 1).astype(F32)
    hits = []
    for k in range(EXPERTS):
        expert = (e_ref[0] ^ k).astype(F32)
        hits.append(jnp.where(info == expert, 1.0, 0.0))
    moe = None
    for k in range(EXPERTS):
        blocks = [[], [], []]
        for s in range(EXPERTS):
            h0 = hits[k][:, 8 * s : 8 * s + 1]
            h1 = hits[k][:, 8 * s + 1 : 8 * s + 2]
            hit = jnp.broadcast_to(h0 + h1, (tokens, ROWS))
            rank = dot(earlier, hit.astype(BF))
            line = s ^ k
            want = jnp.where(rank < 8.0, rank + 8.0 * line, 32.0 + line)
            chosen = (lane == want) & (hit > 0.5)
            for p in range(3):
                g0 = info[:, 8 * s + 2 + p : 8 * s + 3 + p]
                g1 = info[:, 8 * s + 5 + p : 8 * s + 6 + p]
                gate = jnp.broadcast_to(h0 * g0 + h1 * g1, (tokens, ROWS))
                blocks[p].append(jnp.where(chosen, gate, 0.0))
        weights = jnp.concatenate(blocks[0] + blocks[1] + blocks[2], axis=0).astype(BF)
        term = dot(weights, outs_e[k][...])
        moe = term if moe is None else moe + term
    total = EXPERTS * tokens
    moe = moe[:total] + moe[total : 2 * total] + moe[2 * total :]
    mixed = jnp.concatenate([h[...].astype(F32) for h in hid], axis=0) + moe
    square = jnp.sum(mixed * mixed, axis=-1, keepdims=True)
    scaled = (mixed * gain_ref[...]).astype(BF)
    for c in copies:
        c.wait()
    rows = dot(scaled, kv_ref[...])
    padded = own_sum.shape[1]
    for s in range(EXPERTS):
        span = slice(s * tokens, (s + 1) * tokens)
        rest = jnp.broadcast_to(square[span], (tokens, padded - lat))
        first = iota(rest.shape, 1) == 0
        if s:
            high = rest.astype(BF).astype(F32)
            sent[s - 1][:, :lat] = rows[span].astype(BF)
            sent[s - 1][:, lat:padded] = jnp.where(first, high, rest - high).astype(BF)
            sent[s - 1][:, padded:] = mixed[span].astype(BF)
        else:
            own_sum[:, :lat] = rows[span]
            own_sum[:, lat:] = jnp.where(first, rest, 0.0)
            own_part[...] = mixed[span].astype(BF)


def combine(place, outs_e, hid, info, gain, kvs):
    split = len(kvs)
    tokens, quarter = hid[0].shape
    part, lat = kvs[0].shape
    padded = (lat // 128 + 1) * 128
    outs = [pltpu.VMEM((tokens, padded), F32), pltpu.VMEM((tokens, quarter), BF)]
    outs += [pltpu.VMEM((tokens, padded + quarter), BF)] * (EXPERTS - 1)
    return pl.pallas_call(
        functools.partial(combine_kernel, split, tokens),
        out_shape=outs,
        grid_spec=pltpu.PrefetchScalarGridSpec(
            num_scalar_prefetch=1,
            grid=(1,),
            in_specs=[whole(o.shape) for o in outs_e]
            + [whole(h.shape) for h in hid]
            + [
                whole(info.shape),
                pl.BlockSpec((1, quarter), lambda t, e: (0, e[0])),
            ]
            + [pl.BlockSpec(memory_space=pl.ANY)] * split,
            out_specs=[whole(o.shape) for o in outs],
            scratch_shapes=[
                pltpu.VMEM((split * part, lat), BF),
                pltpu.SemaphoreType.DMA((split,)),
            ],
        ),
        compiler_params=params(8),
        cost_estimate=COST,
        name="combine",
    )(place, *outs_e, *hid, info, gain, *kvs)


def cached_kernel(begin, per, length_ref, *refs):
    q_hbm, cache_hbm, w_hbm, out_ref, stat_ref, w_ref, q_ref, cache_ref, keys_ref, sem = refs
    nodes, lat, heads = q_ref.shape
    ctx = cache_ref.shape[2]
    spare = keys_ref.shape[1] - lat
    copies = [
        pltpu.make_async_copy(cache_hbm, cache_ref, sem.at[0]),
        pltpu.make_async_copy(q_hbm.at[pl.ds(begin, nodes)], q_ref, sem.at[1]),
        pltpu.make_async_copy(w_hbm, w_ref, sem.at[2]),
    ]
    for c in copies:
        c.start()
    unused = (iota((ctx, spare), 0) >= length_ref[0]) & (iota((ctx, spare), 1) == 0)
    keys_ref[:, lat:] = jnp.where(unused, -jnp.inf, 0.0).astype(BF)
    one = (iota((spare, per * heads), 0) == 0).astype(BF)
    factor = softmax_scale * LOG2E
    copies[0].wait()
    keys_ref[:, :lat] = cache_ref[0].T
    copies[1].wait()

    for g in range(nodes // per):
        q = jnp.concatenate([q_ref[g * per + i] for i in range(per)], axis=1)
        q = jnp.concatenate([q, one], axis=0)
        scores = dot(keys_ref[...], q)
        top = jnp.max(scores, axis=0, keepdims=True) * factor
        weight = jnp.exp2(scores * factor - top)
        total = jnp.sum(weight, axis=0, keepdims=True)
        out = dot(cache_ref[0, :KEY_VALUE_RANK, :], weight.astype(BF)) * (1.0 / total)
        for i in range(per):
            span = slice(i * heads, (i + 1) * heads)
            out_ref[g * per + i] = out[:, span].T.astype(out_ref.dtype)
            stat_ref[g * per + i] = jnp.concatenate([top[:, span], total[:, span]], axis=0)
    copies[2].wait()


def cached_attention(lengths, q_t, cache_t, weight, first, count, per=4):
    tokens, lat, heads = q_t.shape
    ctx = cache_t.shape[2]
    hbm = pl.BlockSpec(memory_space=pltpu.HBM)
    vmem = pl.BlockSpec(memory_space=pltpu.VMEM)
    given = [pltpu.with_memory_space_constraint(a, pltpu.HBM) for a in (q_t, cache_t, weight)]
    return pl.pallas_call(
        functools.partial(cached_kernel, first, per),
        out_shape=[
            pltpu.VMEM((count, heads, KEY_VALUE_RANK), BF),
            pltpu.VMEM((count, 2, heads), F32),
            pltpu.VMEM(weight.shape, weight.dtype),
        ],
        in_specs=[pl.BlockSpec(memory_space=pltpu.SMEM), hbm, hbm, hbm],
        out_specs=[vmem, vmem, vmem],
        scratch_shapes=[
            pltpu.VMEM((count, lat, heads), BF),
            pltpu.VMEM(cache_t.shape, BF),
            pltpu.VMEM((ctx, (lat // 128 + 1) * 128), BF),
            pltpu.SemaphoreType.DMA((3,)),
        ],
        compiler_params=params(16),
        cost_estimate=pl.CostEstimate(
            flops=4 * count * heads * ctx * (lat + KEY_VALUE_RANK),
            bytes_accessed=2 * weight.size,
            transcendentals=count * heads * ctx,
        ),
        name="cached",
    )(lengths, *given)


def final_kernel(width, per, e_ref, *refs):
    own_sum, own_part = refs[:2]
    got = refs[2 : 1 + EXPERTS]
    gain_ref, turn_ref, allow_ref, q_ref = refs[1 + EXPERTS : 5 + EXPERTS]
    halves = refs[5 + EXPERTS : 7 + EXPERTS], refs[7 + EXPERTS : 9 + EXPERTS]
    part_ref, entry_ref, out_hbm, out_ref, sem = refs[9 + EXPERTS :]
    nodes, lat, heads = q_ref.shape
    padded = own_sum.shape[1]
    quarter = own_part.shape[1]
    raw = own_sum[...]
    for g in got:
        raw = raw + g[:, :padded].astype(F32)
    square = raw[:, lat : lat + 1] + raw[:, lat + 1 : lat + 2]
    raw = raw * lax.rsqrt(square / width + 1e-06)
    head = raw[:, :KEY_VALUE_RANK]
    head = head * lax.rsqrt(jnp.mean(head * head, axis=-1, keepdims=True) + 1e-06)
    head = head * gain_ref[...]
    tail = raw[:, KEY_VALUE_RANK:]
    half = (lat - KEY_VALUE_RANK) // 2
    lanes = tail.shape[1]
    tail = (
        tail * turn_ref[0]
        + pltpu.roll(tail, lanes - half, 1) * turn_ref[1]
        + pltpu.roll(tail, half, 1) * turn_ref[2]
    )
    keys = jnp.concatenate([head, tail], axis=1).astype(BF)[:, :lat]
    entry_ref[...] = keys
    count = keys.shape[0]
    in_half = halves[0][0].shape[0]
    copies = []
    for g in range(nodes // per):
        span = range(g * per, (g + 1) * per)

        def side(ref):
            return jnp.concatenate([ref[i] for i in span], axis=1)

        ctx_ref, stat_ref = halves[g * per // in_half]
        begin = g * per % in_half
        scores = dot(keys, side(q_ref)) * (softmax_scale * LOG2E)
        scores = jnp.where(side(allow_ref) > 0.5, scores, -jnp.inf)
        stats = jnp.concatenate([stat_ref[begin + i] for i in range(per)], axis=1)
        old = stats[0:1]
        top = jnp.maximum(old, jnp.max(scores, axis=0, keepdims=True))
        weight = jnp.exp2(scores - top)
        share = stats[1:2] * jnp.exp2(old - top)
        scale = 1.0 / (share + jnp.sum(weight, axis=0, keepdims=True))
        share = jnp.broadcast_to(share * scale, (8, per * heads))
        both = jnp.concatenate([weight * scale, share], axis=0).T
        for i in range(per):
            mine = both[i * heads : (i + 1) * heads]
            out = ctx_ref[begin + i].astype(F32) * mine[:, count : count + 1]
            out = out + dot(mine[:, :count].astype(BF), keys[:, :KEY_VALUE_RANK])
            out_ref[g * per + i] = out.astype(BF)
        here = pl.ds(g * per, per)
        copies.append(pltpu.make_async_copy(out_ref.at[here], out_hbm.at[here], sem.at[g]))
        copies[-1].start()
    for k in range(EXPERTS):
        start = pl.multiple_of((e_ref[0] ^ k) * quarter, 128)
        part_ref[:, pl.ds(start, quarter)] = got[k - 1][:, padded:] if k else own_part[...]
    for c in copies:
        c.wait()


def final_attention(place, width, rows, gain, turn, allow, q_t, first, second, per=4):
    tokens, lat, heads = q_t.shape
    vmem = pl.BlockSpec(memory_space=pltpu.VMEM)
    given = [*rows, gain, turn, allow, q_t, *first, *second]
    given = [pltpu.with_memory_space_constraint(x, pltpu.VMEM) for x in given]
    out = jax.ShapeDtypeStruct((tokens, heads, KEY_VALUE_RANK), BF)
    return pl.pallas_call(
        functools.partial(final_kernel, width, per),
        out_shape=[
            jax.ShapeDtypeStruct((tokens, width), BF),
            jax.ShapeDtypeStruct((tokens, lat), BF),
            out,
        ],
        in_specs=[pl.BlockSpec(memory_space=pltpu.SMEM)] + [vmem] * len(given),
        out_specs=[vmem, vmem, pl.BlockSpec(memory_space=pltpu.HBM)],
        scratch_shapes=[
            pltpu.VMEM(out.shape, BF),
            pltpu.SemaphoreType.DMA((tokens // per,)),
        ],
        compiler_params=params(12),
        cost_estimate=COST,
        name="final",
    )(place, *given)


def tree(parents, lengths, rank, lat):
    count = parents.shape[1]
    link = (parents[0][:, None] == jnp.arange(count, dtype=jnp.int32)[None, :]).astype(F32)
    reach = jnp.eye(count, dtype=F32) + link
    for _ in range(max(1, (count - 1).bit_length())):
        reach = jnp.minimum(jnp.dot(reach, reach, precision=lax.Precision.HIGHEST), 1.0)
    depth = jnp.sum(reach, axis=-1) - 1.0
    position = lengths.astype(F32) + depth
    half = (lat - rank) // 2
    index = jnp.arange(half, dtype=F32)
    inverse = 10000.0 ** (-2.0 * index / (2 * half))
    angle = position[:, None] * inverse[None, :]
    c, s = jnp.cos(angle), jnp.sin(angle)
    gap = jnp.zeros((count, 128 - 2 * half), F32)
    none = jnp.zeros_like(s)
    turn = jnp.stack(
        [
            jnp.concatenate([c, c, gap], axis=1),
            jnp.concatenate([-s, none, gap], axis=1),
            jnp.concatenate([none, s, gap], axis=1),
        ]
    )
    return reach, turn


def local(
    hidden,
    ffn_gain,
    attn_gain,
    latent_norm_gain,
    routes,
    gate_weights,
    expert_in,
    expert_down,
    kv_down,
    parents,
    lengths,
    queries,
    cache,
):
    size = lax.axis_size("ep")
    split = size // EXPERTS
    bits = [1 << b for b in range(split.bit_length() - 1)]
    width = hidden.shape[1]
    lat = kv_down.shape[1]
    heads = queries.shape[1]
    index = lax.axis_index("ep")
    place = jnp.stack([index // split, index % split]).astype(jnp.int32)

    def swap(x, bit):
        return lax.ppermute(x, "ep", [(i, i ^ bit) for i in range(size)])

    def spread(have, some):
        for bit in some:
            for r in sorted(have):
                have = have | {r ^ bit: swap(have[r], bit)}
        return have

    def to_line(xs):
        return [xs[0]] + [swap(xs[k], k * split) for k in range(1, EXPERTS)]

    q_t = jnp.transpose(queries, (0, 2, 1))
    cache_t = jnp.transpose(cache, (0, 2, 1))
    half = queries.shape[0] // 2
    reach, turn = tree(parents, lengths, KEY_VALUE_RANK, lat)
    allow = jnp.broadcast_to(reach[:, :, None], reach.shape + (heads,))

    packed = pack(place, hidden, ffn_gain[None], routes.T, gate_weights.T)
    near = to_line(packed[:EXPERTS])
    kv_far = swap(kv_down, bits[-1])
    first = cached_attention(lengths, after(q_t, packed[0]), cache_t, expert_in, 0, half)
    near, kv_far, first = lax.optimization_barrier((near, kv_far, first))
    *first, w_in = first
    line = jnp.concatenate(near, axis=0)
    info = jnp.concatenate([c[:, -TAIL:] for c in near], axis=0)
    groups = spread({0: line}, bits[:0:-1])
    own_quarters = to_line(after(packed[EXPERTS:], near[0]))
    second = cached_attention(lengths, after(q_t, line), cache_t, expert_down, half, half)
    groups, own_quarters, info, allow, turn, second = lax.optimization_barrier(
        (groups, own_quarters, info, allow, turn, second)
    )
    *second, w_out = second
    groups = spread(groups, bits[:1])
    kvs = spread({0: kv_down, bits[-1]: kv_far}, bits[-2::-1])
    groups, kvs = lax.optimization_barrier((groups, kvs))
    groups = [groups[r] for r in range(split)]
    kvs = [kvs[r] for r in range(split)]
    keep_a, send_a, keep_b, send_b = expert_slice(place, groups, w_in, w_out)

    def gathered(keep, got):
        terms = [keep, got]
        for bit in bits[1:]:
            out = sum(t[1::2].astype(F32) for t in terms).astype(BF)
            terms = [t[0::2] for t in terms] + [swap(out, bit)]
        return [sum(t[0, k].astype(F32) for t in terms).astype(BF) for k in range(EXPERTS // 2)]

    far = gathered(keep_a, swap(send_a, bits[0]))
    close = gathered(keep_b, swap(send_b, bits[0]))
    outs_e = to_line(close + far)
    own_sum, own_part, *rows = combine(place, outs_e, own_quarters, info, attn_gain[None], kvs)
    rows = [own_sum, own_part] + [swap(r, (k + 1) * split) for k, r in enumerate(rows)]
    return final_attention(
        place, width, rows, latent_norm_gain[None], turn, allow, q_t, first, second
    )


def solution(mesh):
    placed = (
        P(("group", "ep"), None),
        P(),
        P(),
        P(),
        P(("group", "ep"), None),
        P(("group", "ep"), None),
        P("ep", None, None),
        P("ep", None, None),
        P("ep", None),
        P(("group", "ep"), None),
        P(("group", "ep")),
        P(("group", "ep"), None, None),
        P(("group", "ep"), None, None),
    )
    return jax.shard_map(
        local,
        mesh=mesh,
        in_specs=placed,
        out_specs=(
            P(("group", "ep"), None),
            P(("group", "ep"), None),
            P(("group", "ep"), None, None),
        ),
        check_vma=False,
    )
```

```python
import functools

import jax
import jax.numpy as jnp
from jax import lax
from jax.experimental import pallas as pl
from jax.experimental.pallas import tpu as pltpu
from jax.sharding import PartitionSpec as P

KEY_VALUE_RANK = 512
NODES = 16
EXPERTS = 4
CAP = 9
TAIL = 128
ROWS = 40
BF = jnp.bfloat16
F32 = jnp.float32
softmax_scale = 192.0 ** (-0.5)
MIB = 1024 * 1024
COST = pl.CostEstimate(flops=1024, bytes_accessed=1024, transcendentals=0)
LOG2E = 1.4426950408889634


def iota(shape, dim):
    return lax.broadcasted_iota(jnp.int32, shape, dim)


def dot(a, b):
    return jnp.dot(a, b, preferred_element_type=F32)


def dot_t(a, b):
    return lax.dot_general(a, b, (((1,), (1,)), ((), ())), preferred_element_type=F32)


def params(mib, semantics=None):
    return pltpu.CompilerParams(vmem_limit_bytes=mib * MIB, dimension_semantics=semantics)


def after(x, *others):
    return lax.optimization_barrier((x, others))[0]


def whole(shape):
    zeros = (0,) * len(shape)
    return pl.BlockSpec(shape, lambda *_: zeros)


def pack_kernel(e_ref, *refs):
    ins, outs = refs[:4], refs[4 : 4 + 2 * EXPERTS]
    held, sem = refs[4 + 2 * EXPERTS : -1], refs[-1]
    copies = [pltpu.make_async_copy(a, b, sem.at[i]) for i, (a, b) in enumerate(zip(ins, held))]
    for c in copies:
        c.start()
    for c in copies:
        c.wait()
    hidden_ref, gain_ref, routes_ref, gates_ref = held
    chunks, parts = outs[:EXPERTS], outs[EXPERTS:]
    tokens, width = hidden_ref.shape
    piece = width // 8
    quarter = width // EXPERTS
    x = hidden_ref[...].astype(F32)
    scale = lax.rsqrt(jnp.mean(x * x, axis=-1, keepdims=True) + 1e-06)
    units = (x * scale * gain_ref[...]).astype(BF)
    first = jnp.broadcast_to(routes_ref[0:1, :], (8, tokens))
    second = jnp.broadcast_to(routes_ref[1:2, :], (8, tokens))
    row = iota((8, tokens), 0)
    before = (iota((tokens, tokens), 0) < iota((tokens, tokens), 1)).astype(BF)
    main, ninth = [], []
    for k in range(EXPERTS):
        expert = e_ref[0] ^ k
        hit = jnp.where((first == expert) | (second == expert), 1.0, 0.0)
        rank = dot(hit.astype(BF), before)
        main.append(jnp.where(rank == row.astype(F32), hit, 0.0))
        ninth.append(jnp.where(rank == 8.0, hit, 0.0))
    main = jnp.concatenate(main, axis=0).astype(BF)
    ninth = jnp.concatenate(ninth, axis=0)
    rows = iota(ninth.shape, 0) % 8
    picked = dot(main, units).astype(BF)
    cut = jnp.zeros((8 * EXPERTS, piece), F32)
    for j in range(8):
        cut = cut + dot(
            jnp.where(rows == j, ninth, 0.0).astype(BF), units[:, j * piece : (j + 1) * piece]
        )
    cut = cut.astype(BF)
    info = jnp.where(row == 0, first.astype(F32), second.astype(F32))
    for choice in range(2):
        gate = jnp.broadcast_to(gates_ref[choice : choice + 1, :], (8, tokens))
        for part in range(3):
            rounded = gate.astype(BF).astype(F32)
            info = jnp.where(row == 2 + 3 * choice + part, rounded, info)
            gate = gate - rounded
    spread = (iota((tokens, TAIL), 0) == iota((tokens, TAIL), 1)).astype(BF)
    tail = dot(info.astype(BF), spread).astype(BF)
    for k in range(EXPERTS):
        expert = e_ref[0] ^ k
        chunks[k][:, :width] = picked[8 * k : 8 * k + 8]
        chunks[k][:, width : width + piece] = cut[8 * k : 8 * k + 8]
        chunks[k][:, width + piece :] = tail
        start = pl.multiple_of(expert * quarter, 128)
        parts[k][...] = hidden_ref[:, pl.ds(start, quarter)]


def pack(e, hidden, gain, routes_t, gates_t):
    tokens, width = hidden.shape
    chunk = jax.ShapeDtypeStruct((8, width + width // 8 + TAIL), BF)
    part = jax.ShapeDtypeStruct((tokens, width // EXPERTS), BF)
    hbm = pl.BlockSpec(memory_space=pltpu.HBM)
    vmem = pl.BlockSpec(memory_space=pltpu.VMEM)
    given = [hidden, gain, routes_t, gates_t]
    placed = [pltpu.with_memory_space_constraint(a, pltpu.HBM) for a in given]
    return pl.pallas_call(
        pack_kernel,
        out_shape=[chunk] * EXPERTS + [part] * EXPERTS,
        in_specs=[pl.BlockSpec(memory_space=pltpu.SMEM)] + [hbm] * 4,
        out_specs=[vmem] * (2 * EXPERTS),
        scratch_shapes=[pltpu.VMEM(a.shape, a.dtype) for a in given]
        + [pltpu.SemaphoreType.DMA((4,))],
        compiler_params=params(8),
        cost_estimate=COST,
        name="pack",
    )(e, *placed)


def down(split, e_ref, act, w_out, keep, send, first):
    quarter = keep.shape[3]
    step = quarter // 2
    main_rows = 32 * split
    for k in range(keep.shape[1]):
        start = (e_ref[0] ^ (first + k)) * quarter
        for h in range(2):
            columns = pl.ds(pl.multiple_of(start + h * step, 128), step)
            out = dot(act[...], w_out[0, :, columns])
            for r in range(split):
                lower = out[32 * r : 32 * r + 32]
                upper = out[main_rows + 8 * r : main_rows + 8 * r + 8]
                mine = jnp.concatenate([lower, upper], axis=0).astype(BF)
                (send if r % 2 else keep)[r // 2, k, :, h * step : (h + 1) * step] = mine


def expert_kernel(split, e_ref, *refs):
    groups = refs[:split]
    w_in, w_out, act, *pieces, x = refs[split:]
    width = w_in.shape[1]
    hid = act.shape[1]
    piece = width // 8
    main_rows, last_rows = 32 * split, 8 * split
    for r in range(split):
        x[32 * r : 32 * r + 32, :] = groups[r][:, :width]
    ext = jnp.concatenate([g[:, width : width + piece] for g in groups], axis=0)
    row = iota((8 * last_rows, main_rows), 0)
    col = iota((8 * last_rows, main_rows), 1)
    place = row % last_rows
    want = 32 * (place // 8) + 8 * (place % 8) + row // last_rows
    pick = jnp.where((place % 8 < 4) & (col == want), 1.0, 0.0).astype(BF)
    last = dot(pick, ext).astype(BF)
    for j in range(8):
        x[main_rows:, j * piece : (j + 1) * piece] = last[j * last_rows : (j + 1) * last_rows]
    step = min(256, hid)
    for i in range(hid // step):
        gate = dot(x[...], w_in[0, :, i * step : (i + 1) * step])
        up = dot(x[...], w_in[0, :, hid + i * step : hid + (i + 1) * step])
        act[:, i * step : (i + 1) * step] = (gate / (1.0 + jnp.exp(-gate)) * up).astype(BF)
    down(split, e_ref, act, w_out, pieces[0], pieces[1], 3)
    down(split, e_ref, act, w_out, pieces[2], pieces[3], 2)


def expert_rest_kernel(split, e_ref, act, w_out, keep, send):
    down(split, e_ref, act, w_out, keep, send, 0)


def expert_slice(e, groups, w_in, w_out):
    split = len(groups)
    width, hid2 = w_in.shape[1:]
    hid = hid2 // 2
    quarter = width // EXPERTS
    half = jax.ShapeDtypeStruct((split // 2, EXPERTS // 2, ROWS, quarter), BF)
    single = jax.ShapeDtypeStruct((split // 2, 1, ROWS, quarter), BF)
    rows = ROWS * split
    act = jax.ShapeDtypeStruct((rows, hid), BF)
    vmem = pl.BlockSpec(memory_space=pltpu.VMEM)
    smem = pl.BlockSpec(memory_space=pltpu.SMEM)
    act, *single = pl.pallas_call(
        functools.partial(expert_kernel, split),
        out_shape=[act] + [single] * 4,
        in_specs=[smem] + [vmem] * (split + 2),
        out_specs=[vmem] * 5,
        scratch_shapes=[pltpu.VMEM((rows, width), BF)],
        compiler_params=params(10),
        cost_estimate=COST,
        name="experts",
    )(e, *groups, w_in, w_out)
    rest = pl.pallas_call(
        functools.partial(expert_rest_kernel, split),
        out_shape=[half, half],
        in_specs=[smem] + [vmem] * 2,
        out_specs=[vmem] * 2,
        compiler_params=params(6),
        cost_estimate=COST,
        name="experts_rest",
    )(e, act, w_out)
    return single[:2], single[2:], rest


def combine_kernel(split, tokens, e_ref, *refs):
    outs_e, hid = refs[:EXPERTS], refs[EXPERTS : 2 * EXPERTS]
    info_ref, gain_ref = refs[2 * EXPERTS : 2 * EXPERTS + 2]
    kvs = refs[2 * EXPERTS + 2 : 2 * EXPERTS + 2 + split]
    rest = refs[2 * EXPERTS + 2 + split :]
    own_sum, own_part = rest[:2]
    sent = rest[2 : 1 + EXPERTS]
    kv_ref, sem = rest[1 + EXPERTS :]
    part = kvs[0].shape[0]
    lat = kvs[0].shape[1]
    copies = []
    for r in range(split):
        place = pl.multiple_of((e_ref[1] ^ r) * part, 16)
        copies.append(
            pltpu.make_async_copy(kvs[r], kv_ref.at[pl.ds(place, part), :], sem.at[r])
        )
        copies[-1].start()
    one = (iota((tokens, TAIL), 0) == iota((tokens, TAIL), 1)).astype(BF)
    info = dot_t(one, info_ref[...])
    earlier = (iota((tokens, tokens), 1) < iota((tokens, tokens), 0)).astype(BF)
    lane = iota((tokens, ROWS), 1).astype(F32)
    hits = []
    for k in range(EXPERTS):
        expert = (e_ref[0] ^ k).astype(F32)
        hits.append(jnp.where(info == expert, 1.0, 0.0))
    moe = None
    for k in range(EXPERTS):
        blocks = [[], [], []]
        for s in range(EXPERTS):
            h0 = hits[k][:, 8 * s : 8 * s + 1]
            h1 = hits[k][:, 8 * s + 1 : 8 * s + 2]
            hit = jnp.broadcast_to(h0 + h1, (tokens, ROWS))
            rank = dot(earlier, hit.astype(BF))
            line = s ^ k
            want = jnp.where(rank < 8.0, rank + 8.0 * line, 32.0 + line)
            chosen = (lane == want) & (hit > 0.5)
            for p in range(3):
                g0 = info[:, 8 * s + 2 + p : 8 * s + 3 + p]
                g1 = info[:, 8 * s + 5 + p : 8 * s + 6 + p]
                gate = jnp.broadcast_to(h0 * g0 + h1 * g1, (tokens, ROWS))
                blocks[p].append(jnp.where(chosen, gate, 0.0))
        weights = jnp.concatenate(blocks[0] + blocks[1] + blocks[2], axis=0).astype(BF)
        term = dot(weights, outs_e[k][...])
        moe = term if moe is None else moe + term
    total = EXPERTS * tokens
    moe = moe[:total] + moe[total : 2 * total] + moe[2 * total :]
    mixed = jnp.concatenate([h[...].astype(F32) for h in hid], axis=0) + moe
    square = jnp.sum(mixed * mixed, axis=-1, keepdims=True)
    scaled = (mixed * gain_ref[...]).astype(BF)
    for c in copies:
        c.wait()
    rows = dot(scaled, kv_ref[...])
    padded = own_sum.shape[1]
    for s in range(EXPERTS):
        span = slice(s * tokens, (s + 1) * tokens)
        rest = jnp.broadcast_to(square[span], (tokens, padded - lat))
        first = iota(rest.shape, 1) == 0
        if s:
            high = rest.astype(BF).astype(F32)
            sent[s - 1][:, :lat] = rows[span].astype(BF)
            sent[s - 1][:, lat:padded] = jnp.where(first, high, rest - high).astype(BF)
            sent[s - 1][:, padded:] = mixed[span].astype(BF)
        else:
            own_sum[:, :lat] = rows[span]
            own_sum[:, lat:] = jnp.where(first, rest, 0.0)
            own_part[...] = mixed[span].astype(BF)


def combine(place, outs_e, hid, info, gain, kvs):
    split = len(kvs)
    tokens, quarter = hid[0].shape
    part, lat = kvs[0].shape
    padded = (lat // 128 + 1) * 128
    outs = [pltpu.VMEM((tokens, padded), F32), pltpu.VMEM((tokens, quarter), BF)]
    outs += [pltpu.VMEM((tokens, padded + quarter), BF)] * (EXPERTS - 1)
    return pl.pallas_call(
        functools.partial(combine_kernel, split, tokens),
        out_shape=outs,
        grid_spec=pltpu.PrefetchScalarGridSpec(
            num_scalar_prefetch=1,
            grid=(1,),
            in_specs=[whole(o.shape) for o in outs_e]
            + [whole(h.shape) for h in hid]
            + [
                whole(info.shape),
                pl.BlockSpec((1, quarter), lambda t, e: (0, e[0])),
            ]
            + [pl.BlockSpec(memory_space=pl.ANY)] * split,
            out_specs=[whole(o.shape) for o in outs],
            scratch_shapes=[
                pltpu.VMEM((split * part, lat), BF),
                pltpu.SemaphoreType.DMA((split,)),
            ],
        ),
        compiler_params=params(8),
        cost_estimate=COST,
        name="combine",
    )(place, *outs_e, *hid, info, gain, *kvs)


def cached_kernel(begin, per, length_ref, *refs):
    q_hbm, cache_hbm, w_hbm, out_ref, stat_ref, w_ref, q_ref, cache_ref, keys_ref, sem = refs
    nodes, lat, heads = q_ref.shape
    ctx = cache_ref.shape[2]
    spare = keys_ref.shape[1] - lat
    copies = [
        pltpu.make_async_copy(cache_hbm, cache_ref, sem.at[0]),
        pltpu.make_async_copy(q_hbm.at[pl.ds(begin, nodes)], q_ref, sem.at[1]),
        pltpu.make_async_copy(w_hbm, w_ref, sem.at[2]),
    ]
    for c in copies:
        c.start()
    unused = (iota((ctx, spare), 0) >= length_ref[0]) & (iota((ctx, spare), 1) == 0)
    keys_ref[:, lat:] = jnp.where(unused, -jnp.inf, 0.0).astype(BF)
    one = (iota((spare, per * heads), 0) == 0).astype(BF)
    factor = softmax_scale * LOG2E
    copies[0].wait()
    keys_ref[:, :lat] = cache_ref[0].T
    copies[1].wait()

    for g in range(nodes // per):
        q = jnp.concatenate([q_ref[g * per + i] for i in range(per)], axis=1)
        q = jnp.concatenate([q, one], axis=0)
        scores = dot(keys_ref[...], q)
        top = jnp.max(scores, axis=0, keepdims=True) * factor
        weight = jnp.exp2(scores * factor - top)
        total = jnp.sum(weight, axis=0, keepdims=True)
        out = dot(cache_ref[0, :KEY_VALUE_RANK, :], weight.astype(BF)) * (1.0 / total)
        for i in range(per):
            span = slice(i * heads, (i + 1) * heads)
            out_ref[g * per + i] = out[:, span].T.astype(out_ref.dtype)
            stat_ref[g * per + i] = jnp.concatenate([top[:, span], total[:, span]], axis=0)
    copies[2].wait()


def cached_attention(lengths, q_t, cache_t, weight, first, count, per=4):
    tokens, lat, heads = q_t.shape
    ctx = cache_t.shape[2]
    hbm = pl.BlockSpec(memory_space=pltpu.HBM)
    vmem = pl.BlockSpec(memory_space=pltpu.VMEM)
    given = [pltpu.with_memory_space_constraint(a, pltpu.HBM) for a in (q_t, cache_t, weight)]
    return pl.pallas_call(
        functools.partial(cached_kernel, first, per),
        out_shape=[
            pltpu.VMEM((count, heads, KEY_VALUE_RANK), BF),
            pltpu.VMEM((count, 2, heads), F32),
            pltpu.VMEM(weight.shape, weight.dtype),
        ],
        in_specs=[pl.BlockSpec(memory_space=pltpu.SMEM), hbm, hbm, hbm],
        out_specs=[vmem, vmem, vmem],
        scratch_shapes=[
            pltpu.VMEM((count, lat, heads), BF),
            pltpu.VMEM(cache_t.shape, BF),
            pltpu.VMEM((ctx, (lat // 128 + 1) * 128), BF),
            pltpu.SemaphoreType.DMA((3,)),
        ],
        compiler_params=params(14),
        cost_estimate=pl.CostEstimate(
            flops=4 * count * heads * ctx * (lat + KEY_VALUE_RANK),
            bytes_accessed=2 * weight.size,
            transcendentals=count * heads * ctx,
        ),
        name="cached",
    )(lengths, *given)


def final_kernel(width, per, e_ref, *refs):
    own_sum, own_part = refs[:2]
    got = refs[2 : 1 + EXPERTS]
    gain_ref, turn_ref, allow_ref, q_ref = refs[1 + EXPERTS : 5 + EXPERTS]
    halves = refs[5 + EXPERTS : 7 + EXPERTS], refs[7 + EXPERTS : 9 + EXPERTS]
    part_ref, entry_ref, out_hbm, out_ref, sem = refs[9 + EXPERTS :]
    nodes, lat, heads = q_ref.shape
    padded = own_sum.shape[1]
    quarter = own_part.shape[1]
    raw = own_sum[...]
    for g in got:
        raw = raw + g[:, :padded].astype(F32)
    square = raw[:, lat : lat + 1] + raw[:, lat + 1 : lat + 2]
    raw = raw * lax.rsqrt(square / width + 1e-06)
    head = raw[:, :KEY_VALUE_RANK]
    head = head * lax.rsqrt(jnp.mean(head * head, axis=-1, keepdims=True) + 1e-06)
    head = head * gain_ref[...]
    tail = raw[:, KEY_VALUE_RANK:]
    half = (lat - KEY_VALUE_RANK) // 2
    lanes = tail.shape[1]
    tail = (
        tail * turn_ref[0]
        + pltpu.roll(tail, lanes - half, 1) * turn_ref[1]
        + pltpu.roll(tail, half, 1) * turn_ref[2]
    )
    keys = jnp.concatenate([head, tail], axis=1).astype(BF)[:, :lat]
    entry_ref[...] = keys
    count = keys.shape[0]
    in_half = halves[0][0].shape[0]
    copies = []
    for g in range(nodes // per):
        span = range(g * per, (g + 1) * per)

        def side(ref):
            return jnp.concatenate([ref[i] for i in span], axis=1)

        ctx_ref, stat_ref = halves[g * per // in_half]
        begin = g * per % in_half
        scores = dot(keys, side(q_ref)) * (softmax_scale * LOG2E)
        scores = jnp.where(side(allow_ref) > 0.5, scores, -jnp.inf)
        stats = jnp.concatenate([stat_ref[begin + i] for i in range(per)], axis=1)
        old = stats[0:1]
        top = jnp.maximum(old, jnp.max(scores, axis=0, keepdims=True))
        weight = jnp.exp2(scores - top)
        share = stats[1:2] * jnp.exp2(old - top)
        scale = 1.0 / (share + jnp.sum(weight, axis=0, keepdims=True))
        share = jnp.broadcast_to(share * scale, (8, per * heads))
        both = jnp.concatenate([weight * scale, share], axis=0).T
        for i in range(per):
            mine = both[i * heads : (i + 1) * heads]
            out = ctx_ref[begin + i].astype(F32) * mine[:, count : count + 1]
            out = out + dot(mine[:, :count].astype(BF), keys[:, :KEY_VALUE_RANK])
            out_ref[g * per + i] = out.astype(BF)
        here = pl.ds(g * per, per)
        copies.append(pltpu.make_async_copy(out_ref.at[here], out_hbm.at[here], sem.at[g]))
        copies[-1].start()
    for k in range(EXPERTS):
        start = pl.multiple_of((e_ref[0] ^ k) * quarter, 128)
        part_ref[:, pl.ds(start, quarter)] = got[k - 1][:, padded:] if k else own_part[...]
    for c in copies:
        c.wait()


def final_attention(place, width, rows, gain, turn, allow, q_t, first, second, per=4):
    tokens, lat, heads = q_t.shape
    vmem = pl.BlockSpec(memory_space=pltpu.VMEM)
    given = [*rows, gain, turn, allow, q_t, *first, *second]
    given = [pltpu.with_memory_space_constraint(x, pltpu.VMEM) for x in given]
    out = jax.ShapeDtypeStruct((tokens, heads, KEY_VALUE_RANK), BF)
    return pl.pallas_call(
        functools.partial(final_kernel, width, per),
        out_shape=[
            jax.ShapeDtypeStruct((tokens, width), BF),
            jax.ShapeDtypeStruct((tokens, lat), BF),
            out,
        ],
        in_specs=[pl.BlockSpec(memory_space=pltpu.SMEM)] + [vmem] * len(given),
        out_specs=[vmem, vmem, pl.BlockSpec(memory_space=pltpu.HBM)],
        scratch_shapes=[
            pltpu.VMEM(out.shape, BF),
            pltpu.SemaphoreType.DMA((tokens // per,)),
        ],
        compiler_params=params(12),
        cost_estimate=COST,
        name="final",
    )(place, *given)


def tree(parents, lengths, rank, lat):
    count = parents.shape[1]
    link = (parents[0][:, None] == jnp.arange(count, dtype=jnp.int32)[None, :]).astype(F32)
    reach = jnp.eye(count, dtype=F32) + link
    for _ in range(max(1, (count - 1).bit_length())):
        reach = jnp.minimum(jnp.dot(reach, reach, precision=lax.Precision.HIGHEST), 1.0)
    depth = jnp.sum(reach, axis=-1) - 1.0
    position = lengths.astype(F32) + depth
    half = (lat - rank) // 2
    index = jnp.arange(half, dtype=F32)
    inverse = 10000.0 ** (-2.0 * index / (2 * half))
    angle = position[:, None] * inverse[None, :]
    c, s = jnp.cos(angle), jnp.sin(angle)
    gap = jnp.zeros((count, 128 - 2 * half), F32)
    none = jnp.zeros_like(s)
    turn = jnp.stack(
        [
            jnp.concatenate([c, c, gap], axis=1),
            jnp.concatenate([-s, none, gap], axis=1),
            jnp.concatenate([none, s, gap], axis=1),
        ]
    )
    return reach, turn


def local(
    hidden,
    ffn_gain,
    attn_gain,
    latent_norm_gain,
    routes,
    gate_weights,
    expert_in,
    expert_down,
    kv_down,
    parents,
    lengths,
    queries,
    cache,
):
    size = lax.axis_size("ep")
    split = size // EXPERTS
    bits = [1 << b for b in range(split.bit_length() - 1)]
    width = hidden.shape[1]
    lat = kv_down.shape[1]
    heads = queries.shape[1]
    index = lax.axis_index("ep")
    place = jnp.stack([index // split, index % split]).astype(jnp.int32)

    def swap(x, bit):
        return lax.ppermute(x, "ep", [(i, i ^ bit) for i in range(size)])

    def spread(have, some):
        for bit in some:
            for r in sorted(have):
                have = have | {r ^ bit: swap(have[r], bit)}
        return have

    def to_line(xs):
        return [xs[0]] + [swap(xs[k], k * split) for k in range(1, EXPERTS)]

    q_t = jnp.transpose(queries, (0, 2, 1))
    cache_t = jnp.transpose(cache, (0, 2, 1))
    half = queries.shape[0] // 2
    reach, turn = tree(parents, lengths, KEY_VALUE_RANK, lat)
    allow = jnp.broadcast_to(reach[:, :, None], reach.shape + (heads,))

    packed = pack(place, hidden, ffn_gain[None], routes.T, gate_weights.T)
    near = to_line(packed[:EXPERTS])
    kv_far = swap(kv_down, bits[-1])
    *first, w_out = cached_attention(lengths, after(q_t, packed[0]), cache_t, expert_down, 0, half)
    near, kv_far, first = lax.optimization_barrier((near, kv_far, first))
    line = jnp.concatenate(near, axis=0)
    info = jnp.concatenate([c[:, -TAIL:] for c in near], axis=0)
    groups = spread({0: line}, bits[:0:-1])
    own_quarters = to_line(after(packed[EXPERTS:], near[0]))
    *second, w_in = cached_attention(lengths, after(q_t, line), cache_t, expert_in, half, half)
    groups, own_quarters, info, allow, turn, second = lax.optimization_barrier(
        (groups, own_quarters, info, allow, turn, second)
    )
    groups = spread(groups, bits[:1])
    groups = [groups[r] for r in range(split)]
    pieces = expert_slice(place, groups, w_in, w_out)
    kvs = {0: after(kv_down, pieces[0]), bits[-1]: kv_far}
    kvs = spread(kvs, bits[-2::-1])
    kvs = [kvs[r] for r in range(split)]

    def gathered(keep, send):
        terms = [keep, swap(send, bits[0])]
        for bit in bits[1:]:
            out = sum(t[1::2].astype(F32) for t in terms).astype(BF)
            terms = [t[0::2] for t in terms] + [swap(out, bit)]
        return [sum(t[0, k].astype(F32) for t in terms).astype(BF) for k in range(keep.shape[1])]

    far, middle, close = [gathered(*p) for p in pieces]
    close = close + middle + far
    outs_e = to_line(close)
    own_sum, own_part, *rows = combine(place, outs_e, own_quarters, info, attn_gain[None], kvs)
    rows = [own_sum, own_part] + [swap(r, (k + 1) * split) for k, r in enumerate(rows)]
    return final_attention(
        place, width, rows, latent_norm_gain[None], turn, allow, q_t, first, second
    )


def solution(mesh):
    placed = (
        P(("group", "ep"), None),
        P(),
        P(),
        P(),
        P(("group", "ep"), None),
        P(("group", "ep"), None),
        P("ep", None, None),
        P("ep", None, None),
        P("ep", None),
        P(("group", "ep"), None),
        P(("group", "ep")),
        P(("group", "ep"), None, None),
        P(("group", "ep"), None, None),
    )
    return jax.shard_map(
        local,
        mesh=mesh,
        in_specs=placed,
        out_specs=(
            P(("group", "ep"), None),
            P(("group", "ep"), None),
            P(("group", "ep"), None, None),
        ),
        check_vma=False,
    )
```

```python
import functools

import jax
import jax.numpy as jnp
from jax import lax
from jax.experimental import pallas as pl
from jax.experimental.pallas import tpu as pltpu
from jax.sharding import PartitionSpec as P

KEY_VALUE_RANK = 512
NODES = 16
EXPERTS = 4
CAP = 9
TAIL = 128
ROWS = 40
BF = jnp.bfloat16
F32 = jnp.float32
softmax_scale = 192.0 ** (-0.5)
MIB = 1024 * 1024
LONG = pl.CostEstimate(flops=1 << 34, bytes_accessed=1 << 24, transcendentals=0)
COST = pl.CostEstimate(flops=1024, bytes_accessed=1024, transcendentals=0)
LOG2E = 1.4426950408889634


def iota(shape, dim):
    return lax.broadcasted_iota(jnp.int32, shape, dim)


def dot(a, b):
    return jnp.dot(a, b, preferred_element_type=F32)


def dot_t(a, b):
    return lax.dot_general(a, b, (((1,), (1,)), ((), ())), preferred_element_type=F32)


def params(mib, semantics=None):
    return pltpu.CompilerParams(vmem_limit_bytes=mib * MIB, dimension_semantics=semantics)


def after(x, *others):
    return lax.optimization_barrier((x, others))[0]


def whole(shape):
    zeros = (0,) * len(shape)
    return pl.BlockSpec(shape, lambda *_: zeros)


def pack_kernel(e_ref, *refs):
    ins, outs = refs[:4], refs[4 : 4 + 2 * EXPERTS]
    held, sem = refs[4 + 2 * EXPERTS : -1], refs[-1]
    copies = [pltpu.make_async_copy(a, b, sem.at[i]) for i, (a, b) in enumerate(zip(ins, held))]
    for c in copies:
        c.start()
    for c in copies:
        c.wait()
    hidden_ref, gain_ref, routes_ref, gates_ref = held
    chunks, parts = outs[:EXPERTS], outs[EXPERTS:]
    tokens, width = hidden_ref.shape
    piece = width // 8
    quarter = width // EXPERTS
    x = hidden_ref[...].astype(F32)
    scale = lax.rsqrt(jnp.mean(x * x, axis=-1, keepdims=True) + 1e-06)
    units = (x * scale * gain_ref[...]).astype(BF)
    first = jnp.broadcast_to(routes_ref[0:1, :], (8, tokens))
    second = jnp.broadcast_to(routes_ref[1:2, :], (8, tokens))
    row = iota((8, tokens), 0)
    before = (iota((tokens, tokens), 0) < iota((tokens, tokens), 1)).astype(BF)
    main, ninth = [], []
    for k in range(EXPERTS):
        expert = e_ref[0] ^ k
        hit = jnp.where((first == expert) | (second == expert), 1.0, 0.0)
        rank = dot(hit.astype(BF), before)
        main.append(jnp.where(rank == row.astype(F32), hit, 0.0))
        ninth.append(jnp.where(rank == 8.0, hit, 0.0))
    main = jnp.concatenate(main, axis=0).astype(BF)
    ninth = jnp.concatenate(ninth, axis=0)
    rows = iota(ninth.shape, 0) % 8
    picked = dot(main, units).astype(BF)
    cut = jnp.zeros((8 * EXPERTS, piece), F32)
    for j in range(8):
        cut = cut + dot(
            jnp.where(rows == j, ninth, 0.0).astype(BF), units[:, j * piece : (j + 1) * piece]
        )
    cut = cut.astype(BF)
    info = jnp.where(row == 0, first.astype(F32), second.astype(F32))
    for choice in range(2):
        gate = jnp.broadcast_to(gates_ref[choice : choice + 1, :], (8, tokens))
        for part in range(3):
            rounded = gate.astype(BF).astype(F32)
            info = jnp.where(row == 2 + 3 * choice + part, rounded, info)
            gate = gate - rounded
    spread = (iota((tokens, TAIL), 0) == iota((tokens, TAIL), 1)).astype(BF)
    tail = dot(info.astype(BF), spread).astype(BF)
    for k in range(EXPERTS):
        expert = e_ref[0] ^ k
        chunks[k][:, :width] = picked[8 * k : 8 * k + 8]
        chunks[k][:, width : width + piece] = cut[8 * k : 8 * k + 8]
        chunks[k][:, width + piece :] = tail
        start = pl.multiple_of(expert * quarter, 128)
        parts[k][...] = hidden_ref[:, pl.ds(start, quarter)]


def pack(e, hidden, gain, routes_t, gates_t):
    tokens, width = hidden.shape
    chunk = jax.ShapeDtypeStruct((8, width + width // 8 + TAIL), BF)
    part = jax.ShapeDtypeStruct((tokens, width // EXPERTS), BF)
    hbm = pl.BlockSpec(memory_space=pltpu.HBM)
    vmem = pl.BlockSpec(memory_space=pltpu.VMEM)
    given = [hidden, gain, routes_t, gates_t]
    placed = [pltpu.with_memory_space_constraint(a, pltpu.HBM) for a in given]
    return pl.pallas_call(
        pack_kernel,
        out_shape=[chunk] * EXPERTS + [part] * EXPERTS,
        in_specs=[pl.BlockSpec(memory_space=pltpu.SMEM)] + [hbm] * 4,
        out_specs=[vmem] * (2 * EXPERTS),
        scratch_shapes=[pltpu.VMEM(a.shape, a.dtype) for a in given]
        + [pltpu.SemaphoreType.DMA((4,))],
        compiler_params=params(8),
        cost_estimate=COST,
        name="pack",
    )(e, *placed)


def down(split, e_ref, act, w_out, keep, send, first):
    quarter = keep.shape[3]
    step = quarter // 2
    main_rows = 32 * split
    for k in range(keep.shape[1]):
        start = (e_ref[0] ^ (first + k)) * quarter
        for h in range(2):
            columns = pl.ds(pl.multiple_of(start + h * step, 128), step)
            out = dot(act[...], w_out[0, :, columns])
            for r in range(split):
                lower = out[32 * r : 32 * r + 32]
                upper = out[main_rows + 8 * r : main_rows + 8 * r + 8]
                mine = jnp.concatenate([lower, upper], axis=0).astype(BF)
                (send if r % 2 else keep)[r // 2, k, :, h * step : (h + 1) * step] = mine


def expert_kernel(split, e_ref, *refs):
    groups = refs[: 2 * split]
    w_in, w_out, act, *pieces, x = refs[2 * split :]
    width = w_in.shape[1]
    hid = act.shape[1]
    piece = width // 8
    main_rows, last_rows = 32 * split, 8 * split
    for r in range(2 * split):
        x[16 * r : 16 * r + 16, :] = groups[r][:, :width]
    ext = jnp.concatenate([g[:, width : width + piece] for g in groups], axis=0)
    row = iota((8 * last_rows, main_rows), 0)
    col = iota((8 * last_rows, main_rows), 1)
    place = row % last_rows
    want = 32 * (place // 8) + 8 * (place % 8) + row // last_rows
    pick = jnp.where((place % 8 < 4) & (col == want), 1.0, 0.0).astype(BF)
    last = dot(pick, ext).astype(BF)
    for j in range(8):
        x[main_rows:, j * piece : (j + 1) * piece] = last[j * last_rows : (j + 1) * last_rows]
    step = min(256, hid)
    for i in range(hid // step):
        gate = dot(x[...], w_in[0, :, i * step : (i + 1) * step])
        up = dot(x[...], w_in[0, :, hid + i * step : hid + (i + 1) * step])
        act[:, i * step : (i + 1) * step] = (gate / (1.0 + jnp.exp(-gate)) * up).astype(BF)
    down(split, e_ref, act, w_out, pieces[0], pieces[1], 3)
    down(split, e_ref, act, w_out, pieces[2], pieces[3], 2)


def expert_rest_kernel(split, e_ref, act, w_out, keep, send):
    down(split, e_ref, act, w_out, keep, send, 0)


def expert_slice(e, groups, w_in, w_out):
    split = len(groups) // 2
    width, hid2 = w_in.shape[1:]
    hid = hid2 // 2
    quarter = width // EXPERTS
    half = jax.ShapeDtypeStruct((split // 2, EXPERTS // 2, ROWS, quarter), BF)
    single = jax.ShapeDtypeStruct((split // 2, 1, ROWS, quarter), BF)
    rows = ROWS * split
    act = jax.ShapeDtypeStruct((rows, hid), BF)
    vmem = pl.BlockSpec(memory_space=pltpu.VMEM)
    smem = pl.BlockSpec(memory_space=pltpu.SMEM)
    act, *single = pl.pallas_call(
        functools.partial(expert_kernel, split),
        out_shape=[act] + [single] * 4,
        in_specs=[smem] + [vmem] * (2 * split + 2),
        out_specs=[vmem] * 5,
        scratch_shapes=[pltpu.VMEM((rows, width), BF)],
        compiler_params=params(10),
        cost_estimate=COST,
        name="experts",
    )(e, *groups, w_in, w_out)
    rest = pl.pallas_call(
        functools.partial(expert_rest_kernel, split),
        out_shape=[half, half],
        in_specs=[smem] + [vmem] * 2,
        out_specs=[vmem] * 2,
        compiler_params=params(6),
        cost_estimate=COST,
        name="experts_rest",
    )(e, act, w_out)
    return single[:2], single[2:], rest


def join_kernel(a_ref, b_ref, out_ref):
    rows = a_ref.shape[0]
    out_ref[:rows, :] = a_ref[...]
    out_ref[rows:, :] = b_ref[...]


def join(a, b):
    vmem = pl.BlockSpec(memory_space=pltpu.VMEM)
    return pl.pallas_call(
        join_kernel,
        out_shape=pltpu.VMEM((2 * a.shape[0], a.shape[1]), a.dtype),
        in_specs=[vmem, vmem],
        out_specs=vmem,
        compiler_params=params(2),
        cost_estimate=COST,
        name="join",
    )(a, b)


def gate_kernel(tokens, e_ref, *refs):
    out_ref = refs[-1]
    info = jnp.concatenate([r[:, r.shape[1] - TAIL :] for r in refs[:-1]], axis=0)
    one = (iota((tokens, TAIL), 0) == iota((tokens, TAIL), 1)).astype(BF)
    info = dot_t(one, info)
    earlier = (iota((tokens, tokens), 1) < iota((tokens, tokens), 0)).astype(BF)
    lane = iota((tokens, ROWS), 1).astype(F32)
    hits = []
    for k in range(EXPERTS):
        expert = (e_ref[0] ^ k).astype(F32)
        hits.append(jnp.where(info == expert, 1.0, 0.0))
    for k in range(EXPERTS):
        blocks = [[], [], []]
        for s in range(EXPERTS):
            h0 = hits[k][:, 8 * s : 8 * s + 1]
            h1 = hits[k][:, 8 * s + 1 : 8 * s + 2]
            hit = jnp.broadcast_to(h0 + h1, (tokens, ROWS))
            rank = dot(earlier, hit.astype(BF))
            line = s ^ k
            want = jnp.where(rank < 8.0, rank + 8.0 * line, 32.0 + line)
            chosen = (lane == want) & (hit > 0.5)
            for p in range(3):
                g0 = info[:, 8 * s + 2 + p : 8 * s + 3 + p]
                g1 = info[:, 8 * s + 5 + p : 8 * s + 6 + p]
                gate = jnp.broadcast_to(h0 * g0 + h1 * g1, (tokens, ROWS))
                blocks[p].append(jnp.where(chosen, gate, 0.0))
        out_ref[k] = jnp.concatenate(blocks[0] + blocks[1] + blocks[2], axis=0).astype(BF)

def gate_matrices(place, halves, tokens):
    vmem = pl.BlockSpec(memory_space=pltpu.VMEM)
    return pl.pallas_call(
        functools.partial(gate_kernel, tokens),
        out_shape=pltpu.VMEM((EXPERTS, 3 * EXPERTS * tokens, ROWS), BF),
        in_specs=[pl.BlockSpec(memory_space=pltpu.SMEM)] + [vmem] * len(halves),
        out_specs=vmem,
        compiler_params=params(4),
        cost_estimate=LONG,
        name="gates",
    )(place, *halves)


def combine_kernel(spots, tokens, e_ref, *refs):
    outs_e, hid = refs[:EXPERTS], refs[EXPERTS : 2 * EXPERTS]
    gates_ref, gain_ref = refs[2 * EXPERTS : 2 * EXPERTS + 2]
    kvs = refs[2 * EXPERTS + 2 : 2 * EXPERTS + 2 + len(spots)]
    rest = refs[2 * EXPERTS + 2 + len(spots) :]
    own_sum, own_part = rest[:2]
    sent = rest[2 : 1 + EXPERTS]
    kv_ref, sem = rest[1 + EXPERTS :]
    lat = kvs[0].shape[1]
    part = spots[0][1]
    copies = []
    for i, (r, rows, first) in enumerate(spots):
        place = pl.multiple_of((e_ref[1] ^ r) * part + first, 16)
        copies.append(pltpu.make_async_copy(kvs[i], kv_ref.at[pl.ds(place, rows), :], sem.at[i]))
        copies[-1].start()
    moe = None
    for k in range(EXPERTS):
        term = dot(gates_ref[k], outs_e[k][...])
        moe = term if moe is None else moe + term
    total = EXPERTS * tokens
    moe = moe[:total] + moe[total : 2 * total] + moe[2 * total :]
    mixed = jnp.concatenate([h[...].astype(F32) for h in hid], axis=0) + moe
    square = jnp.sum(mixed * mixed, axis=-1, keepdims=True)
    scaled = (mixed * gain_ref[...]).astype(BF)
    for c in copies:
        c.wait()
    rows = dot(scaled, kv_ref[...])
    padded = own_sum.shape[1]
    for s in range(EXPERTS):
        span = slice(s * tokens, (s + 1) * tokens)
        rest = jnp.broadcast_to(square[span], (tokens, padded - lat))
        first = iota(rest.shape, 1) == 0
        if s:
            high = rest.astype(BF).astype(F32)
            sent[s - 1][:, :lat] = rows[span].astype(BF)
            sent[s - 1][:, lat:padded] = jnp.where(first, high, rest - high).astype(BF)
            sent[s - 1][:, padded:] = mixed[span].astype(BF)
        else:
            own_sum[:, :lat] = rows[span]
            own_sum[:, lat:] = jnp.where(first, rest, 0.0)
            own_part[...] = mixed[span].astype(BF)


def combine(place, outs_e, hid, gates, gain, kvs):
    spots = [(r, x.shape[0], first) for r, first, x in kvs]
    kvs = [x for _, _, x in kvs]
    tokens, quarter = hid[0].shape
    lat = kvs[0].shape[1]
    padded = (lat // 128 + 1) * 128
    outs = [pltpu.VMEM((tokens, padded), F32), pltpu.VMEM((tokens, quarter), BF)]
    outs += [pltpu.VMEM((tokens, padded + quarter), BF)] * (EXPERTS - 1)
    return pl.pallas_call(
        functools.partial(combine_kernel, spots, tokens),
        out_shape=outs,
        grid_spec=pltpu.PrefetchScalarGridSpec(
            num_scalar_prefetch=1,
            grid=(1,),
            in_specs=[whole(o.shape) for o in outs_e]
            + [whole(h.shape) for h in hid]
            + [
                whole(gates.shape),
                pl.BlockSpec((1, quarter), lambda t, e: (0, e[0])),
            ]
            + [pl.BlockSpec(memory_space=pl.ANY)] * len(kvs),
            out_specs=[whole(o.shape) for o in outs],
            scratch_shapes=[
                pltpu.VMEM((quarter, lat), BF),
                pltpu.SemaphoreType.DMA((len(kvs),)),
            ],
        ),
        compiler_params=params(8),
        cost_estimate=COST,
        name="combine",
    )(place, *outs_e, *hid, gates, gain, *kvs)


def cached_kernel(begin, per, length_ref, *refs):
    q_ref, cache_ref, keys_ref, sem = refs[-4:]
    loads = (len(refs) - 8) // 2
    q_hbm, cache_hbm = refs[:2]
    w_hbm = refs[2 : 2 + loads]
    out_ref, stat_ref = refs[2 + loads : 4 + loads]
    w_ref = refs[4 + loads : -4]
    nodes, lat, heads = q_ref.shape
    ctx = cache_ref.shape[2]
    spare = keys_ref.shape[1] - lat
    copies = [
        pltpu.make_async_copy(cache_hbm, cache_ref, sem.at[0]),
        pltpu.make_async_copy(q_hbm.at[pl.ds(begin, nodes)], q_ref, sem.at[1]),
    ]
    for i in range(loads):
        copies.append(pltpu.make_async_copy(w_hbm[i], w_ref[i], sem.at[2 + i]))
    for c in copies:
        c.start()
    unused = (iota((ctx, spare), 0) >= length_ref[0]) & (iota((ctx, spare), 1) == 0)
    keys_ref[:, lat:] = jnp.where(unused, -jnp.inf, 0.0).astype(BF)
    one = (iota((spare, per * heads), 0) == 0).astype(BF)
    factor = softmax_scale * LOG2E
    copies[0].wait()
    keys_ref[:, :lat] = cache_ref[0].T
    copies[1].wait()

    for g in range(nodes // per):
        q = jnp.concatenate([q_ref[g * per + i] for i in range(per)], axis=1)
        q = jnp.concatenate([q, one], axis=0)
        scores = dot(keys_ref[...], q)
        top = jnp.max(scores, axis=0, keepdims=True) * factor
        weight = jnp.exp2(scores * factor - top)
        total = jnp.sum(weight, axis=0, keepdims=True)
        out = dot(cache_ref[0, :KEY_VALUE_RANK, :], weight.astype(BF)) * (1.0 / total)
        for i in range(per):
            span = slice(i * heads, (i + 1) * heads)
            out_ref[g * per + i] = out[:, span].T.astype(out_ref.dtype)
            stat_ref[g * per + i] = jnp.concatenate([top[:, span], total[:, span]], axis=0)
    for c in copies[2:]:
        c.wait()


def cached_attention(lengths, q_t, cache_t, weights, first, count, per=4):
    tokens, lat, heads = q_t.shape
    ctx = cache_t.shape[2]
    hbm = pl.BlockSpec(memory_space=pltpu.HBM)
    vmem = pl.BlockSpec(memory_space=pltpu.VMEM)
    given = [pltpu.with_memory_space_constraint(a, pltpu.HBM) for a in (q_t, cache_t, *weights)]
    return pl.pallas_call(
        functools.partial(cached_kernel, first, per),
        out_shape=[
            pltpu.VMEM((count, heads, KEY_VALUE_RANK), BF),
            pltpu.VMEM((count, 2, heads), F32),
        ]
        + [pltpu.VMEM(w.shape, w.dtype) for w in weights],
        in_specs=[pl.BlockSpec(memory_space=pltpu.SMEM)] + [hbm] * len(given),
        out_specs=[vmem] * len(given),
        scratch_shapes=[
            pltpu.VMEM((count, lat, heads), BF),
            pltpu.VMEM(cache_t.shape, BF),
            pltpu.VMEM((ctx, (lat // 128 + 1) * 128), BF),
            pltpu.SemaphoreType.DMA((2 + len(weights),)),
        ],
        compiler_params=params(10),
        cost_estimate=pl.CostEstimate(
            flops=4 * count * heads * ctx * (lat + KEY_VALUE_RANK),
            bytes_accessed=4 * count * heads * lat,
            transcendentals=count * heads * ctx,
        ),
        name="cached",
    )(lengths, *given)


def final_kernel(width, per, e_ref, *refs):
    own_sum, own_part = refs[:2]
    got = refs[2 : 1 + EXPERTS]
    gain_ref, turn_ref, allow_ref, q_ref = refs[1 + EXPERTS : 5 + EXPERTS]
    halves = refs[5 + EXPERTS : 7 + EXPERTS], refs[7 + EXPERTS : 9 + EXPERTS]
    part_ref, entry_ref, out_hbm, out_ref, sem = refs[9 + EXPERTS :]
    nodes, lat, heads = q_ref.shape
    padded = own_sum.shape[1]
    quarter = own_part.shape[1]
    raw = own_sum[...]
    for g in got:
        raw = raw + g[:, :padded].astype(F32)
    square = raw[:, lat : lat + 1] + raw[:, lat + 1 : lat + 2]
    raw = raw * lax.rsqrt(square / width + 1e-06)
    head = raw[:, :KEY_VALUE_RANK]
    head = head * lax.rsqrt(jnp.mean(head * head, axis=-1, keepdims=True) + 1e-06)
    head = head * gain_ref[...]
    tail = raw[:, KEY_VALUE_RANK:]
    half = (lat - KEY_VALUE_RANK) // 2
    lanes = tail.shape[1]
    tail = (
        tail * turn_ref[0]
        + pltpu.roll(tail, lanes - half, 1) * turn_ref[1]
        + pltpu.roll(tail, half, 1) * turn_ref[2]
    )
    keys = jnp.concatenate([head, tail], axis=1).astype(BF)[:, :lat]
    entry_ref[...] = keys
    count = keys.shape[0]
    in_half = halves[0][0].shape[0]
    copies = []
    for g in range(nodes // per):
        span = range(g * per, (g + 1) * per)

        def side(ref):
            return jnp.concatenate([ref[i] for i in span], axis=1)

        ctx_ref, stat_ref = halves[g * per // in_half]
        begin = g * per % in_half
        scores = dot(keys, side(q_ref)) * (softmax_scale * LOG2E)
        scores = jnp.where(side(allow_ref) > 0.5, scores, -jnp.inf)
        stats = jnp.concatenate([stat_ref[begin + i] for i in range(per)], axis=1)
        old = stats[0:1]
        top = jnp.maximum(old, jnp.max(scores, axis=0, keepdims=True))
        weight = jnp.exp2(scores - top)
        share = stats[1:2] * jnp.exp2(old - top)
        scale = 1.0 / (share + jnp.sum(weight, axis=0, keepdims=True))
        share = jnp.broadcast_to(share * scale, (8, per * heads))
        both = jnp.concatenate([weight * scale, share], axis=0).T
        for i in range(per):
            mine = both[i * heads : (i + 1) * heads]
            out = ctx_ref[begin + i].astype(F32) * mine[:, count : count + 1]
            out = out + dot(mine[:, :count].astype(BF), keys[:, :KEY_VALUE_RANK])
            out_ref[g * per + i] = out.astype(BF)
        here = pl.ds(g * per, per)
        copies.append(pltpu.make_async_copy(out_ref.at[here], out_hbm.at[here], sem.at[g]))
        copies[-1].start()
    for k in range(EXPERTS):
        start = pl.multiple_of((e_ref[0] ^ k) * quarter, 128)
        part_ref[:, pl.ds(start, quarter)] = got[k - 1][:, padded:] if k else own_part[...]
    for c in copies:
        c.wait()


def final_attention(place, width, rows, gain, turn, allow, q_t, first, second, per=4):
    tokens, lat, heads = q_t.shape
    vmem = pl.BlockSpec(memory_space=pltpu.VMEM)
    given = [*rows, gain, turn, allow, q_t, *first, *second]
    given = [pltpu.with_memory_space_constraint(x, pltpu.VMEM) for x in given]
    out = jax.ShapeDtypeStruct((tokens, heads, KEY_VALUE_RANK), BF)
    return pl.pallas_call(
        functools.partial(final_kernel, width, per),
        out_shape=[
            jax.ShapeDtypeStruct((tokens, width), BF),
            jax.ShapeDtypeStruct((tokens, lat), BF),
            out,
        ],
        in_specs=[pl.BlockSpec(memory_space=pltpu.SMEM)] + [vmem] * len(given),
        out_specs=[vmem, vmem, pl.BlockSpec(memory_space=pltpu.HBM)],
        scratch_shapes=[
            pltpu.VMEM(out.shape, BF),
            pltpu.SemaphoreType.DMA((tokens // per,)),
        ],
        compiler_params=params(12),
        cost_estimate=COST,
        name="final",
    )(place, *given)


def tree(parents, lengths, rank, lat):
    count = parents.shape[1]
    link = (parents[0][:, None] == jnp.arange(count, dtype=jnp.int32)[None, :]).astype(F32)
    reach = jnp.eye(count, dtype=F32) + link
    for _ in range(max(1, (count - 1).bit_length())):
        reach = jnp.minimum(jnp.dot(reach, reach, precision=lax.Precision.HIGHEST), 1.0)
    depth = jnp.sum(reach, axis=-1) - 1.0
    position = lengths.astype(F32) + depth
    half = (lat - rank) // 2
    index = jnp.arange(half, dtype=F32)
    inverse = 10000.0 ** (-2.0 * index / (2 * half))
    angle = position[:, None] * inverse[None, :]
    c, s = jnp.cos(angle), jnp.sin(angle)
    gap = jnp.zeros((count, 128 - 2 * half), F32)
    none = jnp.zeros_like(s)
    turn = jnp.stack(
        [
            jnp.concatenate([c, c, gap], axis=1),
            jnp.concatenate([-s, none, gap], axis=1),
            jnp.concatenate([none, s, gap], axis=1),
        ]
    )
    return reach, turn


def local(
    hidden,
    ffn_gain,
    attn_gain,
    latent_norm_gain,
    routes,
    gate_weights,
    expert_in,
    expert_down,
    kv_down,
    parents,
    lengths,
    queries,
    cache,
):
    size = lax.axis_size("ep")
    split = size // EXPERTS
    bits = [1 << b for b in range(split.bit_length() - 1)]
    width = hidden.shape[1]
    lat = kv_down.shape[1]
    heads = queries.shape[1]
    index = lax.axis_index("ep")
    place = jnp.stack([index // split, index % split]).astype(jnp.int32)

    def swap(x, bit):
        return lax.ppermute(x, "ep", [(i, i ^ bit) for i in range(size)])

    def spread(have, some):
        for bit in some:
            for r in sorted(have):
                have = have | {r ^ bit: swap(have[r], bit)}
        return have

    def to_line(xs):
        got = {k: swap(xs[k], k * split) for k in (3, 2, 1)}
        return [xs[0], got[1], got[2], got[3]]

    q_t = jnp.transpose(queries, (0, 2, 1))
    cache_t = jnp.transpose(cache, (0, 2, 1))
    half = queries.shape[0] // 2
    reach, turn = tree(parents, lengths, KEY_VALUE_RANK, lat)
    allow = jnp.broadcast_to(reach[:, :, None], reach.shape + (heads,))

    packed = pack(place, hidden, ffn_gain[None], routes.T, gate_weights.T)
    own = packed[:EXPERTS]
    top, low = bits[-1], bits[:-1]
    kvs = spread({0: kv_down}, [top])
    near = to_line(own)
    lower = join(near[0], near[1])
    lowers = spread({0: lower}, [top])
    q_first = after(q_t, lower, allow, turn)
    *first, w_in, w_out = cached_attention(
        lengths, q_first, cache_t, [expert_in, expert_down], 0, half
    )
    distant, first, kvs = lax.optimization_barrier((near[2:], first, kvs))
    upper = join(*distant)
    across = {top: swap(upper, top)}
    uppers = spread({0: upper}, low[::-1])
    own_quarters = to_line(after(packed[EXPERTS:], uppers))
    lowers = spread(lowers, low[::-1])
    gates = gate_matrices(place, (lower, upper), hidden.shape[0])
    lowers, uppers, across, own_quarters, gates = lax.optimization_barrier(
        (lowers, uppers, across, own_quarters, gates)
    )
    uppers = uppers | spread(across, low[::-1])
    groups = [x for r in range(split) for x in (lowers[r], uppers[r])]
    pieces = expert_slice(place, groups, w_in, w_out)

    kvs = spread(after(kvs, pieces[0]), low[::-1])
    kvs = [(r, 0, x) for r, x in kvs.items()]

    def inner(keep, send):
        terms = [keep, swap(send, bits[0])]
        for bit in bits[1:-1]:
            out = sum(t[1::2].astype(F32) for t in terms).astype(BF)
            terms = [t[0::2] for t in terms] + [swap(out, bit)]
        return [t[0] for t in terms], sum(t[1].astype(F32) for t in terms).astype(BF)

    def outer(terms, got):
        return [sum(t[k].astype(F32) for t in (*terms, got)).astype(BF) for k in range(len(got))]

    kept, out = zip(*[inner(*p) for p in pieces])
    got = [swap(x, top) for x in out]
    far = outer(kept[0], after(got[0], out[2]))
    middle = outer(kept[1], got[1])
    close = outer(kept[2], got[2])
    outs_e = to_line(close + middle + far)
    second = cached_attention(lengths, after(q_t, close[1]), cache_t, [], half, half)
    outs_e, second = lax.optimization_barrier((outs_e, second))

    own_sum, own_part, *rows = combine(place, outs_e, own_quarters, gates, attn_gain[None], kvs)
    rows = [own_sum, own_part] + [swap(r, (k + 1) * split) for k, r in enumerate(rows)]
    return final_attention(
        place, width, rows, latent_norm_gain[None], turn, allow, q_t, first, second
    )


def solution(mesh):
    placed = (
        P(("group", "ep"), None),
        P(),
        P(),
        P(),
        P(("group", "ep"), None),
        P(("group", "ep"), None),
        P("ep", None, None),
        P("ep", None, None),
        P("ep", None),
        P(("group", "ep"), None),
        P(("group", "ep")),
        P(("group", "ep"), None, None),
        P(("group", "ep"), None, None),
    )
    return jax.shard_map(
        local,
        mesh=mesh,
        in_specs=placed,
        out_specs=(
            P(("group", "ep"), None),
            P(("group", "ep"), None),
            P(("group", "ep"), None, None),
        ),
        check_vma=False,
    )
```

```python
import functools

import jax
import jax.numpy as jnp
from jax import lax
from jax.experimental import pallas as pl
from jax.experimental.pallas import tpu as pltpu
from jax.sharding import PartitionSpec as P

KEY_VALUE_RANK = 512
NODES = 16
EXPERTS = 4
CAP = 9
TAIL = 128
ROWS = 40
BF = jnp.bfloat16
F32 = jnp.float32
softmax_scale = 192.0 ** (-0.5)
MIB = 1024 * 1024
LONG = pl.CostEstimate(flops=1 << 34, bytes_accessed=1 << 24, transcendentals=0)
COST = pl.CostEstimate(flops=1024, bytes_accessed=1024, transcendentals=0)
LOG2E = 1.4426950408889634


def iota(shape, dim):
    return lax.broadcasted_iota(jnp.int32, shape, dim)


def dot(a, b):
    return jnp.dot(a, b, preferred_element_type=F32)


def dot_t(a, b):
    return lax.dot_general(a, b, (((1,), (1,)), ((), ())), preferred_element_type=F32)


def params(mib, semantics=None):
    return pltpu.CompilerParams(vmem_limit_bytes=mib * MIB, dimension_semantics=semantics)


def after(x, *others):
    return lax.optimization_barrier((x, others))[0]


def whole(shape):
    zeros = (0,) * len(shape)
    return pl.BlockSpec(shape, lambda *_: zeros)


def pack_kernel(e_ref, *refs):
    ins, outs = refs[:4], refs[4 : 4 + 2 * EXPERTS]
    held, sem = refs[4 + 2 * EXPERTS : -1], refs[-1]
    copies = [pltpu.make_async_copy(a, b, sem.at[i]) for i, (a, b) in enumerate(zip(ins, held))]
    for c in copies:
        c.start()
    for c in copies:
        c.wait()
    hidden_ref, gain_ref, routes_ref, gates_ref = held
    chunks, parts = outs[:EXPERTS], outs[EXPERTS:]
    tokens, width = hidden_ref.shape
    piece = width // 8
    quarter = width // EXPERTS
    x = hidden_ref[...].astype(F32)
    scale = lax.rsqrt(jnp.mean(x * x, axis=-1, keepdims=True) + 1e-06)
    units = (x * scale * gain_ref[...]).astype(BF)
    first = jnp.broadcast_to(routes_ref[0:1, :], (8, tokens))
    second = jnp.broadcast_to(routes_ref[1:2, :], (8, tokens))
    row = iota((8, tokens), 0)
    before = (iota((tokens, tokens), 0) < iota((tokens, tokens), 1)).astype(BF)
    main, ninth = [], []
    for k in range(EXPERTS):
        expert = e_ref[0] ^ k
        hit = jnp.where((first == expert) | (second == expert), 1.0, 0.0)
        rank = dot(hit.astype(BF), before)
        main.append(jnp.where(rank == row.astype(F32), hit, 0.0))
        ninth.append(jnp.where(rank == 8.0, hit, 0.0))
    main = jnp.concatenate(main, axis=0).astype(BF)
    ninth = jnp.concatenate(ninth, axis=0)
    rows = iota(ninth.shape, 0) % 8
    picked = dot(main, units).astype(BF)
    cut = jnp.zeros((8 * EXPERTS, piece), F32)
    for j in range(8):
        cut = cut + dot(
            jnp.where(rows == j, ninth, 0.0).astype(BF), units[:, j * piece : (j + 1) * piece]
        )
    cut = cut.astype(BF)
    info = jnp.where(row == 0, first.astype(F32), second.astype(F32))
    for choice in range(2):
        gate = jnp.broadcast_to(gates_ref[choice : choice + 1, :], (8, tokens))
        for part in range(3):
            rounded = gate.astype(BF).astype(F32)
            info = jnp.where(row == 2 + 3 * choice + part, rounded, info)
            gate = gate - rounded
    spread = (iota((tokens, TAIL), 0) == iota((tokens, TAIL), 1)).astype(BF)
    tail = dot(info.astype(BF), spread).astype(BF)
    for k in range(EXPERTS):
        expert = e_ref[0] ^ k
        chunks[k][:, :width] = picked[8 * k : 8 * k + 8]
        chunks[k][:, width : width + piece] = cut[8 * k : 8 * k + 8]
        chunks[k][:, width + piece :] = tail
        start = pl.multiple_of(expert * quarter, 128)
        parts[k][...] = hidden_ref[:, pl.ds(start, quarter)]


def pack(e, hidden, gain, routes_t, gates_t):
    tokens, width = hidden.shape
    chunk = jax.ShapeDtypeStruct((8, width + width // 8 + TAIL), BF)
    part = jax.ShapeDtypeStruct((tokens, width // EXPERTS), BF)
    hbm = pl.BlockSpec(memory_space=pltpu.HBM)
    vmem = pl.BlockSpec(memory_space=pltpu.VMEM)
    given = [hidden, gain, routes_t, gates_t]
    placed = [pltpu.with_memory_space_constraint(a, pltpu.HBM) for a in given]
    return pl.pallas_call(
        pack_kernel,
        out_shape=[chunk] * EXPERTS + [part] * EXPERTS,
        in_specs=[pl.BlockSpec(memory_space=pltpu.SMEM)] + [hbm] * 4,
        out_specs=[vmem] * (2 * EXPERTS),
        scratch_shapes=[pltpu.VMEM(a.shape, a.dtype) for a in given]
        + [pltpu.SemaphoreType.DMA((4,))],
        compiler_params=params(8),
        cost_estimate=COST,
        name="pack",
    )(e, *placed)


def down(split, e_ref, act, w_out, keep, send, first):
    quarter = keep.shape[3]
    step = quarter // 2
    main_rows = 32 * split
    for k in range(keep.shape[1]):
        start = (e_ref[0] ^ (first + k)) * quarter
        for h in range(2):
            columns = pl.ds(pl.multiple_of(start + h * step, 128), step)
            out = dot(act[...], w_out[0, :, columns])
            for r in range(split):
                lower = out[32 * r : 32 * r + 32]
                upper = out[main_rows + 8 * r : main_rows + 8 * r + 8]
                mine = jnp.concatenate([lower, upper], axis=0).astype(BF)
                (send if r % 2 else keep)[r // 2, k, :, h * step : (h + 1) * step] = mine


def expert_kernel(split, e_ref, *refs):
    groups = refs[: 2 * split]
    w_in, w_out, act, *pieces, x = refs[2 * split :]
    width = w_in.shape[1]
    hid = act.shape[1]
    piece = width // 8
    main_rows, last_rows = 32 * split, 8 * split
    for r in range(2 * split):
        x[16 * r : 16 * r + 16, :] = groups[r][:, :width]
    ext = jnp.concatenate([g[:, width : width + piece] for g in groups], axis=0)
    row = iota((8 * last_rows, main_rows), 0)
    col = iota((8 * last_rows, main_rows), 1)
    place = row % last_rows
    want = 32 * (place // 8) + 8 * (place % 8) + row // last_rows
    pick = jnp.where((place % 8 < 4) & (col == want), 1.0, 0.0).astype(BF)
    last = dot(pick, ext).astype(BF)
    for j in range(8):
        x[main_rows:, j * piece : (j + 1) * piece] = last[j * last_rows : (j + 1) * last_rows]
    step = min(256, hid)
    for i in range(hid // step):
        gate = dot(x[...], w_in[0, :, i * step : (i + 1) * step])
        up = dot(x[...], w_in[0, :, hid + i * step : hid + (i + 1) * step])
        act[:, i * step : (i + 1) * step] = (gate / (1.0 + jnp.exp(-gate)) * up).astype(BF)
    down(split, e_ref, act, w_out, pieces[0], pieces[1], 3)
    down(split, e_ref, act, w_out, pieces[2], pieces[3], 2)


def expert_rest_kernel(split, e_ref, act, w_out, keep, send):
    down(split, e_ref, act, w_out, keep, send, 0)


def expert_slice(e, groups, w_in, w_out):
    split = len(groups) // 2
    width, hid2 = w_in.shape[1:]
    hid = hid2 // 2
    quarter = width // EXPERTS
    half = jax.ShapeDtypeStruct((split // 2, EXPERTS // 2, ROWS, quarter), BF)
    single = jax.ShapeDtypeStruct((split // 2, 1, ROWS, quarter), BF)
    rows = ROWS * split
    act = jax.ShapeDtypeStruct((rows, hid), BF)
    vmem = pl.BlockSpec(memory_space=pltpu.VMEM)
    smem = pl.BlockSpec(memory_space=pltpu.SMEM)
    act, *single = pl.pallas_call(
        functools.partial(expert_kernel, split),
        out_shape=[act] + [single] * 4,
        in_specs=[smem] + [vmem] * (2 * split + 2),
        out_specs=[vmem] * 5,
        scratch_shapes=[pltpu.VMEM((rows, width), BF)],
        compiler_params=params(10),
        cost_estimate=COST,
        name="experts",
    )(e, *groups, w_in, w_out)
    rest = pl.pallas_call(
        functools.partial(expert_rest_kernel, split),
        out_shape=[half, half],
        in_specs=[smem] + [vmem] * 2,
        out_specs=[vmem] * 2,
        compiler_params=params(6),
        cost_estimate=COST,
        name="experts_rest",
    )(e, act, w_out)
    return single[:2], single[2:], rest


def join_kernel(a_ref, b_ref, out_ref):
    rows = a_ref.shape[0]
    out_ref[:rows, :] = a_ref[...]
    out_ref[rows:, :] = b_ref[...]


def join(a, b):
    vmem = pl.BlockSpec(memory_space=pltpu.VMEM)
    return pl.pallas_call(
        join_kernel,
        out_shape=pltpu.VMEM((2 * a.shape[0], a.shape[1]), a.dtype),
        in_specs=[vmem, vmem],
        out_specs=vmem,
        compiler_params=params(2),
        cost_estimate=COST,
        name="join",
    )(a, b)


def gate_kernel(tokens, e_ref, *refs):
    out_ref = refs[-1]
    info = jnp.concatenate([r[:, r.shape[1] - TAIL :] for r in refs[:-1]], axis=0)
    one = (iota((tokens, TAIL), 0) == iota((tokens, TAIL), 1)).astype(BF)
    info = dot_t(one, info)
    earlier = (iota((tokens, tokens), 1) < iota((tokens, tokens), 0)).astype(BF)
    lane = iota((tokens, ROWS), 1).astype(F32)
    hits = []
    for k in range(EXPERTS):
        expert = (e_ref[0] ^ k).astype(F32)
        hits.append(jnp.where(info == expert, 1.0, 0.0))
    for k in range(EXPERTS):
        blocks = [[], [], []]
        for s in range(EXPERTS):
            h0 = hits[k][:, 8 * s : 8 * s + 1]
            h1 = hits[k][:, 8 * s + 1 : 8 * s + 2]
            hit = jnp.broadcast_to(h0 + h1, (tokens, ROWS))
            rank = dot(earlier, hit.astype(BF))
            line = s ^ k
            want = jnp.where(rank < 8.0, rank + 8.0 * line, 32.0 + line)
            chosen = (lane == want) & (hit > 0.5)
            for p in range(3):
                g0 = info[:, 8 * s + 2 + p : 8 * s + 3 + p]
                g1 = info[:, 8 * s + 5 + p : 8 * s + 6 + p]
                gate = jnp.broadcast_to(h0 * g0 + h1 * g1, (tokens, ROWS))
                blocks[p].append(jnp.where(chosen, gate, 0.0))
        out_ref[k] = jnp.concatenate(blocks[0] + blocks[1] + blocks[2], axis=0).astype(BF)

def gate_matrices(place, halves, tokens):
    vmem = pl.BlockSpec(memory_space=pltpu.VMEM)
    return pl.pallas_call(
        functools.partial(gate_kernel, tokens),
        out_shape=pltpu.VMEM((EXPERTS, 3 * EXPERTS * tokens, ROWS), BF),
        in_specs=[pl.BlockSpec(memory_space=pltpu.SMEM)] + [vmem] * len(halves),
        out_specs=vmem,
        compiler_params=params(4),
        cost_estimate=LONG,
        name="gates",
    )(place, *halves)


def combine_kernel(spots, tokens, e_ref, *refs):
    outs_e, hid = refs[:EXPERTS], refs[EXPERTS : 2 * EXPERTS]
    gates_ref, gain_ref = refs[2 * EXPERTS : 2 * EXPERTS + 2]
    kvs = refs[2 * EXPERTS + 2 : 2 * EXPERTS + 2 + len(spots)]
    rest = refs[2 * EXPERTS + 2 + len(spots) :]
    own_sum, own_part = rest[:2]
    sent = rest[2 : 1 + EXPERTS]
    kv_ref, sem = rest[1 + EXPERTS :]
    lat = kvs[0].shape[1]
    part = spots[0][1]
    copies = []
    for i, (r, rows, first) in enumerate(spots):
        place = pl.multiple_of((e_ref[1] ^ r) * part + first, 16)
        copies.append(pltpu.make_async_copy(kvs[i], kv_ref.at[pl.ds(place, rows), :], sem.at[i]))
        copies[-1].start()
    moe = None
    for k in range(EXPERTS):
        term = dot(gates_ref[k], outs_e[k][...])
        moe = term if moe is None else moe + term
    total = EXPERTS * tokens
    moe = moe[:total] + moe[total : 2 * total] + moe[2 * total :]
    mixed = jnp.concatenate([h[...].astype(F32) for h in hid], axis=0) + moe
    square = jnp.sum(mixed * mixed, axis=-1, keepdims=True)
    scaled = (mixed * gain_ref[...]).astype(BF)
    for c in copies:
        c.wait()
    rows = dot(scaled, kv_ref[...])
    padded = own_sum.shape[1]
    for s in range(EXPERTS):
        span = slice(s * tokens, (s + 1) * tokens)
        rest = jnp.broadcast_to(square[span], (tokens, padded - lat))
        first = iota(rest.shape, 1) == 0
        if s:
            high = rest.astype(BF).astype(F32)
            sent[s - 1][:, :lat] = rows[span].astype(BF)
            sent[s - 1][:, lat:padded] = jnp.where(first, high, rest - high).astype(BF)
            sent[s - 1][:, padded:] = mixed[span].astype(BF)
        else:
            own_sum[:, :lat] = rows[span]
            own_sum[:, lat:] = jnp.where(first, rest, 0.0)
            own_part[...] = mixed[span].astype(BF)


def combine(place, outs_e, hid, gates, gain, kvs):
    spots = [(r, x.shape[0], first) for r, first, x in kvs]
    kvs = [x for _, _, x in kvs]
    tokens, quarter = hid[0].shape
    lat = kvs[0].shape[1]
    padded = (lat // 128 + 1) * 128
    outs = [pltpu.VMEM((tokens, padded), F32), pltpu.VMEM((tokens, quarter), BF)]
    outs += [pltpu.VMEM((tokens, padded + quarter), BF)] * (EXPERTS - 1)
    return pl.pallas_call(
        functools.partial(combine_kernel, spots, tokens),
        out_shape=outs,
        grid_spec=pltpu.PrefetchScalarGridSpec(
            num_scalar_prefetch=1,
            grid=(1,),
            in_specs=[whole(o.shape) for o in outs_e]
            + [whole(h.shape) for h in hid]
            + [
                whole(gates.shape),
                pl.BlockSpec((1, quarter), lambda t, e: (0, e[0])),
            ]
            + [pl.BlockSpec(memory_space=pl.ANY)] * len(kvs),
            out_specs=[whole(o.shape) for o in outs],
            scratch_shapes=[
                pltpu.VMEM((quarter, lat), BF),
                pltpu.SemaphoreType.DMA((len(kvs),)),
            ],
        ),
        compiler_params=params(8),
        cost_estimate=COST,
        name="combine",
    )(place, *outs_e, *hid, gates, gain, *kvs)


def cached_kernel(begin, per, length_ref, *refs):
    q_ref, cache_ref, keys_ref, sem = refs[-4:]
    loads = (len(refs) - 8) // 2
    q_hbm, cache_hbm = refs[:2]
    w_hbm = refs[2 : 2 + loads]
    out_ref, stat_ref = refs[2 + loads : 4 + loads]
    w_ref = refs[4 + loads : -4]
    nodes, lat, heads = q_ref.shape
    ctx = cache_ref.shape[2]
    spare = keys_ref.shape[1] - lat
    copies = [
        pltpu.make_async_copy(cache_hbm, cache_ref, sem.at[0]),
        pltpu.make_async_copy(q_hbm.at[pl.ds(begin, nodes)], q_ref, sem.at[1]),
    ]
    for i in range(loads):
        copies.append(pltpu.make_async_copy(w_hbm[i], w_ref[i], sem.at[2 + i]))
    for c in copies:
        c.start()
    unused = (iota((ctx, spare), 0) >= length_ref[0]) & (iota((ctx, spare), 1) == 0)
    keys_ref[:, lat:] = jnp.where(unused, -jnp.inf, 0.0).astype(BF)
    one = (iota((spare, per * heads), 0) == 0).astype(BF)
    factor = softmax_scale * LOG2E
    copies[0].wait()
    keys_ref[:, :lat] = cache_ref[0].T
    copies[1].wait()

    for g in range(nodes // per):
        q = jnp.concatenate([q_ref[g * per + i] for i in range(per)], axis=1)
        q = jnp.concatenate([q, one], axis=0)
        scores = dot(keys_ref[...], q)
        top = jnp.max(scores, axis=0, keepdims=True) * factor
        weight = jnp.exp2(scores * factor - top)
        total = jnp.sum(weight, axis=0, keepdims=True)
        out = dot(cache_ref[0, :KEY_VALUE_RANK, :], weight.astype(BF)) * (1.0 / total)
        for i in range(per):
            span = slice(i * heads, (i + 1) * heads)
            out_ref[g * per + i] = out[:, span].T.astype(out_ref.dtype)
            stat_ref[g * per + i] = jnp.concatenate([top[:, span], total[:, span]], axis=0)
    for c in copies[2:]:
        c.wait()


def cached_attention(lengths, q_t, cache_t, weights, first, count, per=4, cost=None):
    tokens, lat, heads = q_t.shape
    ctx = cache_t.shape[2]
    hbm = pl.BlockSpec(memory_space=pltpu.HBM)
    vmem = pl.BlockSpec(memory_space=pltpu.VMEM)
    given = [pltpu.with_memory_space_constraint(a, pltpu.HBM) for a in (q_t, cache_t, *weights)]
    return pl.pallas_call(
        functools.partial(cached_kernel, first, per),
        out_shape=[
            pltpu.VMEM((count, heads, KEY_VALUE_RANK), BF),
            pltpu.VMEM((count, 2, heads), F32),
        ]
        + [pltpu.VMEM(w.shape, w.dtype) for w in weights],
        in_specs=[pl.BlockSpec(memory_space=pltpu.SMEM)] + [hbm] * len(given),
        out_specs=[vmem] * len(given),
        scratch_shapes=[
            pltpu.VMEM((count, lat, heads), BF),
            pltpu.VMEM(cache_t.shape, BF),
            pltpu.VMEM((ctx, (lat // 128 + 1) * 128), BF),
            pltpu.SemaphoreType.DMA((2 + len(weights),)),
        ],
        compiler_params=params(10),
        cost_estimate=cost
        or pl.CostEstimate(
            flops=4 * count * heads * ctx * (lat + KEY_VALUE_RANK),
            bytes_accessed=4 * count * heads * lat,
            transcendentals=count * heads * ctx,
        ),
        name="cached",
    )(lengths, *given)


def final_kernel(width, per, e_ref, *refs):
    own_sum, own_part = refs[:2]
    got = refs[2 : 1 + EXPERTS]
    gain_ref, turn_ref, allow_ref, q_ref = refs[1 + EXPERTS : 5 + EXPERTS]
    cached = refs[5 + EXPERTS : -5]
    part_ref, entry_ref, out_hbm, out_ref, sem = refs[-5:]
    found = []
    for ctx_ref, stat_ref in zip(cached[0::2], cached[1::2]):
        found += [(ctx_ref, stat_ref, i) for i in range(ctx_ref.shape[0])]
    nodes, lat, heads = q_ref.shape
    padded = own_sum.shape[1]
    quarter = own_part.shape[1]
    raw = own_sum[...]
    for g in got:
        raw = raw + g[:, :padded].astype(F32)
    square = raw[:, lat : lat + 1] + raw[:, lat + 1 : lat + 2]
    raw = raw * lax.rsqrt(square / width + 1e-06)
    head = raw[:, :KEY_VALUE_RANK]
    head = head * lax.rsqrt(jnp.mean(head * head, axis=-1, keepdims=True) + 1e-06)
    head = head * gain_ref[...]
    tail = raw[:, KEY_VALUE_RANK:]
    half = (lat - KEY_VALUE_RANK) // 2
    lanes = tail.shape[1]
    tail = (
        tail * turn_ref[0]
        + pltpu.roll(tail, lanes - half, 1) * turn_ref[1]
        + pltpu.roll(tail, half, 1) * turn_ref[2]
    )
    keys = jnp.concatenate([head, tail], axis=1).astype(BF)[:, :lat]
    entry_ref[...] = keys
    count = keys.shape[0]
    copies = []
    for g in range(nodes // per):
        span = range(g * per, (g + 1) * per)

        def side(ref):
            return jnp.concatenate([ref[i] for i in span], axis=1)

        scores = dot(keys, side(q_ref)) * (softmax_scale * LOG2E)
        scores = jnp.where(side(allow_ref) > 0.5, scores, -jnp.inf)
        stats = jnp.concatenate([found[i][1][found[i][2]] for i in span], axis=1)
        old = stats[0:1]
        top = jnp.maximum(old, jnp.max(scores, axis=0, keepdims=True))
        weight = jnp.exp2(scores - top)
        share = stats[1:2] * jnp.exp2(old - top)
        scale = 1.0 / (share + jnp.sum(weight, axis=0, keepdims=True))
        share = jnp.broadcast_to(share * scale, (8, per * heads))
        both = jnp.concatenate([weight * scale, share], axis=0).T
        for i in range(per):
            mine = both[i * heads : (i + 1) * heads]
            ctx_ref, _, place = found[g * per + i]
            out = ctx_ref[place].astype(F32) * mine[:, count : count + 1]
            out = out + dot(mine[:, :count].astype(BF), keys[:, :KEY_VALUE_RANK])
            out_ref[g * per + i] = out.astype(BF)
        here = pl.ds(g * per, per)
        copies.append(pltpu.make_async_copy(out_ref.at[here], out_hbm.at[here], sem.at[g]))
        copies[-1].start()
    for k in range(EXPERTS):
        start = pl.multiple_of((e_ref[0] ^ k) * quarter, 128)
        part_ref[:, pl.ds(start, quarter)] = got[k - 1][:, padded:] if k else own_part[...]
    for c in copies:
        c.wait()


def final_attention(place, width, rows, gain, turn, allow, q_t, cached, per=8):
    tokens, lat, heads = q_t.shape
    vmem = pl.BlockSpec(memory_space=pltpu.VMEM)
    given = [*rows, gain, turn, allow, q_t, *cached]
    given = [pltpu.with_memory_space_constraint(x, pltpu.VMEM) for x in given]
    out = jax.ShapeDtypeStruct((tokens, heads, KEY_VALUE_RANK), BF)
    return pl.pallas_call(
        functools.partial(final_kernel, width, per),
        out_shape=[
            jax.ShapeDtypeStruct((tokens, width), BF),
            jax.ShapeDtypeStruct((tokens, lat), BF),
            out,
        ],
        in_specs=[pl.BlockSpec(memory_space=pltpu.SMEM)] + [vmem] * len(given),
        out_specs=[vmem, vmem, pl.BlockSpec(memory_space=pltpu.HBM)],
        scratch_shapes=[
            pltpu.VMEM(out.shape, BF),
            pltpu.SemaphoreType.DMA((tokens // per,)),
        ],
        compiler_params=params(12),
        cost_estimate=COST,
        name="final",
    )(place, *given)


def tree(parents, lengths, rank, lat):
    count = parents.shape[1]
    link = (parents[0][:, None] == jnp.arange(count, dtype=jnp.int32)[None, :]).astype(F32)
    reach = jnp.eye(count, dtype=F32) + link
    for _ in range(max(1, (count - 1).bit_length())):
        reach = jnp.minimum(jnp.dot(reach, reach, precision=lax.Precision.HIGHEST), 1.0)
    depth = jnp.sum(reach, axis=-1) - 1.0
    position = lengths.astype(F32) + depth
    half = (lat - rank) // 2
    index = jnp.arange(half, dtype=F32)
    inverse = 10000.0 ** (-2.0 * index / (2 * half))
    angle = position[:, None] * inverse[None, :]
    c, s = jnp.cos(angle), jnp.sin(angle)
    gap = jnp.zeros((count, 128 - 2 * half), F32)
    none = jnp.zeros_like(s)
    turn = jnp.stack(
        [
            jnp.concatenate([c, c, gap], axis=1),
            jnp.concatenate([-s, none, gap], axis=1),
            jnp.concatenate([none, s, gap], axis=1),
        ]
    )
    return reach, turn


def local(
    hidden,
    ffn_gain,
    attn_gain,
    latent_norm_gain,
    routes,
    gate_weights,
    expert_in,
    expert_down,
    kv_down,
    parents,
    lengths,
    queries,
    cache,
):
    size = lax.axis_size("ep")
    split = size // EXPERTS
    bits = [1 << b for b in range(split.bit_length() - 1)]
    width = hidden.shape[1]
    lat = kv_down.shape[1]
    heads = queries.shape[1]
    index = lax.axis_index("ep")
    place = jnp.stack([index // split, index % split]).astype(jnp.int32)

    def swap(x, bit):
        return lax.ppermute(x, "ep", [(i, i ^ bit) for i in range(size)])

    def spread(have, some):
        for bit in some:
            for r in sorted(have):
                have = have | {r ^ bit: swap(have[r], bit)}
        return have

    def to_line(xs):
        got = {k: swap(xs[k], k * split) for k in (3, 2, 1)}
        return [xs[0], got[1], got[2], got[3]]

    q_t = jnp.transpose(queries, (0, 2, 1))
    cache_t = jnp.transpose(cache, (0, 2, 1))
    half = queries.shape[0] // 2
    reach, turn = tree(parents, lengths, KEY_VALUE_RANK, lat)
    allow = jnp.broadcast_to(reach[:, :, None], reach.shape + (heads,))

    packed = pack(place, hidden, ffn_gain[None], routes.T, gate_weights.T)
    own = packed[:EXPERTS]
    top, low = bits[-1], bits[:-1]
    kvs = spread({0: kv_down}, [top])
    near = to_line(own)
    lower = join(near[0], near[1])
    lowers = spread({0: lower}, [top])
    q_first = after(q_t, lower, allow, turn)
    *first, w_in, w_out = cached_attention(
        lengths, q_first, cache_t, [expert_in, expert_down], 0, half
    )
    distant, first, kvs = lax.optimization_barrier((near[2:], first, kvs))
    upper = join(*distant)
    across = {top: swap(upper, top)}
    uppers = spread({0: upper}, low[::-1])
    own_quarters = to_line(after(packed[EXPERTS:], uppers))
    lowers = spread(lowers, low[::-1])
    gates = gate_matrices(place, (lower, upper), hidden.shape[0])
    lowers, uppers, across, own_quarters, gates = lax.optimization_barrier(
        (lowers, uppers, across, own_quarters, gates)
    )
    uppers = uppers | spread(across, low[::-1])
    groups = [x for r in range(split) for x in (lowers[r], uppers[r])]
    pieces = expert_slice(place, groups, w_in, w_out)

    kvs = spread(after(kvs, pieces[0]), low[::-1])
    kvs = [(r, 0, x) for r, x in kvs.items()]

    def inner(keep, send):
        terms = [keep, swap(send, bits[0])]
        for bit in bits[1:-1]:
            out = sum(t[1::2].astype(F32) for t in terms).astype(BF)
            terms = [t[0::2] for t in terms] + [swap(out, bit)]
        return [t[0] for t in terms], sum(t[1].astype(F32) for t in terms).astype(BF)

    def outer(terms, got):
        return [sum(t[k].astype(F32) for t in (*terms, got)).astype(BF) for k in range(len(got))]

    kept, out = zip(*[inner(*p) for p in pieces])
    got = [swap(x, top) for x in out]
    far = outer(kept[0], after(got[0], out[2]))
    middle = outer(kept[1], got[1])
    second = cached_attention(
        lengths, after(q_t, middle, out[2]), cache_t, [], half, half // 2, cost=LONG
    )
    close = outer(kept[2], after(got[2], second))
    outs_e = to_line(close + middle + far)
    third = cached_attention(
        lengths, after(q_t, close[1]), cache_t, [], half + half // 2, half // 2
    )
    outs_e, third = lax.optimization_barrier((outs_e, third))

    own_sum, own_part, *rows = combine(place, outs_e, own_quarters, gates, attn_gain[None], kvs)
    rows = [own_sum, own_part] + [swap(r, (k + 1) * split) for k, r in enumerate(rows)]
    return final_attention(
        place, width, rows, latent_norm_gain[None], turn, allow, q_t, [*first, *second, *third]
    )


def solution(mesh):
    placed = (
        P(("group", "ep"), None),
        P(),
        P(),
        P(),
        P(("group", "ep"), None),
        P(("group", "ep"), None),
        P("ep", None, None),
        P("ep", None, None),
        P("ep", None),
        P(("group", "ep"), None),
        P(("group", "ep")),
        P(("group", "ep"), None, None),
        P(("group", "ep"), None, None),
    )
    return jax.shard_map(
        local,
        mesh=mesh,
        in_specs=placed,
        out_specs=(
            P(("group", "ep"), None),
            P(("group", "ep"), None),
            P(("group", "ep"), None, None),
        ),
        check_vma=False,
    )
```

```python
import functools

import jax
import jax.numpy as jnp
from jax import lax
from jax.experimental import pallas as pl
from jax.experimental.pallas import tpu as pltpu
from jax.sharding import PartitionSpec as P

KEY_VALUE_RANK = 512
NODES = 16
EXPERTS = 4
CAP = 9
TAIL = 128
ROWS = 40
SPACED = 48
BF = jnp.bfloat16
F32 = jnp.float32
softmax_scale = 192.0 ** (-0.5)
MIB = 1024 * 1024
LONG = pl.CostEstimate(flops=1 << 34, bytes_accessed=1 << 24, transcendentals=0)
COST = pl.CostEstimate(flops=1024, bytes_accessed=1024, transcendentals=0)
LOG2E = 1.4426950408889634


def iota(shape, dim):
    return lax.broadcasted_iota(jnp.int32, shape, dim)


def dot(a, b):
    return jnp.dot(a, b, preferred_element_type=F32)


def dot_t(a, b):
    return lax.dot_general(a, b, (((1,), (1,)), ((), ())), preferred_element_type=F32)


def params(mib, semantics=None):
    return pltpu.CompilerParams(vmem_limit_bytes=mib * MIB, dimension_semantics=semantics)


def after(x, *others):
    return lax.optimization_barrier((x, others))[0]


def whole(shape):
    zeros = (0,) * len(shape)
    return pl.BlockSpec(shape, lambda *_: zeros)


def pack_kernel(e_ref, *refs):
    ins, outs = refs[:4], refs[4 : 4 + 2 * EXPERTS]
    held, sem = refs[4 + 2 * EXPERTS : -1], refs[-1]
    copies = [pltpu.make_async_copy(a, b, sem.at[i]) for i, (a, b) in enumerate(zip(ins, held))]
    for c in copies:
        c.start()
    for c in copies:
        c.wait()
    hidden_ref, gain_ref, routes_ref, gates_ref = held
    chunks, parts = outs[:EXPERTS], outs[EXPERTS:]
    tokens, width = hidden_ref.shape
    piece = width // 8
    quarter = width // EXPERTS
    x = hidden_ref[...].astype(F32)
    scale = lax.rsqrt(jnp.mean(x * x, axis=-1, keepdims=True) + 1e-06)
    units = (x * scale * gain_ref[...]).astype(BF)
    first = jnp.broadcast_to(routes_ref[0:1, :], (8, tokens))
    second = jnp.broadcast_to(routes_ref[1:2, :], (8, tokens))
    row = iota((8, tokens), 0)
    before = (iota((tokens, tokens), 0) < iota((tokens, tokens), 1)).astype(BF)
    main, ninth = [], []
    for k in range(EXPERTS):
        expert = e_ref[0] ^ k
        hit = jnp.where((first == expert) | (second == expert), 1.0, 0.0)
        rank = dot(hit.astype(BF), before)
        main.append(jnp.where(rank == row.astype(F32), hit, 0.0))
        ninth.append(jnp.where(rank == 8.0, hit, 0.0))
    main = jnp.concatenate(main, axis=0).astype(BF)
    ninth = jnp.concatenate(ninth, axis=0)
    rows = iota(ninth.shape, 0) % 8
    picked = dot(main, units).astype(BF)
    cut = jnp.zeros((8 * EXPERTS, piece), F32)
    for j in range(8):
        cut = cut + dot(
            jnp.where(rows == j, ninth, 0.0).astype(BF), units[:, j * piece : (j + 1) * piece]
        )
    cut = cut.astype(BF)
    info = jnp.where(row == 0, first.astype(F32), second.astype(F32))
    for choice in range(2):
        gate = jnp.broadcast_to(gates_ref[choice : choice + 1, :], (8, tokens))
        for part in range(3):
            rounded = gate.astype(BF).astype(F32)
            info = jnp.where(row == 2 + 3 * choice + part, rounded, info)
            gate = gate - rounded
    spread = (iota((tokens, TAIL), 0) == iota((tokens, TAIL), 1)).astype(BF)
    tail = dot(info.astype(BF), spread).astype(BF)
    for k in range(EXPERTS):
        expert = e_ref[0] ^ k
        chunks[k][:, :width] = picked[8 * k : 8 * k + 8]
        chunks[k][:, width : width + piece] = cut[8 * k : 8 * k + 8]
        chunks[k][:, width + piece :] = tail
        start = pl.multiple_of(expert * quarter, 128)
        parts[k][...] = hidden_ref[:, pl.ds(start, quarter)]


def pack(e, hidden, gain, routes_t, gates_t):
    tokens, width = hidden.shape
    chunk = jax.ShapeDtypeStruct((8, width + width // 8 + TAIL), BF)
    part = jax.ShapeDtypeStruct((tokens, width // EXPERTS), BF)
    hbm = pl.BlockSpec(memory_space=pltpu.HBM)
    vmem = pl.BlockSpec(memory_space=pltpu.VMEM)
    given = [hidden, gain, routes_t, gates_t]
    placed = [pltpu.with_memory_space_constraint(a, pltpu.HBM) for a in given]
    return pl.pallas_call(
        pack_kernel,
        out_shape=[chunk] * EXPERTS + [part] * EXPERTS,
        in_specs=[pl.BlockSpec(memory_space=pltpu.SMEM)] + [hbm] * 4,
        out_specs=[vmem] * (2 * EXPERTS),
        scratch_shapes=[pltpu.VMEM(a.shape, a.dtype) for a in given]
        + [pltpu.SemaphoreType.DMA((4,))],
        compiler_params=params(8),
        cost_estimate=COST,
        name="pack",
    )(e, *placed)


def down(split, e_ref, act, w_out, keep, send, first):
    quarter = keep.shape[3]
    step = quarter // 2
    main_rows = 32 * split
    for k in range(keep.shape[1]):
        start = (e_ref[0] ^ (first + k)) * quarter
        for h in range(2):
            columns = pl.ds(pl.multiple_of(start + h * step, 128), step)
            out = dot(act[...], w_out[0, :, columns])
            for r in range(split):
                lower = out[32 * r : 32 * r + 32]
                upper = out[main_rows + 8 * r : main_rows + 8 * r + 8]
                mine = jnp.concatenate([lower, upper], axis=0).astype(BF)
                (send if r % 2 else keep)[r // 2, k, :, h * step : (h + 1) * step] = mine


def expert_kernel(split, e_ref, *refs):
    groups = refs[: 2 * split]
    w_in, w_out, act, *pieces, x = refs[2 * split :]
    width = w_in.shape[1]
    hid = act.shape[1]
    piece = width // 8
    main_rows, last_rows = 32 * split, 8 * split
    for r in range(2 * split):
        x[16 * r : 16 * r + 16, :] = groups[r][:, :width]
    ext = jnp.concatenate([g[:, width : width + piece] for g in groups], axis=0)
    row = iota((8 * last_rows, main_rows), 0)
    col = iota((8 * last_rows, main_rows), 1)
    place = row % last_rows
    want = 32 * (place // 8) + 8 * (place % 8) + row // last_rows
    pick = jnp.where((place % 8 < 4) & (col == want), 1.0, 0.0).astype(BF)
    last = dot(pick, ext).astype(BF)
    for j in range(8):
        x[main_rows:, j * piece : (j + 1) * piece] = last[j * last_rows : (j + 1) * last_rows]
    step = min(256, hid)
    for i in range(hid // step):
        gate = dot(x[...], w_in[0, :, i * step : (i + 1) * step])
        up = dot(x[...], w_in[0, :, hid + i * step : hid + (i + 1) * step])
        act[:, i * step : (i + 1) * step] = (gate / (1.0 + jnp.exp(-gate)) * up).astype(BF)
    down(split, e_ref, act, w_out, pieces[0], pieces[1], 3)
    down(split, e_ref, act, w_out, pieces[2], pieces[3], 2)


def expert_rest_kernel(split, e_ref, act, w_out, keep, send):
    down(split, e_ref, act, w_out, keep, send, 0)


def expert_slice(e, groups, w_in, w_out):
    split = len(groups) // 2
    width, hid2 = w_in.shape[1:]
    hid = hid2 // 2
    quarter = width // EXPERTS
    half = jax.ShapeDtypeStruct((split // 2, EXPERTS // 2, ROWS, quarter), BF)
    single = jax.ShapeDtypeStruct((split // 2, 1, ROWS, quarter), BF)
    rows = ROWS * split
    act = jax.ShapeDtypeStruct((rows, hid), BF)
    vmem = pl.BlockSpec(memory_space=pltpu.VMEM)
    smem = pl.BlockSpec(memory_space=pltpu.SMEM)
    act, *single = pl.pallas_call(
        functools.partial(expert_kernel, split),
        out_shape=[act] + [single] * 4,
        in_specs=[smem] + [vmem] * (2 * split + 2),
        out_specs=[vmem] * 5,
        scratch_shapes=[pltpu.VMEM((rows, width), BF)],
        compiler_params=params(10),
        cost_estimate=COST,
        name="experts",
    )(e, *groups, w_in, w_out)
    rest = pl.pallas_call(
        functools.partial(expert_rest_kernel, split),
        out_shape=[half, half],
        in_specs=[smem] + [vmem] * 2,
        out_specs=[vmem] * 2,
        compiler_params=params(6),
        cost_estimate=COST,
        name="experts_rest",
    )(e, act, w_out)
    return single[:2], single[2:], rest


def join_kernel(a_ref, b_ref, out_ref):
    rows = a_ref.shape[0]
    out_ref[:rows, :] = a_ref[...]
    out_ref[rows:, :] = b_ref[...]


def join(a, b):
    vmem = pl.BlockSpec(memory_space=pltpu.VMEM)
    return pl.pallas_call(
        join_kernel,
        out_shape=pltpu.VMEM((2 * a.shape[0], a.shape[1]), a.dtype),
        in_specs=[vmem, vmem],
        out_specs=vmem,
        compiler_params=params(2),
        cost_estimate=COST,
        name="join",
    )(a, b)


def gate_kernel(tokens, e_ref, *refs):
    w_hbm, out_ref, w_ref, sem = refs[-4:]
    load = pltpu.make_async_copy(w_hbm, w_ref, sem)
    load.start()
    info = jnp.concatenate([r[:, r.shape[1] - TAIL :] for r in refs[:-4]], axis=0)
    one = (iota((tokens, TAIL), 0) == iota((tokens, TAIL), 1)).astype(BF)
    info = dot_t(one, info)
    earlier = (iota((tokens, tokens), 1) < iota((tokens, tokens), 0)).astype(BF)
    lanes = EXPERTS * SPACED
    lane = iota((tokens, lanes), 1).astype(F32)
    hits = []
    for k in range(EXPERTS):
        expert = (e_ref[0] ^ k).astype(F32)
        hits.append(jnp.where(info == expert, 1.0, 0.0))
    blocks = [[0.0] * EXPERTS for _ in range(3)]
    for k in range(EXPERTS):
        for s in range(EXPERTS):
            h0 = hits[k][:, 8 * s : 8 * s + 1]
            h1 = hits[k][:, 8 * s + 1 : 8 * s + 2]
            hit = jnp.broadcast_to(h0 + h1, (tokens, lanes))
            rank = dot(earlier, hit.astype(BF))
            line = s ^ k
            want = SPACED * k + jnp.where(rank < 8.0, rank + 8.0 * line, 32.0 + line)
            chosen = (lane == want) & (hit > 0.5)
            for p in range(3):
                g0 = info[:, 8 * s + 2 + p : 8 * s + 3 + p]
                g1 = info[:, 8 * s + 5 + p : 8 * s + 6 + p]
                gate = jnp.broadcast_to(h0 * g0 + h1 * g1, (tokens, lanes))
                blocks[p][s] = jnp.where(chosen, gate, blocks[p][s])
    out_ref[...] = jnp.concatenate(blocks[0] + blocks[1] + blocks[2], axis=0).astype(BF)
    load.wait()

def gate_matrices(place, halves, weight, tokens):
    vmem = pl.BlockSpec(memory_space=pltpu.VMEM)
    return pl.pallas_call(
        functools.partial(gate_kernel, tokens),
        out_shape=[
            pltpu.VMEM((3 * EXPERTS * tokens, EXPERTS * SPACED), BF),
            pltpu.VMEM(weight.shape, weight.dtype),
        ],
        in_specs=[pl.BlockSpec(memory_space=pltpu.SMEM)]
        + [vmem] * len(halves)
        + [pl.BlockSpec(memory_space=pltpu.HBM)],
        out_specs=[vmem] * 2,
        scratch_shapes=[pltpu.SemaphoreType.DMA],
        compiler_params=params(4),
        cost_estimate=LONG,
        name="gates",
    )(place, *halves, pltpu.with_memory_space_constraint(weight, pltpu.HBM))


def combine_kernel(spots, tokens, e_ref, *refs):
    outs_e, hid = refs[:EXPERTS], refs[EXPERTS : 2 * EXPERTS]
    gates_ref, gain_ref = refs[2 * EXPERTS : 2 * EXPERTS + 2]
    kvs = refs[2 * EXPERTS + 2 : 2 * EXPERTS + 2 + len(spots)]
    rest = refs[2 * EXPERTS + 2 + len(spots) :]
    own_sum, own_part = rest[:2]
    sent = rest[2 : 1 + EXPERTS]
    kv_ref, rows_ref, sem = rest[1 + EXPERTS :]
    lat = kvs[0].shape[1]
    part = spots[0][1]
    copies = []
    for i, (r, rows, first) in enumerate(spots):
        place = pl.multiple_of((e_ref[1] ^ r) * part + first, 16)
        copies.append(pltpu.make_async_copy(kvs[i], kv_ref.at[pl.ds(place, rows), :], sem.at[i]))
        copies[-1].start()
    gap = jnp.zeros((SPACED - ROWS, outs_e[0].shape[1]), F32)
    for k in range(EXPERTS):
        spaced = jnp.concatenate([outs_e[k][...].astype(F32), gap], axis=0)
        rows_ref[SPACED * k : SPACED * (k + 1), :] = spaced.astype(BF)
    moe = dot(gates_ref[...], rows_ref[...])
    total = EXPERTS * tokens
    moe = moe[:total] + moe[total : 2 * total] + moe[2 * total :]
    mixed = jnp.concatenate([h[...].astype(F32) for h in hid], axis=0) + moe
    square = jnp.sum(mixed * mixed, axis=-1, keepdims=True)
    scaled = (mixed * gain_ref[...]).astype(BF)
    for c in copies:
        c.wait()
    rows = dot(scaled, kv_ref[...])
    padded = own_sum.shape[1]
    for s in range(EXPERTS):
        span = slice(s * tokens, (s + 1) * tokens)
        rest = jnp.broadcast_to(square[span], (tokens, padded - lat))
        first = iota(rest.shape, 1) == 0
        if s:
            high = rest.astype(BF).astype(F32)
            sent[s - 1][:, :lat] = rows[span].astype(BF)
            sent[s - 1][:, lat:padded] = jnp.where(first, high, rest - high).astype(BF)
            sent[s - 1][:, padded:] = mixed[span].astype(BF)
        else:
            own_sum[:, :lat] = rows[span]
            own_sum[:, lat:] = jnp.where(first, rest, 0.0)
            own_part[...] = mixed[span].astype(BF)


def combine(place, outs_e, hid, gates, gain, kvs):
    spots = [(r, x.shape[0], first) for r, first, x in kvs]
    kvs = [x for _, _, x in kvs]
    tokens, quarter = hid[0].shape
    lat = kvs[0].shape[1]
    padded = (lat // 128 + 1) * 128
    outs = [pltpu.VMEM((tokens, padded), F32), pltpu.VMEM((tokens, quarter), BF)]
    outs += [pltpu.VMEM((tokens, padded + quarter), BF)] * (EXPERTS - 1)
    return pl.pallas_call(
        functools.partial(combine_kernel, spots, tokens),
        out_shape=outs,
        grid_spec=pltpu.PrefetchScalarGridSpec(
            num_scalar_prefetch=1,
            grid=(1,),
            in_specs=[whole(o.shape) for o in outs_e]
            + [whole(h.shape) for h in hid]
            + [
                whole(gates.shape),
                pl.BlockSpec((1, quarter), lambda t, e: (0, e[0])),
            ]
            + [pl.BlockSpec(memory_space=pl.ANY)] * len(kvs),
            out_specs=[whole(o.shape) for o in outs],
            scratch_shapes=[
                pltpu.VMEM((quarter, lat), BF),
                pltpu.VMEM((EXPERTS * SPACED, quarter), BF),
                pltpu.SemaphoreType.DMA((len(kvs),)),
            ],
        ),
        compiler_params=params(8),
        cost_estimate=COST,
        name="combine",
    )(place, *outs_e, *hid, gates, gain, *kvs)


def cached_kernel(begin, per, length_ref, *refs):
    q_ref, cache_ref, keys_ref, sem = refs[-4:]
    loads = (len(refs) - 8) // 2
    q_hbm, cache_hbm = refs[:2]
    w_hbm = refs[2 : 2 + loads]
    out_ref, stat_ref = refs[2 + loads : 4 + loads]
    w_ref = refs[4 + loads : -4]
    nodes, lat, heads = q_ref.shape
    ctx = cache_ref.shape[2]
    spare = keys_ref.shape[1] - lat
    copies = [
        pltpu.make_async_copy(cache_hbm, cache_ref, sem.at[0]),
        pltpu.make_async_copy(q_hbm.at[pl.ds(begin, nodes)], q_ref, sem.at[1]),
    ]
    for i in range(loads):
        copies.append(pltpu.make_async_copy(w_hbm[i], w_ref[i], sem.at[2 + i]))
    for c in copies:
        c.start()
    unused = (iota((ctx, spare), 0) >= length_ref[0]) & (iota((ctx, spare), 1) == 0)
    keys_ref[:, lat:] = jnp.where(unused, -jnp.inf, 0.0).astype(BF)
    one = (iota((spare, per * heads), 0) == 0).astype(BF)
    factor = softmax_scale * LOG2E
    copies[0].wait()
    keys_ref[:, :lat] = cache_ref[0].T
    copies[1].wait()

    for g in range(nodes // per):
        q = jnp.concatenate([q_ref[g * per + i] for i in range(per)], axis=1)
        q = jnp.concatenate([q, one], axis=0)
        scores = dot(keys_ref[...], q)
        top = jnp.max(scores, axis=0, keepdims=True) * factor
        weight = jnp.exp2(scores * factor - top)
        total = jnp.sum(weight, axis=0, keepdims=True)
        out = dot(cache_ref[0, :KEY_VALUE_RANK, :], weight.astype(BF)) * (1.0 / total)
        for i in range(per):
            span = slice(i * heads, (i + 1) * heads)
            out_ref[g * per + i] = out[:, span].T.astype(out_ref.dtype)
            stat_ref[g * per + i] = jnp.concatenate([top[:, span], total[:, span]], axis=0)
    for c in copies[2:]:
        c.wait()


def cached_attention(lengths, q_t, cache_t, weights, first, count, per=4, cost=None):
    tokens, lat, heads = q_t.shape
    ctx = cache_t.shape[2]
    hbm = pl.BlockSpec(memory_space=pltpu.HBM)
    vmem = pl.BlockSpec(memory_space=pltpu.VMEM)
    given = [pltpu.with_memory_space_constraint(a, pltpu.HBM) for a in (q_t, cache_t, *weights)]
    return pl.pallas_call(
        functools.partial(cached_kernel, first, per),
        out_shape=[
            pltpu.VMEM((count, heads, KEY_VALUE_RANK), BF),
            pltpu.VMEM((count, 2, heads), F32),
        ]
        + [pltpu.VMEM(w.shape, w.dtype) for w in weights],
        in_specs=[pl.BlockSpec(memory_space=pltpu.SMEM)] + [hbm] * len(given),
        out_specs=[vmem] * len(given),
        scratch_shapes=[
            pltpu.VMEM((count, lat, heads), BF),
            pltpu.VMEM(cache_t.shape, BF),
            pltpu.VMEM((ctx, (lat // 128 + 1) * 128), BF),
            pltpu.SemaphoreType.DMA((2 + len(weights),)),
        ],
        compiler_params=params(10),
        cost_estimate=cost
        or pl.CostEstimate(
            flops=4 * count * heads * ctx * (lat + KEY_VALUE_RANK),
            bytes_accessed=4 * count * heads * lat,
            transcendentals=count * heads * ctx,
        ),
        name="cached",
    )(lengths, *given)


def final_kernel(width, per, e_ref, *refs):
    own_sum, own_part = refs[:2]
    got = refs[2 : 1 + EXPERTS]
    gain_ref, turn_ref, allow_ref, q_ref = refs[1 + EXPERTS : 5 + EXPERTS]
    cached = refs[5 + EXPERTS : -5]
    part_ref, entry_ref, out_hbm, out_ref, sem = refs[-5:]
    found = []
    for ctx_ref, stat_ref in zip(cached[0::2], cached[1::2]):
        found += [(ctx_ref, stat_ref, i) for i in range(ctx_ref.shape[0])]
    nodes, lat, heads = q_ref.shape
    padded = own_sum.shape[1]
    quarter = own_part.shape[1]
    raw = own_sum[...]
    for g in got:
        raw = raw + g[:, :padded].astype(F32)
    square = raw[:, lat : lat + 1] + raw[:, lat + 1 : lat + 2]
    raw = raw * lax.rsqrt(square / width + 1e-06)
    head = raw[:, :KEY_VALUE_RANK]
    head = head * lax.rsqrt(jnp.mean(head * head, axis=-1, keepdims=True) + 1e-06)
    head = head * gain_ref[...]
    tail = raw[:, KEY_VALUE_RANK:]
    half = (lat - KEY_VALUE_RANK) // 2
    lanes = tail.shape[1]
    tail = (
        tail * turn_ref[0]
        + pltpu.roll(tail, lanes - half, 1) * turn_ref[1]
        + pltpu.roll(tail, half, 1) * turn_ref[2]
    )
    keys = jnp.concatenate([head, tail], axis=1).astype(BF)[:, :lat]
    entry_ref[...] = keys
    count = keys.shape[0]
    copies = []
    for g in range(nodes // per):
        span = range(g * per, (g + 1) * per)

        def side(ref):
            return jnp.concatenate([ref[i] for i in span], axis=1)

        scores = dot(keys, side(q_ref)) * (softmax_scale * LOG2E)
        scores = jnp.where(side(allow_ref) > 0.5, scores, -jnp.inf)
        stats = jnp.concatenate([found[i][1][found[i][2]] for i in span], axis=1)
        old = stats[0:1]
        top = jnp.maximum(old, jnp.max(scores, axis=0, keepdims=True))
        weight = jnp.exp2(scores - top)
        share = stats[1:2] * jnp.exp2(old - top)
        scale = 1.0 / (share + jnp.sum(weight, axis=0, keepdims=True))
        share = jnp.broadcast_to(share * scale, (8, per * heads))
        both = jnp.concatenate([weight * scale, share], axis=0).T
        for i in range(per):
            mine = both[i * heads : (i + 1) * heads]
            ctx_ref, _, place = found[g * per + i]
            out = ctx_ref[place].astype(F32) * mine[:, count : count + 1]
            out = out + dot(mine[:, :count].astype(BF), keys[:, :KEY_VALUE_RANK])
            out_ref[g * per + i] = out.astype(BF)
        here = pl.ds(g * per, per)
        copies.append(pltpu.make_async_copy(out_ref.at[here], out_hbm.at[here], sem.at[g]))
        copies[-1].start()
    for k in range(EXPERTS):
        start = pl.multiple_of((e_ref[0] ^ k) * quarter, 128)
        part_ref[:, pl.ds(start, quarter)] = got[k - 1][:, padded:] if k else own_part[...]
    for c in copies:
        c.wait()


def final_attention(place, width, rows, gain, turn, allow, q_t, cached, per=8):
    tokens, lat, heads = q_t.shape
    vmem = pl.BlockSpec(memory_space=pltpu.VMEM)
    given = [*rows, gain, turn, allow, q_t, *cached]
    given = [pltpu.with_memory_space_constraint(x, pltpu.VMEM) for x in given]
    out = jax.ShapeDtypeStruct((tokens, heads, KEY_VALUE_RANK), BF)
    return pl.pallas_call(
        functools.partial(final_kernel, width, per),
        out_shape=[
            jax.ShapeDtypeStruct((tokens, width), BF),
            jax.ShapeDtypeStruct((tokens, lat), BF),
            out,
        ],
        in_specs=[pl.BlockSpec(memory_space=pltpu.SMEM)] + [vmem] * len(given),
        out_specs=[vmem, vmem, pl.BlockSpec(memory_space=pltpu.HBM)],
        scratch_shapes=[
            pltpu.VMEM(out.shape, BF),
            pltpu.SemaphoreType.DMA((tokens // per,)),
        ],
        compiler_params=params(12),
        cost_estimate=COST,
        name="final",
    )(place, *given)


def tree(parents, lengths, rank, lat):
    count = parents.shape[1]
    link = (parents[0][:, None] == jnp.arange(count, dtype=jnp.int32)[None, :]).astype(F32)
    reach = jnp.eye(count, dtype=F32) + link
    for _ in range(max(1, (count - 1).bit_length())):
        reach = jnp.minimum(jnp.dot(reach, reach, precision=lax.Precision.HIGHEST), 1.0)
    depth = jnp.sum(reach, axis=-1) - 1.0
    position = lengths.astype(F32) + depth
    half = (lat - rank) // 2
    index = jnp.arange(half, dtype=F32)
    inverse = 10000.0 ** (-2.0 * index / (2 * half))
    angle = position[:, None] * inverse[None, :]
    c, s = jnp.cos(angle), jnp.sin(angle)
    gap = jnp.zeros((count, 128 - 2 * half), F32)
    none = jnp.zeros_like(s)
    turn = jnp.stack(
        [
            jnp.concatenate([c, c, gap], axis=1),
            jnp.concatenate([-s, none, gap], axis=1),
            jnp.concatenate([none, s, gap], axis=1),
        ]
    )
    return reach, turn


def local(
    hidden,
    ffn_gain,
    attn_gain,
    latent_norm_gain,
    routes,
    gate_weights,
    expert_in,
    expert_down,
    kv_down,
    parents,
    lengths,
    queries,
    cache,
):
    size = lax.axis_size("ep")
    split = size // EXPERTS
    bits = [1 << b for b in range(split.bit_length() - 1)]
    width = hidden.shape[1]
    lat = kv_down.shape[1]
    heads = queries.shape[1]
    index = lax.axis_index("ep")
    place = jnp.stack([index // split, index % split]).astype(jnp.int32)

    def swap(x, bit):
        return lax.ppermute(x, "ep", [(i, i ^ bit) for i in range(size)])

    def spread(have, some):
        for bit in some:
            for r in sorted(have):
                have = have | {r ^ bit: swap(have[r], bit)}
        return have

    def to_line(xs):
        got = {k: swap(xs[k], k * split) for k in (3, 2, 1)}
        return [xs[0], got[1], got[2], got[3]]

    q_t = jnp.transpose(queries, (0, 2, 1))
    cache_t = jnp.transpose(cache, (0, 2, 1))
    half = queries.shape[0] // 2
    reach, turn = tree(parents, lengths, KEY_VALUE_RANK, lat)
    allow = jnp.broadcast_to(reach[:, :, None], reach.shape + (heads,))

    packed = pack(place, hidden, ffn_gain[None], routes.T, gate_weights.T)
    own = packed[:EXPERTS]
    top, low = bits[-1], bits[:-1]
    kvs = spread({0: kv_down}, [top])
    near = to_line(own)
    lower = join(near[0], near[1])
    lowers = spread({0: lower}, [top])
    q_first = after(q_t, lower, allow, turn)
    *first, w_in = cached_attention(lengths, q_first, cache_t, [expert_in], 0, half, per=8)
    quarters = packed[EXPERTS:]
    near_quarter = swap(quarters[1], split)
    distant, first, kvs, near_quarter = lax.optimization_barrier(
        (near[2:], first, kvs, near_quarter)
    )
    upper = join(*distant)
    across = {top: swap(upper, top)}
    uppers = spread({0: upper}, low[::-1])
    sent = after(quarters[2:], uppers)
    own_quarters = [swap(sent[k - 2], k * split) for k in (3, 2)]
    lowers = spread(lowers, low[::-1])
    gates, w_out = gate_matrices(place, (lower, upper), expert_down, hidden.shape[0])
    lowers, uppers, across, own_quarters, gates = lax.optimization_barrier(
        (lowers, uppers, across, own_quarters, gates)
    )
    uppers = uppers | spread(across, low[::-1])
    groups = [x for r in range(split) for x in (lowers[r], uppers[r])]
    pieces = expert_slice(place, groups, w_in, w_out)

    kvs = spread(after(kvs, pieces[0]), low[::-1])
    kvs = [(r, 0, x) for r, x in kvs.items()]

    def inner(keep, send):
        terms = [keep, swap(send, bits[0])]
        for bit in bits[1:-1]:
            out = sum(t[1::2].astype(F32) for t in terms).astype(BF)
            terms = [t[0::2] for t in terms] + [swap(out, bit)]
        return [t[0] for t in terms], sum(t[1].astype(F32) for t in terms).astype(BF)

    def outer(terms, got):
        return [sum(t[k].astype(F32) for t in (*terms, got)).astype(BF) for k in range(len(got))]

    kept, out = zip(*[inner(*p) for p in pieces])
    got = [swap(x, top) for x in out]
    far = outer(kept[0], after(got[0], out[2]))
    middle = outer(kept[1], got[1])
    second = cached_attention(
        lengths, after(q_t, middle, out[2]), cache_t, [], half, half // 2, cost=LONG
    )
    close = outer(kept[2], after(got[2], second))
    outs_e = to_line(close + middle + far)
    third = cached_attention(
        lengths, after(q_t, close[1]), cache_t, [], half + half // 2, half // 2
    )
    outs_e, third = lax.optimization_barrier((outs_e, third))

    own_quarters = [quarters[0], near_quarter, own_quarters[1], own_quarters[0]]
    own_sum, own_part, *rows = combine(place, outs_e, own_quarters, gates, attn_gain[None], kvs)
    rows = [own_sum, own_part] + [swap(r, (k + 1) * split) for k, r in enumerate(rows)]
    return final_attention(
        place, width, rows, latent_norm_gain[None], turn, allow, q_t, [*first, *second, *third]
    )


def solution(mesh):
    placed = (
        P(("group", "ep"), None),
        P(),
        P(),
        P(),
        P(("group", "ep"), None),
        P(("group", "ep"), None),
        P("ep", None, None),
        P("ep", None, None),
        P("ep", None),
        P(("group", "ep"), None),
        P(("group", "ep")),
        P(("group", "ep"), None, None),
        P(("group", "ep"), None, None),
    )
    return jax.shard_map(
        local,
        mesh=mesh,
        in_specs=placed,
        out_specs=(
            P(("group", "ep"), None),
            P(("group", "ep"), None),
            P(("group", "ep"), None, None),
        ),
        check_vma=False,
    )
```

```python
import functools

import jax
import jax.numpy as jnp
from jax import lax
from jax.experimental import pallas as pl
from jax.experimental.pallas import tpu as pltpu
from jax.sharding import PartitionSpec as P

KEY_VALUE_RANK = 512
NODES = 16
EXPERTS = 4
CAP = 9
TAIL = 128
ROWS = 40
SPACED = 48
BF = jnp.bfloat16
F32 = jnp.float32
softmax_scale = 192.0 ** (-0.5)
MIB = 1024 * 1024
LONG = pl.CostEstimate(flops=1 << 34, bytes_accessed=1 << 24, transcendentals=0)
COST = pl.CostEstimate(flops=1024, bytes_accessed=1024, transcendentals=0)
LOG2E = 1.4426950408889634


def iota(shape, dim):
    return lax.broadcasted_iota(jnp.int32, shape, dim)


def dot(a, b):
    return jnp.dot(a, b, preferred_element_type=F32)


def dot_t(a, b):
    return lax.dot_general(a, b, (((1,), (1,)), ((), ())), preferred_element_type=F32)


def params(mib, semantics=None):
    return pltpu.CompilerParams(vmem_limit_bytes=mib * MIB, dimension_semantics=semantics)


def after(x, *others):
    return lax.optimization_barrier((x, others))[0]


def whole(shape):
    zeros = (0,) * len(shape)
    return pl.BlockSpec(shape, lambda *_: zeros)


def pack_kernel(e_ref, *refs):
    ins, outs = refs[:4], refs[4 : 4 + 2 * EXPERTS]
    held, sem = refs[4 + 2 * EXPERTS : -1], refs[-1]
    copies = [pltpu.make_async_copy(a, b, sem.at[i]) for i, (a, b) in enumerate(zip(ins, held))]
    for c in copies:
        c.start()
    for c in copies:
        c.wait()
    hidden_ref, gain_ref, routes_ref, gates_ref = held
    chunks, parts = outs[:EXPERTS], outs[EXPERTS:]
    tokens, width = hidden_ref.shape
    piece = width // 8
    quarter = width // EXPERTS
    x = hidden_ref[...].astype(F32)
    scale = lax.rsqrt(jnp.mean(x * x, axis=-1, keepdims=True) + 1e-06)
    units = (x * scale * gain_ref[...]).astype(BF)
    first = jnp.broadcast_to(routes_ref[0:1, :], (8, tokens))
    second = jnp.broadcast_to(routes_ref[1:2, :], (8, tokens))
    row = iota((8, tokens), 0)
    before = (iota((tokens, tokens), 0) < iota((tokens, tokens), 1)).astype(BF)
    main, ninth = [], []
    for k in range(EXPERTS):
        expert = e_ref[0] ^ k
        hit = jnp.where((first == expert) | (second == expert), 1.0, 0.0)
        rank = dot(hit.astype(BF), before)
        main.append(jnp.where(rank == row.astype(F32), hit, 0.0))
        ninth.append(jnp.where(rank == 8.0, hit, 0.0))
    main = jnp.concatenate(main, axis=0).astype(BF)
    ninth = jnp.concatenate(ninth, axis=0)
    rows = iota(ninth.shape, 0) % 8
    picked = dot(main, units).astype(BF)
    cut = jnp.zeros((8 * EXPERTS, piece), F32)
    for j in range(8):
        cut = cut + dot(
            jnp.where(rows == j, ninth, 0.0).astype(BF), units[:, j * piece : (j + 1) * piece]
        )
    cut = cut.astype(BF)
    info = jnp.where(row == 0, first.astype(F32), second.astype(F32))
    for choice in range(2):
        gate = jnp.broadcast_to(gates_ref[choice : choice + 1, :], (8, tokens))
        for part in range(3):
            rounded = gate.astype(BF).astype(F32)
            info = jnp.where(row == 2 + 3 * choice + part, rounded, info)
            gate = gate - rounded
    spread = (iota((tokens, TAIL), 0) == iota((tokens, TAIL), 1)).astype(BF)
    tail = dot(info.astype(BF), spread).astype(BF)
    for k in range(EXPERTS):
        expert = e_ref[0] ^ k
        chunks[k][:, :width] = picked[8 * k : 8 * k + 8]
        chunks[k][:, width : width + piece] = cut[8 * k : 8 * k + 8]
        chunks[k][:, width + piece :] = tail
        start = pl.multiple_of(expert * quarter, 128)
        parts[k][...] = hidden_ref[:, pl.ds(start, quarter)]


def pack(e, hidden, gain, routes_t, gates_t):
    tokens, width = hidden.shape
    chunk = jax.ShapeDtypeStruct((8, width + width // 8 + TAIL), BF)
    part = jax.ShapeDtypeStruct((tokens, width // EXPERTS), BF)
    hbm = pl.BlockSpec(memory_space=pltpu.HBM)
    vmem = pl.BlockSpec(memory_space=pltpu.VMEM)
    given = [hidden, gain, routes_t, gates_t]
    placed = [pltpu.with_memory_space_constraint(a, pltpu.HBM) for a in given]
    return pl.pallas_call(
        pack_kernel,
        out_shape=[chunk] * EXPERTS + [part] * EXPERTS,
        in_specs=[pl.BlockSpec(memory_space=pltpu.SMEM)] + [hbm] * 4,
        out_specs=[vmem] * (2 * EXPERTS),
        scratch_shapes=[pltpu.VMEM(a.shape, a.dtype) for a in given]
        + [pltpu.SemaphoreType.DMA((4,))],
        compiler_params=params(8),
        cost_estimate=COST,
        name="pack",
    )(e, *placed)


def down(split, e_ref, act, w_out, keep, send, first):
    quarter = keep.shape[3]
    step = quarter // 2
    main_rows = 32 * split
    for k in range(keep.shape[1]):
        start = (e_ref[0] ^ (first + k)) * quarter
        for h in range(2):
            columns = pl.ds(pl.multiple_of(start + h * step, 128), step)
            out = dot(act[...], w_out[0, :, columns])
            for r in range(split):
                lower = out[32 * r : 32 * r + 32]
                upper = out[main_rows + 8 * r : main_rows + 8 * r + 8]
                mine = jnp.concatenate([lower, upper], axis=0).astype(BF)
                (send if r % 2 else keep)[r // 2, k, :, h * step : (h + 1) * step] = mine


def expert_kernel(split, e_ref, *refs):
    groups = refs[: 2 * split]
    w_in, w_out, act, *pieces, x = refs[2 * split :]
    width = w_in.shape[1]
    hid = act.shape[1]
    piece = width // 8
    main_rows, last_rows = 32 * split, 8 * split
    for r in range(2 * split):
        x[16 * r : 16 * r + 16, :] = groups[r][:, :width]
    ext = jnp.concatenate([g[:, width : width + piece] for g in groups], axis=0)
    row = iota((8 * last_rows, main_rows), 0)
    col = iota((8 * last_rows, main_rows), 1)
    place = row % last_rows
    want = 32 * (place // 8) + 8 * (place % 8) + row // last_rows
    pick = jnp.where((place % 8 < 4) & (col == want), 1.0, 0.0).astype(BF)
    last = dot(pick, ext).astype(BF)
    for j in range(8):
        x[main_rows:, j * piece : (j + 1) * piece] = last[j * last_rows : (j + 1) * last_rows]
    step = min(256, hid)
    for i in range(hid // step):
        gate = dot(x[...], w_in[0, :, i * step : (i + 1) * step])
        up = dot(x[...], w_in[0, :, hid + i * step : hid + (i + 1) * step])
        act[:, i * step : (i + 1) * step] = (gate / (1.0 + jnp.exp(-gate)) * up).astype(BF)
    down(split, e_ref, act, w_out, pieces[0], pieces[1], 3)


def expert_rest_kernel(split, e_ref, act, w_out, *pieces):
    down(split, e_ref, act, w_out, pieces[0], pieces[1], 2)
    down(split, e_ref, act, w_out, pieces[2], pieces[3], 0)


def expert_slice(e, groups, w_in, w_out):
    split = len(groups) // 2
    width, hid2 = w_in.shape[1:]
    hid = hid2 // 2
    quarter = width // EXPERTS
    half = jax.ShapeDtypeStruct((split // 2, EXPERTS // 2, ROWS, quarter), BF)
    single = jax.ShapeDtypeStruct((split // 2, 1, ROWS, quarter), BF)
    rows = ROWS * split
    act = jax.ShapeDtypeStruct((rows, hid), BF)
    vmem = pl.BlockSpec(memory_space=pltpu.VMEM)
    smem = pl.BlockSpec(memory_space=pltpu.SMEM)
    single_shape = single
    act, *single = pl.pallas_call(
        functools.partial(expert_kernel, split),
        out_shape=[act] + [single] * 2,
        in_specs=[smem] + [vmem] * (2 * split + 2),
        out_specs=[vmem] * 3,
        scratch_shapes=[pltpu.VMEM((rows, width), BF)],
        compiler_params=params(10),
        cost_estimate=COST,
        name="experts",
    )(e, *groups, w_in, w_out)
    rest = pl.pallas_call(
        functools.partial(expert_rest_kernel, split),
        out_shape=[single_shape, single_shape, half, half],
        in_specs=[smem] + [vmem] * 2,
        out_specs=[vmem] * 4,
        compiler_params=params(6),
        cost_estimate=COST,
        name="experts_rest",
    )(e, act, w_out)
    return single, rest[:2], rest[2:]


def join_kernel(a_ref, b_ref, out_ref):
    rows = a_ref.shape[0]
    out_ref[:rows, :] = a_ref[...]
    out_ref[rows:, :] = b_ref[...]


def join(a, b):
    vmem = pl.BlockSpec(memory_space=pltpu.VMEM)
    return pl.pallas_call(
        join_kernel,
        out_shape=pltpu.VMEM((2 * a.shape[0], a.shape[1]), a.dtype),
        in_specs=[vmem, vmem],
        out_specs=vmem,
        compiler_params=params(2),
        cost_estimate=COST,
        name="join",
    )(a, b)


def gate_kernel(tokens, e_ref, *refs):
    w_hbm, out_ref, w_ref, sem = refs[-4:]
    load = pltpu.make_async_copy(w_hbm, w_ref, sem)
    load.start()
    info = jnp.concatenate([r[:, r.shape[1] - TAIL :] for r in refs[:-4]], axis=0)
    one = (iota((tokens, TAIL), 0) == iota((tokens, TAIL), 1)).astype(BF)
    info = dot_t(one, info)
    earlier = (iota((tokens, tokens), 1) < iota((tokens, tokens), 0)).astype(BF)
    lanes = EXPERTS * SPACED
    lane = iota((tokens, lanes), 1).astype(F32)
    hits = []
    for k in range(EXPERTS):
        expert = (e_ref[0] ^ k).astype(F32)
        hits.append(jnp.where(info == expert, 1.0, 0.0))
    blocks = [[0.0] * EXPERTS for _ in range(3)]
    for k in range(EXPERTS):
        for s in range(EXPERTS):
            h0 = hits[k][:, 8 * s : 8 * s + 1]
            h1 = hits[k][:, 8 * s + 1 : 8 * s + 2]
            hit = jnp.broadcast_to(h0 + h1, (tokens, lanes))
            rank = dot(earlier, hit.astype(BF))
            line = s ^ k
            want = SPACED * k + jnp.where(rank < 8.0, rank + 8.0 * line, 32.0 + line)
            chosen = (lane == want) & (hit > 0.5)
            for p in range(3):
                g0 = info[:, 8 * s + 2 + p : 8 * s + 3 + p]
                g1 = info[:, 8 * s + 5 + p : 8 * s + 6 + p]
                gate = jnp.broadcast_to(h0 * g0 + h1 * g1, (tokens, lanes))
                blocks[p][s] = jnp.where(chosen, gate, blocks[p][s])
    out_ref[...] = jnp.concatenate(blocks[0] + blocks[1] + blocks[2], axis=0).astype(BF)
    load.wait()

def gate_matrices(place, halves, weight, tokens):
    vmem = pl.BlockSpec(memory_space=pltpu.VMEM)
    return pl.pallas_call(
        functools.partial(gate_kernel, tokens),
        out_shape=[
            pltpu.VMEM((3 * EXPERTS * tokens, EXPERTS * SPACED), BF),
            pltpu.VMEM(weight.shape, weight.dtype),
        ],
        in_specs=[pl.BlockSpec(memory_space=pltpu.SMEM)]
        + [vmem] * len(halves)
        + [pl.BlockSpec(memory_space=pltpu.HBM)],
        out_specs=[vmem] * 2,
        scratch_shapes=[pltpu.SemaphoreType.DMA],
        compiler_params=params(4),
        cost_estimate=LONG,
        name="gates",
    )(place, *halves, pltpu.with_memory_space_constraint(weight, pltpu.HBM))


def combine_kernel(spots, tokens, e_ref, *refs):
    outs_e, hid = refs[:EXPERTS], refs[EXPERTS : 2 * EXPERTS]
    gates_ref, gain_ref = refs[2 * EXPERTS : 2 * EXPERTS + 2]
    kvs = refs[2 * EXPERTS + 2 : 2 * EXPERTS + 2 + len(spots)]
    rest = refs[2 * EXPERTS + 2 + len(spots) :]
    own_sum, own_part = rest[:2]
    sent = rest[2 : 1 + EXPERTS]
    kv_ref, rows_ref, sem = rest[1 + EXPERTS :]
    lat = kvs[0].shape[1]
    part = spots[0][1]
    copies = []
    for i, (r, rows, first) in enumerate(spots):
        place = pl.multiple_of((e_ref[1] ^ r) * part + first, 16)
        copies.append(pltpu.make_async_copy(kvs[i], kv_ref.at[pl.ds(place, rows), :], sem.at[i]))
        copies[-1].start()
    gap = jnp.zeros((SPACED - ROWS, outs_e[0].shape[1]), F32)
    for k in range(EXPERTS):
        spaced = jnp.concatenate([outs_e[k][...].astype(F32), gap], axis=0)
        rows_ref[SPACED * k : SPACED * (k + 1), :] = spaced.astype(BF)
    moe = dot(gates_ref[...], rows_ref[...])
    total = EXPERTS * tokens
    moe = moe[:total] + moe[total : 2 * total] + moe[2 * total :]
    mixed = jnp.concatenate([h[...].astype(F32) for h in hid], axis=0) + moe
    square = jnp.sum(mixed * mixed, axis=-1, keepdims=True)
    scaled = (mixed * gain_ref[...]).astype(BF)
    for c in copies:
        c.wait()
    rows = dot(scaled, kv_ref[...])
    padded = own_sum.shape[1]
    for s in range(EXPERTS):
        span = slice(s * tokens, (s + 1) * tokens)
        rest = jnp.broadcast_to(square[span], (tokens, padded - lat))
        first = iota(rest.shape, 1) == 0
        if s:
            high = rest.astype(BF).astype(F32)
            sent[s - 1][:, :lat] = rows[span].astype(BF)
            sent[s - 1][:, lat:padded] = jnp.where(first, high, rest - high).astype(BF)
            sent[s - 1][:, padded:] = mixed[span].astype(BF)
        else:
            own_sum[:, :lat] = rows[span]
            own_sum[:, lat:] = jnp.where(first, rest, 0.0)
            own_part[...] = mixed[span].astype(BF)


def combine(place, outs_e, hid, gates, gain, kvs):
    spots = [(r, x.shape[0], first) for r, first, x in kvs]
    kvs = [x for _, _, x in kvs]
    tokens, quarter = hid[0].shape
    lat = kvs[0].shape[1]
    padded = (lat // 128 + 1) * 128
    outs = [pltpu.VMEM((tokens, padded), F32), pltpu.VMEM((tokens, quarter), BF)]
    outs += [pltpu.VMEM((tokens, padded + quarter), BF)] * (EXPERTS - 1)
    return pl.pallas_call(
        functools.partial(combine_kernel, spots, tokens),
        out_shape=outs,
        grid_spec=pltpu.PrefetchScalarGridSpec(
            num_scalar_prefetch=1,
            grid=(1,),
            in_specs=[whole(o.shape) for o in outs_e]
            + [whole(h.shape) for h in hid]
            + [
                whole(gates.shape),
                pl.BlockSpec((1, quarter), lambda t, e: (0, e[0])),
            ]
            + [pl.BlockSpec(memory_space=pl.ANY)] * len(kvs),
            out_specs=[whole(o.shape) for o in outs],
            scratch_shapes=[
                pltpu.VMEM((quarter, lat), BF),
                pltpu.VMEM((EXPERTS * SPACED, quarter), BF),
                pltpu.SemaphoreType.DMA((len(kvs),)),
            ],
        ),
        compiler_params=params(8),
        cost_estimate=COST,
        name="combine",
    )(place, *outs_e, *hid, gates, gain, *kvs)


def cached_kernel(begin, per, length_ref, *refs):
    q_ref, cache_ref, keys_ref, sem = refs[-4:]
    loads = (len(refs) - 8) // 2
    q_hbm, cache_hbm = refs[:2]
    w_hbm = refs[2 : 2 + loads]
    out_ref, stat_ref = refs[2 + loads : 4 + loads]
    w_ref = refs[4 + loads : -4]
    nodes, lat, heads = q_ref.shape
    ctx = cache_ref.shape[2]
    spare = keys_ref.shape[1] - lat
    copies = [
        pltpu.make_async_copy(cache_hbm, cache_ref, sem.at[0]),
        pltpu.make_async_copy(q_hbm.at[pl.ds(begin, nodes)], q_ref, sem.at[1]),
    ]
    for i in range(loads):
        copies.append(pltpu.make_async_copy(w_hbm[i], w_ref[i], sem.at[2 + i]))
    for c in copies:
        c.start()
    unused = (iota((ctx, spare), 0) >= length_ref[0]) & (iota((ctx, spare), 1) == 0)
    keys_ref[:, lat:] = jnp.where(unused, -jnp.inf, 0.0).astype(BF)
    one = (iota((spare, per * heads), 0) == 0).astype(BF)
    factor = softmax_scale * LOG2E
    copies[0].wait()
    keys_ref[:, :lat] = cache_ref[0].T
    copies[1].wait()

    for g in range(nodes // per):
        q = jnp.concatenate([q_ref[g * per + i] for i in range(per)], axis=1)
        q = jnp.concatenate([q, one], axis=0)
        scores = dot(keys_ref[...], q)
        top = jnp.max(scores, axis=0, keepdims=True) * factor
        weight = jnp.exp2(scores * factor - top)
        total = jnp.sum(weight, axis=0, keepdims=True)
        out = dot(cache_ref[0, :KEY_VALUE_RANK, :], weight.astype(BF)) * (1.0 / total)
        for i in range(per):
            span = slice(i * heads, (i + 1) * heads)
            out_ref[g * per + i] = out[:, span].T.astype(out_ref.dtype)
            stat_ref[g * per + i] = jnp.concatenate([top[:, span], total[:, span]], axis=0)
    for c in copies[2:]:
        c.wait()


def cached_attention(lengths, q_t, cache_t, weights, first, count, per=4, cost=None):
    tokens, lat, heads = q_t.shape
    ctx = cache_t.shape[2]
    hbm = pl.BlockSpec(memory_space=pltpu.HBM)
    vmem = pl.BlockSpec(memory_space=pltpu.VMEM)
    given = [pltpu.with_memory_space_constraint(a, pltpu.HBM) for a in (q_t, cache_t, *weights)]
    return pl.pallas_call(
        functools.partial(cached_kernel, first, per),
        out_shape=[
            pltpu.VMEM((count, heads, KEY_VALUE_RANK), BF),
            pltpu.VMEM((count, 2, heads), F32),
        ]
        + [pltpu.VMEM(w.shape, w.dtype) for w in weights],
        in_specs=[pl.BlockSpec(memory_space=pltpu.SMEM)] + [hbm] * len(given),
        out_specs=[vmem] * len(given),
        scratch_shapes=[
            pltpu.VMEM((count, lat, heads), BF),
            pltpu.VMEM(cache_t.shape, BF),
            pltpu.VMEM((ctx, (lat // 128 + 1) * 128), BF),
            pltpu.SemaphoreType.DMA((2 + len(weights),)),
        ],
        compiler_params=params(10),
        cost_estimate=cost
        or pl.CostEstimate(
            flops=4 * count * heads * ctx * (lat + KEY_VALUE_RANK),
            bytes_accessed=4 * count * heads * lat,
            transcendentals=count * heads * ctx,
        ),
        name="cached",
    )(lengths, *given)


def final_kernel(width, per, e_ref, *refs):
    own_sum, own_part = refs[:2]
    got = refs[2 : 1 + EXPERTS]
    gain_ref, turn_ref, allow_ref, q_ref = refs[1 + EXPERTS : 5 + EXPERTS]
    cached = refs[5 + EXPERTS : -5]
    part_ref, entry_ref, out_hbm, out_ref, sem = refs[-5:]
    found = []
    for ctx_ref, stat_ref in zip(cached[0::2], cached[1::2]):
        found += [(ctx_ref, stat_ref, i) for i in range(ctx_ref.shape[0])]
    nodes, lat, heads = q_ref.shape
    padded = own_sum.shape[1]
    quarter = own_part.shape[1]
    raw = own_sum[...]
    for g in got:
        raw = raw + g[:, :padded].astype(F32)
    square = raw[:, lat : lat + 1] + raw[:, lat + 1 : lat + 2]
    raw = raw * lax.rsqrt(square / width + 1e-06)
    head = raw[:, :KEY_VALUE_RANK]
    head = head * lax.rsqrt(jnp.mean(head * head, axis=-1, keepdims=True) + 1e-06)
    head = head * gain_ref[...]
    tail = raw[:, KEY_VALUE_RANK:]
    half = (lat - KEY_VALUE_RANK) // 2
    lanes = tail.shape[1]
    tail = (
        tail * turn_ref[0]
        + pltpu.roll(tail, lanes - half, 1) * turn_ref[1]
        + pltpu.roll(tail, half, 1) * turn_ref[2]
    )
    keys = jnp.concatenate([head, tail], axis=1).astype(BF)[:, :lat]
    entry_ref[...] = keys
    count = keys.shape[0]
    copies = []
    for g in range(nodes // per):
        span = range(g * per, (g + 1) * per)

        def side(ref):
            return jnp.concatenate([ref[i] for i in span], axis=1)

        scores = dot(keys, side(q_ref)) * (softmax_scale * LOG2E)
        scores = jnp.where(side(allow_ref) > 0.5, scores, -jnp.inf)
        stats = jnp.concatenate([found[i][1][found[i][2]] for i in span], axis=1)
        old = stats[0:1]
        top = jnp.maximum(old, jnp.max(scores, axis=0, keepdims=True))
        weight = jnp.exp2(scores - top)
        share = stats[1:2] * jnp.exp2(old - top)
        scale = 1.0 / (share + jnp.sum(weight, axis=0, keepdims=True))
        share = jnp.broadcast_to(share * scale, (8, per * heads))
        both = jnp.concatenate([weight * scale, share], axis=0).T
        for i in range(per):
            mine = both[i * heads : (i + 1) * heads]
            ctx_ref, _, place = found[g * per + i]
            out = ctx_ref[place].astype(F32) * mine[:, count : count + 1]
            out = out + dot(mine[:, :count].astype(BF), keys[:, :KEY_VALUE_RANK])
            out_ref[g * per + i] = out.astype(BF)
        here = pl.ds(g * per, per)
        copies.append(pltpu.make_async_copy(out_ref.at[here], out_hbm.at[here], sem.at[g]))
        copies[-1].start()
    for k in range(EXPERTS):
        start = pl.multiple_of((e_ref[0] ^ k) * quarter, 128)
        part_ref[:, pl.ds(start, quarter)] = got[k - 1][:, padded:] if k else own_part[...]
    for c in copies:
        c.wait()


def final_attention(place, width, rows, gain, turn, allow, q_t, cached, per=8):
    tokens, lat, heads = q_t.shape
    vmem = pl.BlockSpec(memory_space=pltpu.VMEM)
    given = [*rows, gain, turn, allow, q_t, *cached]
    given = [pltpu.with_memory_space_constraint(x, pltpu.VMEM) for x in given]
    out = jax.ShapeDtypeStruct((tokens, heads, KEY_VALUE_RANK), BF)
    return pl.pallas_call(
        functools.partial(final_kernel, width, per),
        out_shape=[
            jax.ShapeDtypeStruct((tokens, width), BF),
            jax.ShapeDtypeStruct((tokens, lat), BF),
            out,
        ],
        in_specs=[pl.BlockSpec(memory_space=pltpu.SMEM)] + [vmem] * len(given),
        out_specs=[vmem, vmem, pl.BlockSpec(memory_space=pltpu.HBM)],
        scratch_shapes=[
            pltpu.VMEM(out.shape, BF),
            pltpu.SemaphoreType.DMA((tokens // per,)),
        ],
        compiler_params=params(12),
        cost_estimate=COST,
        name="final",
    )(place, *given)


def tree(parents, lengths, rank, lat):
    count = parents.shape[1]
    link = (parents[0][:, None] == jnp.arange(count, dtype=jnp.int32)[None, :]).astype(F32)
    reach = jnp.eye(count, dtype=F32) + link
    for _ in range(max(1, (count - 1).bit_length())):
        reach = jnp.minimum(jnp.dot(reach, reach, precision=lax.Precision.HIGHEST), 1.0)
    depth = jnp.sum(reach, axis=-1) - 1.0
    position = lengths.astype(F32) + depth
    half = (lat - rank) // 2
    index = jnp.arange(half, dtype=F32)
    inverse = 10000.0 ** (-2.0 * index / (2 * half))
    angle = position[:, None] * inverse[None, :]
    c, s = jnp.cos(angle), jnp.sin(angle)
    gap = jnp.zeros((count, 128 - 2 * half), F32)
    none = jnp.zeros_like(s)
    turn = jnp.stack(
        [
            jnp.concatenate([c, c, gap], axis=1),
            jnp.concatenate([-s, none, gap], axis=1),
            jnp.concatenate([none, s, gap], axis=1),
        ]
    )
    return reach, turn


def local(
    hidden,
    ffn_gain,
    attn_gain,
    latent_norm_gain,
    routes,
    gate_weights,
    expert_in,
    expert_down,
    kv_down,
    parents,
    lengths,
    queries,
    cache,
):
    size = lax.axis_size("ep")
    split = size // EXPERTS
    bits = [1 << b for b in range(split.bit_length() - 1)]
    width = hidden.shape[1]
    lat = kv_down.shape[1]
    heads = queries.shape[1]
    index = lax.axis_index("ep")
    place = jnp.stack([index // split, index % split]).astype(jnp.int32)

    def swap(x, bit):
        return lax.ppermute(x, "ep", [(i, i ^ bit) for i in range(size)])

    def spread(have, some):
        for bit in some:
            for r in sorted(have):
                have = have | {r ^ bit: swap(have[r], bit)}
        return have

    def to_line(xs):
        got = {k: swap(xs[k], k * split) for k in (3, 2, 1)}
        return [xs[0], got[1], got[2], got[3]]

    q_t = jnp.transpose(queries, (0, 2, 1))
    cache_t = jnp.transpose(cache, (0, 2, 1))
    half = queries.shape[0] // 2
    reach, turn = tree(parents, lengths, KEY_VALUE_RANK, lat)
    allow = jnp.broadcast_to(reach[:, :, None], reach.shape + (heads,))

    packed = pack(place, hidden, ffn_gain[None], routes.T, gate_weights.T)
    own = packed[:EXPERTS]
    top, low = bits[-1], bits[:-1]
    kvs = spread({0: kv_down}, [top])
    near = to_line(own)
    lower = join(near[0], near[1])
    lowers = spread({0: lower}, [top])
    q_first = after(q_t, lower, allow, turn)
    *first, w_in = cached_attention(lengths, q_first, cache_t, [expert_in], 0, half, per=8)
    quarters = packed[EXPERTS:]
    near_quarter = swap(quarters[1], split)
    distant, first, kvs, near_quarter = lax.optimization_barrier(
        (near[2:], first, kvs, near_quarter)
    )
    upper = join(*distant)
    across = {top: swap(upper, top)}
    uppers = spread({0: upper}, low[::-1])
    sent = after(quarters[2:], uppers)
    own_quarters = [swap(sent[k - 2], k * split) for k in (3, 2)]
    lowers = spread(lowers, low[::-1])
    gates, w_out = gate_matrices(place, (lower, upper), expert_down, hidden.shape[0])
    lowers, uppers, across, own_quarters, gates = lax.optimization_barrier(
        (lowers, uppers, across, own_quarters, gates)
    )
    uppers = uppers | spread(across, low[::-1])
    groups = [x for r in range(split) for x in (lowers[r], uppers[r])]
    pieces = expert_slice(place, groups, w_in, w_out)

    kvs = spread(after(kvs, pieces[0]), low[::-1])
    kvs = [(r, 0, x) for r, x in kvs.items()]

    def inner(keep, send):
        terms = [keep, swap(send, bits[0])]
        for bit in bits[1:-1]:
            out = sum(t[1::2].astype(F32) for t in terms).astype(BF)
            terms = [t[0::2] for t in terms] + [swap(out, bit)]
        return [t[0] for t in terms], sum(t[1].astype(F32) for t in terms).astype(BF)

    def outer(terms, got):
        return [sum(t[k].astype(F32) for t in (*terms, got)).astype(BF) for k in range(len(got))]

    kept, out = zip(*[inner(*p) for p in pieces])
    got = [swap(x, top) for x in out]
    far = outer(kept[0], after(got[0], out[2]))
    middle = outer(kept[1], got[1])
    second = cached_attention(
        lengths, after(q_t, middle, out[2]), cache_t, [], half, half // 2, cost=LONG
    )
    close = outer(kept[2], after(got[2], second))
    outs_e = to_line(close + middle + far)
    third = cached_attention(
        lengths, after(q_t, close[1]), cache_t, [], half + half // 2, half // 2
    )
    outs_e, third = lax.optimization_barrier((outs_e, third))

    own_quarters = [quarters[0], near_quarter, own_quarters[1], own_quarters[0]]
    own_sum, own_part, *rows = combine(place, outs_e, own_quarters, gates, attn_gain[None], kvs)
    rows = [own_sum, own_part] + [swap(r, (k + 1) * split) for k, r in enumerate(rows)]
    return final_attention(
        place, width, rows, latent_norm_gain[None], turn, allow, q_t, [*first, *second, *third]
    )


def solution(mesh):
    placed = (
        P(("group", "ep"), None),
        P(),
        P(),
        P(),
        P(("group", "ep"), None),
        P(("group", "ep"), None),
        P("ep", None, None),
        P("ep", None, None),
        P("ep", None),
        P(("group", "ep"), None),
        P(("group", "ep")),
        P(("group", "ep"), None, None),
        P(("group", "ep"), None, None),
    )
    return jax.shard_map(
        local,
        mesh=mesh,
        in_specs=placed,
        out_specs=(
            P(("group", "ep"), None),
            P(("group", "ep"), None),
            P(("group", "ep"), None, None),
        ),
        check_vma=False,
    )
```

```python
import functools

import jax
import jax.numpy as jnp
from jax import lax
from jax.experimental import pallas as pl
from jax.experimental.pallas import tpu as pltpu
from jax.sharding import PartitionSpec as P

KEY_VALUE_RANK = 512
NODES = 16
EXPERTS = 4
CAP = 9
TAIL = 128
ROWS = 40
SPACED = 48
BF = jnp.bfloat16
F32 = jnp.float32
softmax_scale = 192.0 ** (-0.5)
MIB = 1024 * 1024
LONG = pl.CostEstimate(flops=1 << 34, bytes_accessed=1 << 24, transcendentals=0)
COST = pl.CostEstimate(flops=1024, bytes_accessed=1024, transcendentals=0)
LOG2E = 1.4426950408889634


def iota(shape, dim):
    return lax.broadcasted_iota(jnp.int32, shape, dim)


def dot(a, b):
    return jnp.dot(a, b, preferred_element_type=F32)


def dot_t(a, b):
    return lax.dot_general(a, b, (((1,), (1,)), ((), ())), preferred_element_type=F32)


def params(mib, semantics=None):
    return pltpu.CompilerParams(vmem_limit_bytes=mib * MIB, dimension_semantics=semantics)


def after(x, *others):
    return lax.optimization_barrier((x, others))[0]


def whole(shape):
    zeros = (0,) * len(shape)
    return pl.BlockSpec(shape, lambda *_: zeros)


def pack_kernel(e_ref, *refs):
    ins, outs = refs[:4], refs[4 : 4 + 2 * EXPERTS]
    held, sem = refs[4 + 2 * EXPERTS : -1], refs[-1]
    copies = [pltpu.make_async_copy(a, b, sem.at[i]) for i, (a, b) in enumerate(zip(ins, held))]
    for c in copies:
        c.start()
    for c in copies:
        c.wait()
    hidden_ref, gain_ref, routes_ref, gates_ref = held
    chunks, parts = outs[:EXPERTS], outs[EXPERTS:]
    tokens, width = hidden_ref.shape
    piece = width // 8
    quarter = width // EXPERTS
    x = hidden_ref[...].astype(F32)
    scale = lax.rsqrt(jnp.mean(x * x, axis=-1, keepdims=True) + 1e-06)
    units = (x * scale * gain_ref[...]).astype(BF)
    first = jnp.broadcast_to(routes_ref[0:1, :], (8, tokens))
    second = jnp.broadcast_to(routes_ref[1:2, :], (8, tokens))
    row = iota((8, tokens), 0)
    before = (iota((tokens, tokens), 0) < iota((tokens, tokens), 1)).astype(BF)
    main, ninth = [], []
    for k in range(EXPERTS):
        expert = e_ref[0] ^ k
        hit = jnp.where((first == expert) | (second == expert), 1.0, 0.0)
        rank = dot(hit.astype(BF), before)
        main.append(jnp.where(rank == row.astype(F32), hit, 0.0))
        ninth.append(jnp.where(rank == 8.0, hit, 0.0))
    main = jnp.concatenate(main, axis=0).astype(BF)
    ninth = jnp.concatenate(ninth, axis=0)
    rows = iota(ninth.shape, 0) % 8
    picked = dot(main, units).astype(BF)
    cut = jnp.zeros((8 * EXPERTS, piece), F32)
    for j in range(8):
        cut = cut + dot(
            jnp.where(rows == j, ninth, 0.0).astype(BF), units[:, j * piece : (j + 1) * piece]
        )
    cut = cut.astype(BF)
    info = jnp.where(row == 0, first.astype(F32), second.astype(F32))
    for choice in range(2):
        gate = jnp.broadcast_to(gates_ref[choice : choice + 1, :], (8, tokens))
        for part in range(3):
            rounded = gate.astype(BF).astype(F32)
            info = jnp.where(row == 2 + 3 * choice + part, rounded, info)
            gate = gate - rounded
    spread = (iota((tokens, TAIL), 0) == iota((tokens, TAIL), 1)).astype(BF)
    tail = dot(info.astype(BF), spread).astype(BF)
    for k in range(EXPERTS):
        expert = e_ref[0] ^ k
        chunks[k][:, :width] = picked[8 * k : 8 * k + 8]
        chunks[k][:, width : width + piece] = cut[8 * k : 8 * k + 8]
        chunks[k][:, width + piece :] = tail
        start = pl.multiple_of(expert * quarter, 128)
        parts[k][...] = hidden_ref[:, pl.ds(start, quarter)]


def pack(e, hidden, gain, routes_t, gates_t):
    tokens, width = hidden.shape
    chunk = jax.ShapeDtypeStruct((8, width + width // 8 + TAIL), BF)
    part = jax.ShapeDtypeStruct((tokens, width // EXPERTS), BF)
    hbm = pl.BlockSpec(memory_space=pltpu.HBM)
    vmem = pl.BlockSpec(memory_space=pltpu.VMEM)
    given = [hidden, gain, routes_t, gates_t]
    placed = [pltpu.with_memory_space_constraint(a, pltpu.HBM) for a in given]
    return pl.pallas_call(
        pack_kernel,
        out_shape=[chunk] * EXPERTS + [part] * EXPERTS,
        in_specs=[pl.BlockSpec(memory_space=pltpu.SMEM)] + [hbm] * 4,
        out_specs=[vmem] * (2 * EXPERTS),
        scratch_shapes=[pltpu.VMEM(a.shape, a.dtype) for a in given]
        + [pltpu.SemaphoreType.DMA((4,))],
        compiler_params=params(8),
        cost_estimate=COST,
        name="pack",
    )(e, *placed)


def down(split, e_ref, act, w_out, keep, send, first):
    quarter = keep.shape[3]
    step = quarter // 2
    main_rows = 32 * split
    for k in range(keep.shape[1]):
        start = (e_ref[0] ^ (first + k)) * quarter
        for h in range(2):
            columns = pl.ds(pl.multiple_of(start + h * step, 128), step)
            out = dot(act[...], w_out[0, :, columns])
            for r in range(split):
                lower = out[32 * r : 32 * r + 32]
                upper = out[main_rows + 8 * r : main_rows + 8 * r + 8]
                mine = jnp.concatenate([lower, upper], axis=0).astype(BF)
                (send if r % 2 else keep)[r // 2, k, :, h * step : (h + 1) * step] = mine


def expert_kernel(split, e_ref, *refs):
    groups = refs[: 2 * split]
    w_in, w_out, act, *pieces, x = refs[2 * split :]
    width = w_in.shape[1]
    hid = act.shape[1]
    piece = width // 8
    main_rows, last_rows = 32 * split, 8 * split
    for r in range(2 * split):
        x[16 * r : 16 * r + 16, :] = groups[r][:, :width]
    ext = jnp.concatenate([g[:, width : width + piece] for g in groups], axis=0)
    row = iota((8 * last_rows, main_rows), 0)
    col = iota((8 * last_rows, main_rows), 1)
    place = row % last_rows
    want = 32 * (place // 8) + 8 * (place % 8) + row // last_rows
    pick = jnp.where((place % 8 < 4) & (col == want), 1.0, 0.0).astype(BF)
    last = dot(pick, ext).astype(BF)
    for j in range(8):
        x[main_rows:, j * piece : (j + 1) * piece] = last[j * last_rows : (j + 1) * last_rows]
    step = min(256, hid)
    for i in range(hid // step):
        gate = dot(x[...], w_in[0, :, i * step : (i + 1) * step])
        up = dot(x[...], w_in[0, :, hid + i * step : hid + (i + 1) * step])
        act[:, i * step : (i + 1) * step] = (gate / (1.0 + jnp.exp(-gate)) * up).astype(BF)
    down(split, e_ref, act, w_out, pieces[0], pieces[1], 3)
    down(split, e_ref, act, w_out, pieces[2], pieces[3], 2)


def expert_rest_kernel(split, e_ref, act, w_out, keep, send):
    down(split, e_ref, act, w_out, keep, send, 0)


def expert_slice(e, groups, w_in, w_out):
    split = len(groups) // 2
    width, hid2 = w_in.shape[1:]
    hid = hid2 // 2
    quarter = width // EXPERTS
    half = jax.ShapeDtypeStruct((split // 2, EXPERTS // 2, ROWS, quarter), BF)
    single = jax.ShapeDtypeStruct((split // 2, 1, ROWS, quarter), BF)
    rows = ROWS * split
    act = jax.ShapeDtypeStruct((rows, hid), BF)
    vmem = pl.BlockSpec(memory_space=pltpu.VMEM)
    smem = pl.BlockSpec(memory_space=pltpu.SMEM)
    act, *single = pl.pallas_call(
        functools.partial(expert_kernel, split),
        out_shape=[act] + [single] * 4,
        in_specs=[smem] + [vmem] * (2 * split + 2),
        out_specs=[vmem] * 5,
        scratch_shapes=[pltpu.VMEM((rows, width), BF)],
        compiler_params=params(10),
        cost_estimate=COST,
        name="experts",
    )(e, *groups, w_in, w_out)
    rest = pl.pallas_call(
        functools.partial(expert_rest_kernel, split),
        out_shape=[half, half],
        in_specs=[smem] + [vmem] * 2,
        out_specs=[vmem] * 2,
        compiler_params=params(6),
        cost_estimate=COST,
        name="experts_rest",
    )(e, act, w_out)
    return single[:2], single[2:], rest


def join_kernel(a_ref, b_ref, out_ref):
    rows = a_ref.shape[0]
    out_ref[:rows, :] = a_ref[...]
    out_ref[rows:, :] = b_ref[...]


def join(a, b):
    vmem = pl.BlockSpec(memory_space=pltpu.VMEM)
    return pl.pallas_call(
        join_kernel,
        out_shape=pltpu.VMEM((2 * a.shape[0], a.shape[1]), a.dtype),
        in_specs=[vmem, vmem],
        out_specs=vmem,
        compiler_params=params(2),
        cost_estimate=COST,
        name="join",
    )(a, b)


def gate_kernel(tokens, e_ref, *refs):
    w_hbm, out_ref, w_ref, sem = refs[-4:]
    load = pltpu.make_async_copy(w_hbm, w_ref, sem)
    load.start()
    info = jnp.concatenate([r[:, r.shape[1] - TAIL :] for r in refs[:-4]], axis=0)
    one = (iota((tokens, TAIL), 0) == iota((tokens, TAIL), 1)).astype(BF)
    info = dot_t(one, info)
    earlier = (iota((tokens, tokens), 1) < iota((tokens, tokens), 0)).astype(BF)
    lanes = EXPERTS * SPACED
    lane = iota((tokens, lanes), 1).astype(F32)
    hits = []
    for k in range(EXPERTS):
        expert = (e_ref[0] ^ k).astype(F32)
        hits.append(jnp.where(info == expert, 1.0, 0.0))
    blocks = [[0.0] * EXPERTS for _ in range(3)]
    for k in range(EXPERTS):
        for s in range(EXPERTS):
            h0 = hits[k][:, 8 * s : 8 * s + 1]
            h1 = hits[k][:, 8 * s + 1 : 8 * s + 2]
            hit = jnp.broadcast_to(h0 + h1, (tokens, lanes))
            rank = dot(earlier, hit.astype(BF))
            line = s ^ k
            want = SPACED * k + jnp.where(rank < 8.0, rank + 8.0 * line, 32.0 + line)
            chosen = (lane == want) & (hit > 0.5)
            for p in range(3):
                g0 = info[:, 8 * s + 2 + p : 8 * s + 3 + p]
                g1 = info[:, 8 * s + 5 + p : 8 * s + 6 + p]
                gate = jnp.broadcast_to(h0 * g0 + h1 * g1, (tokens, lanes))
                blocks[p][s] = jnp.where(chosen, gate, blocks[p][s])
    out_ref[...] = jnp.concatenate(blocks[0] + blocks[1] + blocks[2], axis=0).astype(BF)
    load.wait()

def gate_matrices(place, halves, weight, tokens):
    vmem = pl.BlockSpec(memory_space=pltpu.VMEM)
    return pl.pallas_call(
        functools.partial(gate_kernel, tokens),
        out_shape=[
            pltpu.VMEM((3 * EXPERTS * tokens, EXPERTS * SPACED), BF),
            pltpu.VMEM(weight.shape, weight.dtype),
        ],
        in_specs=[pl.BlockSpec(memory_space=pltpu.SMEM)]
        + [vmem] * len(halves)
        + [pl.BlockSpec(memory_space=pltpu.HBM)],
        out_specs=[vmem] * 2,
        scratch_shapes=[pltpu.SemaphoreType.DMA],
        compiler_params=params(4),
        cost_estimate=LONG,
        name="gates",
    )(place, *halves, pltpu.with_memory_space_constraint(weight, pltpu.HBM))


def combine_kernel(spots, tokens, e_ref, *refs):
    outs_e, hid = refs[:EXPERTS], refs[EXPERTS : 2 * EXPERTS]
    gates_ref, gain_ref = refs[2 * EXPERTS : 2 * EXPERTS + 2]
    kvs = refs[2 * EXPERTS + 2 : 2 * EXPERTS + 2 + len(spots)]
    rest = refs[2 * EXPERTS + 2 + len(spots) :]
    own_sum, own_part = rest[:2]
    sent = rest[2 : 1 + EXPERTS]
    kv_ref, rows_ref, sem = rest[1 + EXPERTS :]
    lat = kvs[0].shape[1]
    part = spots[0][1]
    copies = []
    for i, (r, rows, first) in enumerate(spots):
        place = pl.multiple_of((e_ref[1] ^ r) * part + first, 16)
        copies.append(pltpu.make_async_copy(kvs[i], kv_ref.at[pl.ds(place, rows), :], sem.at[i]))
        copies[-1].start()
    gap = jnp.zeros((SPACED - ROWS, outs_e[0].shape[1]), F32)
    for k in range(EXPERTS):
        spaced = jnp.concatenate([outs_e[k][...].astype(F32), gap], axis=0)
        rows_ref[SPACED * k : SPACED * (k + 1), :] = spaced.astype(BF)
    moe = dot(gates_ref[...], rows_ref[...])
    total = EXPERTS * tokens
    moe = moe[:total] + moe[total : 2 * total] + moe[2 * total :]
    mixed = jnp.concatenate([h[...].astype(F32) for h in hid], axis=0) + moe
    square = jnp.sum(mixed * mixed, axis=-1, keepdims=True)
    scaled = (mixed * gain_ref[...]).astype(BF)
    for c in copies:
        c.wait()
    rows = dot(scaled, kv_ref[...])
    padded = own_sum.shape[1]
    for s in range(EXPERTS):
        span = slice(s * tokens, (s + 1) * tokens)
        rest = jnp.broadcast_to(square[span], (tokens, padded - lat))
        first = iota(rest.shape, 1) == 0
        if s:
            high = rest.astype(BF).astype(F32)
            sent[s - 1][:, :lat] = rows[span].astype(BF)
            sent[s - 1][:, lat:padded] = jnp.where(first, high, rest - high).astype(BF)
            sent[s - 1][:, padded:] = mixed[span].astype(BF)
        else:
            own_sum[:, :lat] = rows[span]
            own_sum[:, lat:] = jnp.where(first, rest, 0.0)
            own_part[...] = mixed[span].astype(BF)


def combine(place, outs_e, hid, gates, gain, kvs):
    spots = [(r, x.shape[0], first) for r, first, x in kvs]
    kvs = [x for _, _, x in kvs]
    tokens, quarter = hid[0].shape
    lat = kvs[0].shape[1]
    padded = (lat // 128 + 1) * 128
    outs = [pltpu.VMEM((tokens, padded), F32), pltpu.VMEM((tokens, quarter), BF)]
    outs += [pltpu.VMEM((tokens, padded + quarter), BF)] * (EXPERTS - 1)
    return pl.pallas_call(
        functools.partial(combine_kernel, spots, tokens),
        out_shape=outs,
        grid_spec=pltpu.PrefetchScalarGridSpec(
            num_scalar_prefetch=1,
            grid=(1,),
            in_specs=[whole(o.shape) for o in outs_e]
            + [whole(h.shape) for h in hid]
            + [
                whole(gates.shape),
                pl.BlockSpec((1, quarter), lambda t, e: (0, e[0])),
            ]
            + [pl.BlockSpec(memory_space=pl.ANY)] * len(kvs),
            out_specs=[whole(o.shape) for o in outs],
            scratch_shapes=[
                pltpu.VMEM((quarter, lat), BF),
                pltpu.VMEM((EXPERTS * SPACED, quarter), BF),
                pltpu.SemaphoreType.DMA((len(kvs),)),
            ],
        ),
        compiler_params=params(8),
        cost_estimate=COST,
        name="combine",
    )(place, *outs_e, *hid, gates, gain, *kvs)


def cached_kernel(begin, per, length_ref, *refs):
    q_ref, cache_ref, keys_ref, sem = refs[-4:]
    loads = (len(refs) - 8) // 2
    q_hbm, cache_hbm = refs[:2]
    w_hbm = refs[2 : 2 + loads]
    out_ref, stat_ref = refs[2 + loads : 4 + loads]
    w_ref = refs[4 + loads : -4]
    nodes, lat, heads = q_ref.shape
    ctx = cache_ref.shape[2]
    spare = keys_ref.shape[1] - lat
    copies = [
        pltpu.make_async_copy(cache_hbm, cache_ref, sem.at[0]),
        pltpu.make_async_copy(q_hbm.at[pl.ds(begin, nodes)], q_ref, sem.at[1]),
    ]
    for i in range(loads):
        copies.append(pltpu.make_async_copy(w_hbm[i], w_ref[i], sem.at[2 + i]))
    for c in copies:
        c.start()
    unused = (iota((ctx, spare), 0) >= length_ref[0]) & (iota((ctx, spare), 1) == 0)
    keys_ref[:, lat:] = jnp.where(unused, -jnp.inf, 0.0).astype(BF)
    one = (iota((spare, per * heads), 0) == 0).astype(BF)
    factor = softmax_scale * LOG2E
    copies[0].wait()
    keys_ref[:, :lat] = cache_ref[0].T
    copies[1].wait()

    for g in range(nodes // per):
        q = jnp.concatenate([q_ref[g * per + i] for i in range(per)], axis=1)
        q = jnp.concatenate([q, one], axis=0)
        scores = dot(keys_ref[...], q)
        top = jnp.max(scores, axis=0, keepdims=True) * factor
        weight = jnp.exp2(scores * factor - top)
        total = jnp.sum(weight, axis=0, keepdims=True)
        out = dot(cache_ref[0, :KEY_VALUE_RANK, :], weight.astype(BF)) * (1.0 / total)
        for i in range(per):
            span = slice(i * heads, (i + 1) * heads)
            out_ref[g * per + i] = out[:, span].T.astype(out_ref.dtype)
            stat_ref[g * per + i] = jnp.concatenate([top[:, span], total[:, span]], axis=0)
    for c in copies[2:]:
        c.wait()


def cached_attention(lengths, q_t, cache_t, weights, first, count, per=4, cost=None):
    tokens, lat, heads = q_t.shape
    ctx = cache_t.shape[2]
    hbm = pl.BlockSpec(memory_space=pltpu.HBM)
    vmem = pl.BlockSpec(memory_space=pltpu.VMEM)
    given = [pltpu.with_memory_space_constraint(a, pltpu.HBM) for a in (q_t, cache_t, *weights)]
    return pl.pallas_call(
        functools.partial(cached_kernel, first, per),
        out_shape=[
            pltpu.VMEM((count, heads, KEY_VALUE_RANK), BF),
            pltpu.VMEM((count, 2, heads), F32),
        ]
        + [pltpu.VMEM(w.shape, w.dtype) for w in weights],
        in_specs=[pl.BlockSpec(memory_space=pltpu.SMEM)] + [hbm] * len(given),
        out_specs=[vmem] * len(given),
        scratch_shapes=[
            pltpu.VMEM((count, lat, heads), BF),
            pltpu.VMEM(cache_t.shape, BF),
            pltpu.VMEM((ctx, (lat // 128 + 1) * 128), BF),
            pltpu.SemaphoreType.DMA((2 + len(weights),)),
        ],
        compiler_params=params(10),
        cost_estimate=cost
        or pl.CostEstimate(
            flops=4 * count * heads * ctx * (lat + KEY_VALUE_RANK),
            bytes_accessed=4 * count * heads * lat,
            transcendentals=count * heads * ctx,
        ),
        name="cached",
    )(lengths, *given)


def final_kernel(width, per, e_ref, *refs):
    own_sum, own_part = refs[:2]
    got = refs[2 : 1 + EXPERTS]
    gain_ref, turn_ref, allow_ref, q_ref = refs[1 + EXPERTS : 5 + EXPERTS]
    cached = refs[5 + EXPERTS : -7]
    part_hbm, entry_hbm, out_hbm, part_ref, entry_ref, out_ref, sem = refs[-7:]
    found = []
    for ctx_ref, stat_ref in zip(cached[0::2], cached[1::2]):
        found += [(ctx_ref, stat_ref, i) for i in range(ctx_ref.shape[0])]
    nodes, lat, heads = q_ref.shape
    padded = own_sum.shape[1]
    quarter = own_part.shape[1]
    raw = own_sum[...]
    for g in got:
        raw = raw + g[:, :padded].astype(F32)
    square = raw[:, lat : lat + 1] + raw[:, lat + 1 : lat + 2]
    raw = raw * lax.rsqrt(square / width + 1e-06)
    head = raw[:, :KEY_VALUE_RANK]
    head = head * lax.rsqrt(jnp.mean(head * head, axis=-1, keepdims=True) + 1e-06)
    head = head * gain_ref[...]
    tail = raw[:, KEY_VALUE_RANK:]
    half = (lat - KEY_VALUE_RANK) // 2
    lanes = tail.shape[1]
    tail = (
        tail * turn_ref[0]
        + pltpu.roll(tail, lanes - half, 1) * turn_ref[1]
        + pltpu.roll(tail, half, 1) * turn_ref[2]
    )
    keys = jnp.concatenate([head, tail], axis=1).astype(BF)[:, :lat]
    entry_ref[...] = keys
    for k in range(EXPERTS):
        start = pl.multiple_of((e_ref[0] ^ k) * quarter, 128)
        part_ref[:, pl.ds(start, quarter)] = got[k - 1][:, padded:] if k else own_part[...]
    copies = [
        pltpu.make_async_copy(part_ref, part_hbm, sem.at[0]),
        pltpu.make_async_copy(entry_ref, entry_hbm, sem.at[1]),
    ]
    for c in copies:
        c.start()
    count = keys.shape[0]
    for g in range(nodes // per):
        span = range(g * per, (g + 1) * per)

        def side(ref):
            return jnp.concatenate([ref[i] for i in span], axis=1)

        scores = dot(keys, side(q_ref)) * (softmax_scale * LOG2E)
        scores = jnp.where(side(allow_ref) > 0.5, scores, -jnp.inf)
        stats = jnp.concatenate([found[i][1][found[i][2]] for i in span], axis=1)
        old = stats[0:1]
        top = jnp.maximum(old, jnp.max(scores, axis=0, keepdims=True))
        weight = jnp.exp2(scores - top)
        share = stats[1:2] * jnp.exp2(old - top)
        scale = 1.0 / (share + jnp.sum(weight, axis=0, keepdims=True))
        share = jnp.broadcast_to(share * scale, (8, per * heads))
        both = jnp.concatenate([weight * scale, share], axis=0).T
        for i in range(per):
            mine = both[i * heads : (i + 1) * heads]
            ctx_ref, _, place = found[g * per + i]
            out = ctx_ref[place].astype(F32) * mine[:, count : count + 1]
            out = out + dot(mine[:, :count].astype(BF), keys[:, :KEY_VALUE_RANK])
            out_ref[g * per + i] = out.astype(BF)
            if i % 2:
                here = pl.ds(g * per + i - 1, 2)
                number = len(copies)
                copies.append(
                    pltpu.make_async_copy(out_ref.at[here], out_hbm.at[here], sem.at[number])
                )
                copies[-1].start()
    for c in copies:
        c.wait()


def final_attention(place, width, rows, gain, turn, allow, q_t, cached, per=8):
    tokens, lat, heads = q_t.shape
    vmem = pl.BlockSpec(memory_space=pltpu.VMEM)
    given = [*rows, gain, turn, allow, q_t, *cached]
    given = [pltpu.with_memory_space_constraint(x, pltpu.VMEM) for x in given]
    out = jax.ShapeDtypeStruct((tokens, heads, KEY_VALUE_RANK), BF)
    return pl.pallas_call(
        functools.partial(final_kernel, width, per),
        out_shape=[
            jax.ShapeDtypeStruct((tokens, width), BF),
            jax.ShapeDtypeStruct((tokens, lat), BF),
            out,
        ],
        in_specs=[pl.BlockSpec(memory_space=pltpu.SMEM)] + [vmem] * len(given),
        out_specs=[pl.BlockSpec(memory_space=pltpu.HBM)] * 3,
        scratch_shapes=[
            pltpu.VMEM((tokens, width), BF),
            pltpu.VMEM((tokens, lat), BF),
            pltpu.VMEM(out.shape, BF),
            pltpu.SemaphoreType.DMA((2 + tokens // 2,)),
        ],
        compiler_params=params(12),
        cost_estimate=COST,
        name="final",
    )(place, *given)


def tree(parents, lengths, rank, lat):
    count = parents.shape[1]
    link = (parents[0][:, None] == jnp.arange(count, dtype=jnp.int32)[None, :]).astype(F32)
    reach = jnp.eye(count, dtype=F32) + link
    for _ in range(max(1, (count - 1).bit_length())):
        reach = jnp.minimum(jnp.dot(reach, reach, precision=lax.Precision.HIGHEST), 1.0)
    depth = jnp.sum(reach, axis=-1) - 1.0
    position = lengths.astype(F32) + depth
    half = (lat - rank) // 2
    index = jnp.arange(half, dtype=F32)
    inverse = 10000.0 ** (-2.0 * index / (2 * half))
    angle = position[:, None] * inverse[None, :]
    c, s = jnp.cos(angle), jnp.sin(angle)
    gap = jnp.zeros((count, 128 - 2 * half), F32)
    none = jnp.zeros_like(s)
    turn = jnp.stack(
        [
            jnp.concatenate([c, c, gap], axis=1),
            jnp.concatenate([-s, none, gap], axis=1),
            jnp.concatenate([none, s, gap], axis=1),
        ]
    )
    return reach, turn


def local(
    hidden,
    ffn_gain,
    attn_gain,
    latent_norm_gain,
    routes,
    gate_weights,
    expert_in,
    expert_down,
    kv_down,
    parents,
    lengths,
    queries,
    cache,
):
    size = lax.axis_size("ep")
    split = size // EXPERTS
    bits = [1 << b for b in range(split.bit_length() - 1)]
    width = hidden.shape[1]
    lat = kv_down.shape[1]
    heads = queries.shape[1]
    index = lax.axis_index("ep")
    place = jnp.stack([index // split, index % split]).astype(jnp.int32)

    def swap(x, bit):
        return lax.ppermute(x, "ep", [(i, i ^ bit) for i in range(size)])

    def spread(have, some):
        for bit in some:
            for r in sorted(have):
                have = have | {r ^ bit: swap(have[r], bit)}
        return have

    def to_line(xs):
        got = {k: swap(xs[k], k * split) for k in (3, 2, 1)}
        return [xs[0], got[1], got[2], got[3]]

    q_t = jnp.transpose(queries, (0, 2, 1))
    cache_t = jnp.transpose(cache, (0, 2, 1))
    half = queries.shape[0] // 2
    reach, turn = tree(parents, lengths, KEY_VALUE_RANK, lat)
    allow = jnp.broadcast_to(reach[:, :, None], reach.shape + (heads,))

    packed = pack(place, hidden, ffn_gain[None], routes.T, gate_weights.T)
    own = packed[:EXPERTS]
    top, low = bits[-1], bits[:-1]
    kvs = spread({0: kv_down}, [top])
    near = to_line(own)
    lower = join(near[0], near[1])
    lowers = spread({0: lower}, [top])
    q_first = after(q_t, lower, allow, turn)
    *first, w_in = cached_attention(lengths, q_first, cache_t, [expert_in], 0, half, per=8)
    quarters = packed[EXPERTS:]
    near_quarter = swap(quarters[1], split)
    distant, first, kvs, near_quarter = lax.optimization_barrier(
        (near[2:], first, kvs, near_quarter)
    )
    upper = join(*distant)
    across = {top: swap(upper, top)}
    uppers = spread({0: upper}, low[::-1])
    sent = after(quarters[2:], uppers)
    own_quarters = [swap(sent[k - 2], k * split) for k in (3, 2)]
    lowers = spread(lowers, low[::-1])
    gates, w_out = gate_matrices(place, (lower, upper), expert_down, hidden.shape[0])
    lowers, uppers, across, own_quarters, gates = lax.optimization_barrier(
        (lowers, uppers, across, own_quarters, gates)
    )
    uppers = uppers | spread(across, low[::-1])
    groups = [x for r in range(split) for x in (lowers[r], uppers[r])]
    pieces = expert_slice(place, groups, w_in, w_out)

    kvs = spread(after(kvs, pieces[0]), low[::-1])
    kvs = [(r, 0, x) for r, x in kvs.items()]

    def inner(keep, send):
        terms = [keep, swap(send, bits[0])]
        for bit in bits[1:-1]:
            out = sum(t[1::2].astype(F32) for t in terms).astype(BF)
            terms = [t[0::2] for t in terms] + [swap(out, bit)]
        return [t[0] for t in terms], sum(t[1].astype(F32) for t in terms).astype(BF)

    def outer(terms, got):
        return [sum(t[k].astype(F32) for t in (*terms, got)).astype(BF) for k in range(len(got))]

    kept, out = zip(*[inner(*p) for p in pieces])
    got = [swap(x, top) for x in out]
    far = outer(kept[0], after(got[0], out[2]))
    middle = outer(kept[1], got[1])
    second = cached_attention(
        lengths, after(q_t, middle, out[2]), cache_t, [], half, half // 2, cost=LONG
    )
    close = outer(kept[2], after(got[2], second))
    outs_e = to_line(close + middle + far)
    third = cached_attention(
        lengths, after(q_t, close[1]), cache_t, [], half + half // 2, half // 2
    )
    outs_e, third = lax.optimization_barrier((outs_e, third))

    own_quarters = [quarters[0], near_quarter, own_quarters[1], own_quarters[0]]
    own_sum, own_part, *rows = combine(place, outs_e, own_quarters, gates, attn_gain[None], kvs)
    rows = [own_sum, own_part] + [swap(r, (k + 1) * split) for k, r in enumerate(rows)]
    return final_attention(
        place, width, rows, latent_norm_gain[None], turn, allow, q_t, [*first, *second, *third]
    )


def solution(mesh):
    placed = (
        P(("group", "ep"), None),
        P(),
        P(),
        P(),
        P(("group", "ep"), None),
        P(("group", "ep"), None),
        P("ep", None, None),
        P("ep", None, None),
        P("ep", None),
        P(("group", "ep"), None),
        P(("group", "ep")),
        P(("group", "ep"), None, None),
        P(("group", "ep"), None, None),
    )
    return jax.shard_map(
        local,
        mesh=mesh,
        in_specs=placed,
        out_specs=(
            P(("group", "ep"), None),
            P(("group", "ep"), None),
            P(("group", "ep"), None, None),
        ),
        check_vma=False,
    )
```
